512 devices in a mesh: row: 16 (over y, core), col: 32 (over z, x).
Axes of the slice: x: 4, y: 8, z: 8, core: 2. Of those that a mesh axis runs over, the one named last changes fastest.
Arguments:
- hessian: float32 [6, 16, 128, 3, 32, 128], P(None, 'row', None, None, 'col'), may hold values from -4 to 9, as said below
Outputs:
- reduced: float32 [6, 16, 128, 3, 32, 128], P(None, 'row', None, None, 'col')
The draws below stay inside these ranges and needn't reach their ends.
Inputs may be any that keep to these rules, and one draw needn't show every extreme that they name: hessian is symmetric as a 12288 x 12288 matrix A, and for every j < 64 the entry A[64 + j, j] is at least twice the Euclidean norm of the other entries of column j in rows 64 and below.
All inputs are finite; a program needn't handle non-finite values.
Results may differ from the reference program's by a relative error of at most 0.0001.
Values sent between devices are 32-bit elements; how exact they have to be, the bound alone decides.
A program may use at most 64 MiB of HBM per device.

```python
import jax
import jax.numpy as jnp
from jax import lax

NB = 64
TILE = 128
COL_TILES = 3
ROW_TILES = 6
ORDER = 12288
N_ROW = 16
N_COL = 32


def draw_hessian(key, part):
    key = jax.random.fold_in(key, 7)
    base_key, pivot_key, off_key, tail_key = jax.random.split(key, 4)
    noise = jnp.clip(jax.random.normal(base_key, (ORDER, ORDER), jnp.float32), -4.0, 4.0)
    symmetric = jnp.triu(noise) + jnp.triu(noise, 1).T
    diagonal = jax.random.uniform(pivot_key, (NB,), jnp.float32, 6.5, 9.0)
    offdiagonal = jax.random.uniform(off_key, (NB, NB), jnp.float32, -0.3, 0.3)
    square = jnp.where(jnp.eye(NB, dtype=bool), diagonal[:, None], offdiagonal)
    reach = 2.0 * (ORDER - 2 * NB) ** (-0.5)
    tail = jax.random.uniform(tail_key, (ORDER - 2 * NB, NB), jnp.float32, -reach, reach)
    panel_rows = jnp.concatenate([symmetric[:NB, :NB], square, tail], axis=0)
    matrix = symmetric.at[:, :NB].set(panel_rows)
    matrix = matrix.at[:NB, :].set(panel_rows.T)
    return matrix.reshape(ROW_TILES, N_ROW, TILE, COL_TILES, N_COL, TILE)


def setup_inputs(seed: int = 0) -> dict:
    splits = jax.random.split(jax.random.key(seed), 2)
    hessian = draw_hessian(jax.random.fold_in(splits[1], 71), 0)
    return {"hessian": hessian}


highest = lax.Precision.HIGHEST

def product(left, right):
    return jnp.dot(left.astype(jnp.float32), right.astype(jnp.float32), precision=highest, preferred_element_type=jnp.float32)

def triangle_solve(matrix, rhs, lower, unit=False):
    return lax.linalg.triangular_solve(matrix, rhs, left_side=True, lower=lower, unit_diagonal=unit)

def householder(panel_rows):
    length = panel_rows.shape[0]
    positions = jnp.arange(length)
    columns = jnp.arange(NB)

    def advance(step, loop_state):
        current, reflectors, factors = loop_state
        column = current[:, step]
        below_part = jnp.where(positions >= step, column, 0.0)
        column_norm = jnp.sqrt(jnp.sum(below_part * below_part))
        denominator = current[step, step] + column_norm
        reflector = jnp.where(positions > step, column / denominator, jnp.where(positions == step, 1.0, 0.0))
        factor = denominator / column_norm
        weights = factor * product(reflector, current)
        weights = jnp.where(columns > step, weights, 0.0)
        current = current - reflector[:, None] * weights[None, :]
        reflectors = reflectors.at[:, step].set(reflector)
        factors = factors.at[step].set(factor)
        return (current, reflectors, factors)
    start = (panel_rows, jnp.zeros_like(panel_rows), jnp.zeros((NB,), panel_rows.dtype))
    final_state = lax.fori_loop(0, NB, advance, start)
    return (final_state[1], final_state[2])

def reference(hessian):
    full = hessian.reshape(ORDER, ORDER)
    reflectors, factors = householder(full[NB:, :NB])
    vector_gram = product(reflectors.T, reflectors)
    inverse_factor = jnp.diag(1.0 / factors) + jnp.triu(vector_gram, 1)
    block_factor = triangle_solve(inverse_factor, jnp.eye(NB, dtype=full.dtype), False)
    padded = jnp.concatenate([jnp.zeros((NB, NB), full.dtype), reflectors], axis=0)
    image = product(product(full, padded), block_factor)
    cross = product(block_factor.T, product(padded.T, image))
    update = image - 0.5 * product(padded, cross)
    reduced = full - product(update, padded.T) - product(padded, update.T)
    return reduced.reshape(hessian.shape)
```

```python
import functools

import jax
import jax.numpy as jnp
from jax import lax
from jax.experimental import pallas as pl
from jax.experimental.pallas import tpu as pltpu
from jax.sharding import PartitionSpec as P

NB = 64
MESH = pl.DeviceIdType.MESH
HIGHEST = lax.Precision.HIGHEST
F32 = jnp.float32


def dot_nn(a, b):
    return lax.dot_general(a, b, (((1,), (0,)), ((), ())), precision=HIGHEST, preferred_element_type=F32)


def dot_nt(a, b):
    return lax.dot_general(a, b, (((1,), (1,)), ((), ())), precision=HIGHEST, preferred_element_type=F32)


def spiral(q, n):
    return lax.rem(n // 2 + (1 - 2 * lax.rem(q, 2)) * lax.div(q + 1, 2), n)


def loop(lo, hi, f):
    def step(i, carry):
        f(i)
        return carry

    lax.fori_loop(lo, hi, step, 0)


def factor_cholesky(g, ct):
    lane1 = lax.broadcasted_iota(jnp.int32, (1, 128), 1)
    for k in range(NB):
        col = g[:, k : k + 1]
        row = g[k : k + 1, :]
        piv = g[k : k + 1, k : k + 1]
        ct[NB + k : NB + k + 1, :] = jnp.where((lane1 >= k) & (lane1 < NB), row * lax.rsqrt(piv), 0.0)
        if k < NB - 1:
            low = (k + 1) // 8 * 8
            part = g[low:, :] - col[low:, :] * (row / piv)
            g = part if low == 0 else jnp.concatenate([g[:low, :], part], axis=0)


def invert(m):
    lane1 = lax.broadcasted_iota(jnp.int32, (1, 128), 1)
    lane = lax.broadcasted_iota(jnp.int32, (NB, 128), 1)
    sub = lax.broadcasted_iota(jnp.int32, (NB, 128), 0)
    for k in range(NB):
        col = m[:, k : k + 1]
        row = m[k : k + 1, :]
        piv = m[k : k + 1, k : k + 1]
        scaled = jnp.where(lane1 == k, 1.0, row) / piv
        m = jnp.where(sub == k, scaled, jnp.where(lane == k, 0.0, m) - col * scaled)
    return m


def kernel(
    a_hbm, o_hbm, a_v, colpb, rowpb, zpart, zrecv, zrows, zcols, gpk, grecv, gfin, p1, hsend, hrecv, hall, ct, c0, om,
    local_sem, out_sem, colp_s, colp_r, fwd_s, sc_s, sc_r, ag_s, ag_r, rs_s, rs_r, zr_s, zr_r, zc_s, zc_r,
    g_s, g_r, gb_s, gb_r, p1_s, p1_r, h_s, h_r, ha_s, ha_r, c0_s, c0_r,
):
    r, c = lax.axis_index("row"), lax.axis_index("col")
    y, core = lax.div(r, 2), lax.rem(r, 2)
    z, x = lax.div(c, 4), lax.rem(c, 4)
    zodd = lax.rem(z, 2)
    mine = lax.div(c, 2)
    owner = lax.rem(x + z, 2) == 0
    my_g, my_h = lax.rem(mine, 8), lax.div(mine, 8)
    partner = c + 1 - 2 * lax.rem(c, 2)
    home = lax.rem(c, 16) == r
    lane = lax.broadcasted_iota(jnp.int32, (NB, 128), 1)

    def panel_owner(k):
        return 2 * k + lax.rem(lax.div(k, 2), 2)

    def col_peer(p):
        return lax.rem(z + spiral(lax.div(p, 4), 8), 8) * 4 + lax.rem(x + spiral(lax.rem(p, 4), 4), 4)

    def row_peer(p):
        return lax.rem(y + spiral(lax.div(p, 2), 8), 8) * 2 + lax.rem(core + 1 - lax.rem(p, 2), 2)

    def copy(src, dst, ssem, rsem, dev):
        return pltpu.make_async_remote_copy(
            src_ref=src, dst_ref=dst, send_sem=ssem, recv_sem=rsem, device_id=dev, device_id_type=MESH
        )

    def chunk(k, part):
        rows = pl.multiple_of(lax.rem(k, 8) * 8 + part * NB, 8)
        return rowpb.at[lax.div(k, 8), :, pl.ds(rows, 8), :]

    load = pltpu.make_async_copy(a_hbm, a_v, local_sem)
    load.start()
    barrier = pltpu.get_barrier_semaphore()

    def greet(dev):
        pl.semaphore_signal(barrier, inc=1, device_id=dev, device_id_type=MESH)

    loop(0, 31, lambda p: greet((r, col_peer(p))))
    loop(0, 15, lambda p: greet((row_peer(p), c)))

    @pl.when(jnp.logical_not(home))
    def _():
        loop(0, 8, lambda g: greet((lax.rem(c, 16), panel_owner(g + 8 * lax.div(c, 16)))))

    load.wait()

    def panel_cols(ref, s):
        return jnp.where((c == 0) & (s == 0) & (lane < NB), 0.0, ref[pl.ds(s, NB, stride=3), :])

    @pl.when(c == 0)
    def _():
        full = lax.broadcasted_iota(jnp.int32, (128, 128), 0)
        fulll = lax.broadcasted_iota(jnp.int32, (128, 128), 1)
        for t in range(6):
            block = jnp.transpose(a_v[pl.ds(t * 384, 128, stride=3), :])
            if t == 0:
                block = jnp.where((r == 0) & (full < NB) & (fulll < NB), 0.0, block)
            rowpb[t % 2, t // 2] = block

    @pl.when(r == 0)
    def _():
        panel = jnp.concatenate([panel_cols(a_v, s) for s in range(3)], axis=1)
        zero = jnp.zeros_like(panel)
        gpk[...] = dot_nt(panel[:32], jnp.concatenate([panel, zero], axis=0)) + dot_nt(
            panel[32:], jnp.concatenate([zero, panel], axis=0)
        )

    @pl.when(owner)
    def _():
        pl.semaphore_wait(barrier, 61)

    @pl.when(jnp.logical_not(owner))
    def _():
        pl.semaphore_wait(barrier, 46)

    def send_col(part):
        rows = pl.ds(192 * part, 192)

        def to(q):
            other = 2 * spiral(q, 8) + jnp.where(q == 7, 1, 0)
            copy(a_v.at[rows], colpb.at[rows], colp_s.at[part * 8 + q], colp_r.at[part], (other, c)).start()

        loop(0, 8, to)

    def wait_col(part):
        rows = pl.ds(192 * part, 192)

        @pl.when(r == 0)
        def _():
            colpb[rows, :] = a_v[rows, :]

        @pl.when(r != 0)
        def _():
            copy(a_v.at[rows], colpb.at[rows], colp_s.at[0], colp_r.at[part], (0, c)).wait_recv()

            @pl.when(core == 0)
            def _():
                copy(colpb.at[rows], colpb.at[rows], fwd_s.at[part], colp_r.at[part], (r + 1, c)).start()

    def scatter(part):
        def to(k):
            dev = panel_owner(k) if part == 0 else 4 * lax.div(k, 2) * 1 + 2 * lax.rem(k, 2) + 1 - lax.rem(lax.div(k, 2), 2)
            copy(chunk(k, part), chunk(k, part), sc_s.at[part * 16 + k], sc_r, (r, dev)).start()

        loop(1 - part, 16, to)

    @pl.when(r == 0)
    def _():
        send_col(0)

    @pl.when(c == 0)
    def _():
        scatter(0)

    @pl.when(r == 0)
    def _():
        grecv[c] = gpk[...]
        loop(0, 31, lambda p: copy(gpk, grecv.at[c], g_s.at[p], g_r.at[c], (r, col_peer(p))).start())

    @pl.when(c == 0)
    def _():
        scatter(1)

    @pl.when(r == 0)
    def _():
        send_col(1)

    wait_col(0)

    panel = jnp.concatenate([panel_cols(colpb, s) for s in range(3)], axis=1)
    for t in range(6):
        tile = jnp.concatenate([a_v[pl.ds(t * 384 + s, 128, stride=3), :] for s in range(3)], axis=1)
        zt = dot_nt(panel, tile)
        for g in range(8):
            zpart[g + 8 * (t % 2), t // 2] = zt[8 * g : 8 * g + 8, :]

    def reduce_to(p):
        k = lax.rem(z + spiral(lax.div(p, 2), 8), 8) * 2 + lax.rem(p, 2)
        dev = panel_owner(k)

        @pl.when(dev != c)
        def _():
            copy(zpart.at[k], zrecv.at[c], rs_s.at[k], rs_r.at[c], (r, dev)).start()

    loop(0, 16, reduce_to)

    part = jnp.where(owner, 0, 1)

    @pl.when(c != 0)
    def _():
        copy(chunk(mine, part), chunk(mine, part), sc_s.at[0], sc_r, (r, 0)).wait_recv()

    def pass_on(p):
        dev = col_peer(p)

        @pl.when(dev != 0)
        def _():
            copy(chunk(mine, part), chunk(mine, part), ag_s.at[p], ag_r.at[mine + 16 * part], (r, dev)).start()

    loop(0, 31, pass_on)

    def wait_rows(part):
        def one(k):
            @pl.when((c != 0) & ((k != mine) | (owner != (part == 0))))
            def _():
                copy(chunk(k, part), chunk(k, part), ag_s.at[0], ag_r.at[k + 16 * part], (r, 0)).wait_recv()

        loop(0, 16, one)

    wait_col(1)

    @pl.when(r == 0)
    def _():
        def arrived(p):
            dev = col_peer(p)
            copy(gpk, grecv.at[dev], g_s.at[p], g_r.at[dev], (r, dev)).wait_recv()

        loop(0, 31, arrived)
        gfin[...] = lax.fori_loop(1, 32, lambda i, total: total + grecv[i], grecv[0])
        loop(0, 15, lambda p: copy(gfin, gfin, gb_s.at[p], gb_r, (row_peer(p), c)).start())

    def send_corner(part):
        rows = pl.ds(NB * part, NB)

        @pl.when(r == 0)
        def _():
            p1[rows, :] = rowpb[0, 0, rows, :]

            def to(p):
                copy(p1.at[rows], p1.at[rows], p1_s.at[15 * part + p], p1_r.at[part], (row_peer(p), c)).start()

            loop(0, 15, to)

    def wait_corner(part):
        rows = pl.ds(NB * part, NB)

        @pl.when(r != 0)
        def _():
            copy(p1.at[rows], p1.at[rows], p1_s.at[0], p1_r.at[part], (0, c)).wait_recv()

    @pl.when(owner)
    def _():
        def arrived(p):
            dev = col_peer(p)
            copy(zpart.at[0], zrecv.at[dev], rs_s.at[0], rs_r.at[dev], (r, dev)).wait_recv()

        loop(0, 31, arrived)
        zrecv[c] = zpart[mine]
        zsum = lax.fori_loop(1, 32, lambda i, total: total + zrecv[i], zrecv[0])
        zrows[mine] = zsum
        there = r + 16 * my_h

        def to_cols(p):
            copy(zrows.at[mine], zcols.at[my_g], zc_s.at[p], zc_r.at[my_g], (row_peer(p), there)).start()

        loop(0, 15, to_cols)
        loop(
            0, 31, lambda p: copy(zrows.at[mine], zrows.at[mine], zr_s.at[p], zr_r.at[mine], (r, col_peer(p))).start()
        )
        wait_rows(0)
        send_corner(0)
        total = jnp.zeros((8, 128), F32)
        for i in range(3):
            rows = rowpb[my_h, i, 0:NB, :]
            total = total + dot_nt(zsum[i], jnp.concatenate([rows, jnp.zeros_like(rows)], axis=0))
        lane8 = lax.broadcasted_iota(jnp.int32, (8, 128), 1)
        total = total + jnp.where((r == 0) & (my_h == 0) & (lane8 >= NB), zsum[0], 0.0)
        hsend[0] = total
        hrecv[r] = total
        loop(
            0, 15, lambda p: copy(hsend.at[0], hrecv.at[r], h_s.at[p], h_r.at[r], (row_peer(p), c)).start()
        )

        def h_arrived(p):
            dev = row_peer(p)
            copy(hsend.at[0], hrecv.at[dev], h_s.at[0], h_r.at[dev], (dev, c)).wait_recv()

        loop(0, 15, h_arrived)
        hsum = lax.fori_loop(1, 16, lambda i, total: total + hrecv[i], hrecv[0])
        hall[mine] = hsum
        loop(0, 31, lambda p: copy(hall.at[mine], hall.at[mine], ha_s.at[p], ha_r.at[mine], (r, col_peer(p))).start())
        wait_rows(1)
        send_corner(1)

        @pl.when(r != 0)
        def _():
            copy(gfin, gfin, gb_s.at[0], gb_r, (0, c)).wait_recv()

        wait_corner(0)
        copy(c0, c0, c0_s.at[0], c0_r.at[0], (r, partner)).wait_recv()
        copy(om, om, c0_s.at[1], c0_r.at[1], (r, partner)).wait_recv()

    @pl.when(jnp.logical_not(owner))
    def _():
        wait_rows(0)
        send_corner(0)

        @pl.when(r != 0)
        def _():
            copy(gfin, gfin, gb_s.at[0], gb_r, (0, c)).wait_recv()

        packed = gfin[...]
        gram = jnp.concatenate([packed, pltpu.roll(packed, 64, 1)], axis=0)
        gram = jnp.where(lane < NB, gram, 0.0)
        ct[0:NB, :] = jnp.zeros((NB, 128), F32)
        factor_cholesky(gram, ct)
        c0[...] = jnp.transpose(ct[...])[0:NB, :]
        copy(c0, c0, c0_s.at[0], c0_r.at[0], (r, partner)).start()
        wait_corner(0)
        corner = p1[0:NB, :]
        om[...] = invert(gram + dot_nt(c0[...], jnp.concatenate([corner, jnp.zeros_like(corner)], axis=0)))
        copy(om, om, c0_s.at[1], c0_r.at[1], (r, partner)).start()
        wait_rows(1)
        send_corner(1)

    def z_arrived(k):
        @pl.when(jnp.logical_not(owner) | (k != mine))
        def _():
            copy(zrows.at[k], zrows.at[k], zr_s.at[0], zr_r.at[k], (r, c)).wait_recv()

    loop(0, 16, z_arrived)

    @pl.when(home)
    def _():
        zcols[...] = zrows[pl.ds(8 * lax.div(c, 16), 8)]

    @pl.when(jnp.logical_not(home))
    def _():
        loop(0, 8, lambda g: copy(zcols.at[g], zcols.at[g], zc_s.at[0], zc_r.at[g], (r, c)).wait_recv())

    @pl.when(r == 0)
    def _():
        def sent(part):
            rows = pl.ds(192 * part, 192)
            loop(
                0, 8,
                lambda q: copy(a_v.at[rows], colpb.at[rows], colp_s.at[8 * part + q], colp_r.at[part], (1, c)).wait_send(),
            )

        sent(0)
        sent(1)

    wait_corner(1)
    sub = lax.broadcasted_iota(jnp.int32, (NB, 128), 0)
    c0v = c0[...]
    unit = jnp.where(sub == lane, 1.0, 0.0)
    pad = jnp.zeros((NB, 128), F32)
    s_mat = dot_nn(om[...], jnp.concatenate([unit + c0v, pad], axis=0))
    c_cols = jnp.where(c == 0, c0v, 0.0)
    c_rows = jnp.where(r == 0, c0v, 0.0)

    def h_all(k):
        @pl.when(jnp.logical_not(owner) | (k != mine))
        def _():
            copy(hall.at[k], hall.at[k], ha_s.at[0], ha_r.at[k], (r, c)).wait_recv()

    loop(0, 16, h_all)
    top = (hall[0:8] + hall[8:16]).reshape(NB, 128)
    turned = jnp.transpose(jnp.concatenate([top, pad], axis=0))
    bottom = jnp.where(lane < NB, turned[NB:, :], p1[NB:, :])
    x_mat = dot_nt(dot_nn(s_mat, jnp.concatenate([top, bottom], axis=0)), jnp.concatenate([s_mat, pad], axis=0))
    right = []
    for s in range(3):
        n_t = panel_cols(colpb, s)
        if s == 0:
            n_t = n_t + c_cols
        zb = jnp.concatenate([zcols[:, s].reshape(NB, 128), colpb[pl.ds(192 + s, NB, stride=3), :]], axis=0)
        v_t = dot_nn(s_mat, zb) - dot_nn(x_mat, jnp.concatenate([n_t, pad], axis=0))
        right.append(jnp.concatenate([n_t, v_t], axis=0))
    right = jnp.concatenate(right, axis=1)
    for t in range(6):
        h, i = t % 2, t // 2
        n_t = rowpb[h, i, 0:NB, :]
        if t == 0:
            n_t = n_t + c_rows
        zb = jnp.concatenate([zrows[8 * h : 8 * h + 8, i].reshape(NB, 128), rowpb[h, i, NB:, :]], axis=0)
        left = jnp.transpose(jnp.concatenate([dot_nn(s_mat, zb), n_t], axis=0))
        change = dot_nn(left, right)
        for s in range(3):
            rows = pl.ds(t * 384 + s, 128, stride=3)
            a_v[rows, :] = a_v[rows, :] - change[:, 128 * s : 128 * s + 128]
        rows = pl.ds(t * 384, 384)
        pltpu.make_async_copy(a_v.at[rows], o_hbm.at[rows], out_sem.at[t]).start()

    @pl.when(r == 0)
    def _():
        loop(0, 31, lambda p: copy(gpk, grecv.at[c], g_s.at[p], g_r.at[c], (r, col_peer(p))).wait_send())
        loop(0, 15, lambda p: copy(gfin, gfin, gb_s.at[p], gb_r, (row_peer(p), c)).wait_send())
        rows = pl.ds(0, NB)
        loop(0, 30, lambda p: copy(p1.at[rows], p1.at[rows], p1_s.at[p], p1_r.at[0], (1, c)).wait_send())

    @pl.when((r != 0) & (core == 0))
    def _():
        rows = pl.ds(0, 192)
        loop(0, 2, lambda q: copy(colpb.at[rows], colpb.at[rows], fwd_s.at[q], colp_r.at[0], (r + 1, c)).wait_send())

    @pl.when(c == 0)
    def _():
        loop(1, 32, lambda k: copy(chunk(0, 0), chunk(0, 0), sc_s.at[k], sc_r, (r, 1)).wait_send())

    def reduced_sent(k):
        @pl.when(panel_owner(k) != c)
        def _():
            copy(zpart.at[k], zrecv.at[c], rs_s.at[k], rs_r.at[c], (r, panel_owner(k))).wait_send()

    loop(0, 16, reduced_sent)

    def passed_on(p):
        dev = col_peer(p)

        @pl.when(dev != 0)
        def _():
            copy(chunk(mine, part), chunk(mine, part), ag_s.at[p], ag_r.at[0], (r, dev)).wait_send()

    loop(0, 31, passed_on)

    @pl.when(owner)
    def _():
        loop(0, 15, lambda p: copy(zrows.at[mine], zcols.at[my_g], zc_s.at[p], zc_r.at[0], (row_peer(p), c)).wait_send())
        loop(0, 31, lambda p: copy(zrows.at[mine], zrows.at[0], zr_s.at[p], zr_r.at[0], (r, col_peer(p))).wait_send())
        loop(0, 15, lambda p: copy(hsend.at[0], hrecv.at[r], h_s.at[p], h_r.at[r], (row_peer(p), c)).wait_send())
        loop(0, 31, lambda p: copy(hall.at[mine], hall.at[0], ha_s.at[p], ha_r.at[0], (r, col_peer(p))).wait_send())

    @pl.when(jnp.logical_not(owner))
    def _():
        copy(c0, c0, c0_s.at[0], c0_r.at[0], (r, partner)).wait_send()
        copy(om, om, c0_s.at[1], c0_r.at[1], (r, partner)).wait_send()

    def stored(t):
        rows = pl.ds(0, 384)
        pltpu.make_async_copy(a_v.at[rows], o_hbm.at[rows], out_sem.at[t]).wait()

    loop(0, 6, stored)


def vmem(*shape):
    return pltpu.VMEM(shape, F32)


def dma(*shape):
    return pltpu.SemaphoreType.DMA(shape)


def body(hessian):
    flat = hessian.reshape(2304, 128)
    out = pl.pallas_call(
        kernel,
        out_shape=jax.ShapeDtypeStruct((2304, 128), F32),
        in_specs=[pl.BlockSpec(memory_space=pl.ANY)],
        out_specs=pl.BlockSpec(memory_space=pl.ANY),
        scratch_shapes=[
            vmem(2304, 128), vmem(384, 128), vmem(2, 3, 128, 128), vmem(16, 3, 8, 128), vmem(32, 3, 8, 128),
            vmem(16, 3, 8, 128), vmem(8, 3, 8, 128), vmem(32, 128), vmem(32, 32, 128), vmem(32, 128), vmem(128, 128),
            vmem(1, 8, 128), vmem(16, 8, 128), vmem(16, 8, 128), vmem(128, 128), vmem(64, 128), vmem(64, 128),
            dma(), dma(6), dma(16), dma(2), dma(2), dma(32), dma(), dma(31), dma(32), dma(16), dma(32), dma(31), dma(16),
            dma(15), dma(8), dma(31), dma(32), dma(15), dma(), dma(30), dma(2), dma(15), dma(16), dma(31), dma(16),
            dma(2), dma(2),
        ],
        compiler_params=pltpu.CompilerParams(collective_id=0, has_side_effects=True, vmem_limit_bytes=32 << 20),
        name="panel",
    )(flat)
    return out.reshape(hessian.shape)


def solution(mesh):
    return jax.shard_map(
        body,
        mesh=mesh,
        in_specs=(P(None, "row", None, None, "col", None),),
        out_specs=P(None, "row", None, None, "col", None),
        check_vma=False,
    )
```

```python
import functools

import jax
import jax.numpy as jnp
from jax import lax
from jax.experimental import pallas as pl
from jax.experimental.pallas import tpu as pltpu
from jax.sharding import PartitionSpec as P

NB = 64
MESH = pl.DeviceIdType.MESH
HIGHEST = lax.Precision.HIGHEST
F32 = jnp.float32


def dot_nn(a, b):
    return lax.dot_general(a, b, (((1,), (0,)), ((), ())), precision=HIGHEST, preferred_element_type=F32)


def dot_nt(a, b):
    return lax.dot_general(a, b, (((1,), (1,)), ((), ())), precision=HIGHEST, preferred_element_type=F32)


def split(a):
    high = a.astype(jnp.bfloat16)
    return high, (a - high.astype(F32)).astype(jnp.bfloat16)


def dot3(a, b, dims):
    (ah, al), (bh, bl) = split(a), split(b)
    left = jnp.concatenate([ah, ah, al], axis=dims[0])
    right = jnp.concatenate([bh, bl, bh], axis=dims[1])
    return lax.dot_general(left, right, (((dims[0],), (dims[1],)), ((), ())), preferred_element_type=F32)


def spiral(q, n):
    return lax.rem(n // 2 + (1 - 2 * lax.rem(q, 2)) * lax.div(q + 1, 2), n)


def loop(lo, hi, f):
    def step(i, carry):
        f(i)
        return carry

    lax.fori_loop(lo, hi, step, 0)


def factor_cholesky(g, ct):
    lane1 = lax.broadcasted_iota(jnp.int32, (1, 128), 1)
    for k in range(NB):
        col = g[:, k : k + 1]
        row = g[k : k + 1, :]
        piv = g[k : k + 1, k : k + 1]
        ct[NB + k : NB + k + 1, :] = jnp.where((lane1 >= k) & (lane1 < NB), row * lax.rsqrt(piv), 0.0)
        if k < NB - 1:
            low = (k + 1) // 8 * 8
            part = g[low:, :] - col[low:, :] * (row / piv)
            g = part if low == 0 else jnp.concatenate([g[:low, :], part], axis=0)


def invert(m):
    lane1 = lax.broadcasted_iota(jnp.int32, (1, 128), 1)
    lane = lax.broadcasted_iota(jnp.int32, (NB, 128), 1)
    sub = lax.broadcasted_iota(jnp.int32, (NB, 128), 0)
    for k in range(NB):
        col = m[:, k : k + 1]
        row = m[k : k + 1, :]
        piv = m[k : k + 1, k : k + 1]
        scaled = jnp.where(lane1 == k, 1.0, row) / piv
        m = jnp.where(sub == k, scaled, jnp.where(lane == k, 0.0, m) - col * scaled)
    return m


def kernel(
    a_hbm, left_o, right_o, a_v, colpb, rowpb, zpart, zrecv, zrows, zcols, gx, gz, gfin, p1, hsend, hrecv, hall, ct, c0, om,
    load_s, colp_s, colp_r, fwd_s, sc_s, sc_r, ag_s, ag_r, rs_s, rs_r, zr_s, zr_r, zc_s, zc_r,
    g_s, g_r, p1_s, p1_r, h_s, h_r, ha_s, ha_r, c0_s, c0_r,
):
    r, c = lax.axis_index("row"), lax.axis_index("col")
    y, core = lax.div(r, 2), lax.rem(r, 2)
    z, x = lax.div(c, 4), lax.rem(c, 4)
    mine = lax.div(c, 2)
    owner = lax.rem(x + z, 2) == 0
    plain = jnp.logical_not(owner)
    my_g, my_h = lax.rem(mine, 8), lax.div(mine, 8)
    partner = c + 1 - 2 * lax.rem(c, 2)
    home = lax.rem(c, 16) == r
    lane = lax.broadcasted_iota(jnp.int32, (NB, 128), 1)

    def panel_owner(k):
        return 2 * k + lax.rem(lax.div(k, 2), 2)

    def other_owner(k):
        return 2 * k + 1 - lax.rem(lax.div(k, 2), 2)

    def col_peer(p):
        return lax.rem(z + spiral(lax.div(p, 4), 8), 8) * 4 + lax.rem(x + spiral(lax.rem(p, 4), 4), 4)

    def x_peer(p):
        return z * 4 + lax.rem(x + spiral(p, 4), 4)

    def z_peer(p):
        return lax.rem(z + spiral(p, 8), 8) * 4 + x

    def row_peer(p):
        return lax.rem(y + spiral(lax.div(p, 2), 8), 8) * 2 + lax.rem(core + 1 - lax.rem(p, 2), 2)

    def copy(src, dst, ssem, rsem, dev):
        return pltpu.make_async_remote_copy(
            src_ref=src, dst_ref=dst, send_sem=ssem, recv_sem=rsem, device_id=dev, device_id_type=MESH
        )

    def sent(ref, sem):
        copy(ref, ref, sem, sem, (r, partner)).wait_send()

    def arrived(ref, sem):
        copy(ref, ref, sem, sem, (r, partner)).wait_recv()

    def when(condition, f):
        pl.when(condition)(f)

    def chunk(k, part):
        rows = pl.multiple_of(lax.rem(k, 8) * 8 + part * NB, 8)
        return rowpb.at[lax.div(k, 8), :, pl.ds(rows, 8), :]

    def some(n):
        return zrecv.at[pl.ds(0, n)]

    load = pltpu.make_async_copy(a_hbm, a_v, load_s)
    load.start()
    barrier = pltpu.get_barrier_semaphore()

    def greet(dev):
        pl.semaphore_signal(barrier, inc=1, device_id=dev, device_id_type=MESH)

    loop(0, 31, lambda p: greet((r, col_peer(p))))
    loop(0, 15, lambda p: greet((row_peer(p), c)))

    @pl.when(jnp.logical_not(home))
    def _():
        loop(0, 8, lambda g: greet((lax.rem(c, 16), panel_owner(g + 8 * lax.div(c, 16)))))

    load.wait()

    def panel_cols(ref, s):
        return jnp.where((c == 0) & (s == 0) & (lane < NB), 0.0, ref[pl.ds(s, NB, stride=3), :])

    @pl.when(c == 0)
    def _():
        full = lax.broadcasted_iota(jnp.int32, (128, 128), 0)
        full_lane = lax.broadcasted_iota(jnp.int32, (128, 128), 1)
        for t in range(6):
            block = jnp.transpose(a_v[pl.ds(t * 384, 128, stride=3), :])
            if t == 0:
                block = jnp.where((r == 0) & (full < NB) & (full_lane < NB), 0.0, block)
            rowpb[t % 2, t // 2] = block

    @pl.when(r == 0)
    def _():
        panel = jnp.concatenate([panel_cols(a_v, s) for s in range(3)], axis=1)
        zero = jnp.zeros_like(panel)
        gx[x] = dot_nt(panel[:32], jnp.concatenate([panel, zero], axis=0)) + dot_nt(
            panel[32:], jnp.concatenate([zero, panel], axis=0)
        )

        @pl.when(c == 0)
        def _():
            p1[...] = a_v[pl.ds(3 * NB, NB, stride=3), :]

        colpb[...] = a_v[0:384, :]

    when(owner, lambda: pl.semaphore_wait(barrier, 61))
    when(plain, lambda: pl.semaphore_wait(barrier, 46))

    def send_col(part):
        rows = pl.ds(192 * part, 192)

        def to(q):
            other = 2 * spiral(q, 8) + jnp.where(q == 7, 1, 0)
            copy(a_v.at[rows], colpb.at[rows], colp_s.at[part], colp_r.at[part], (other, c)).start()

        loop(0, 8, to)

    def wait_col(part):
        rows = pl.ds(192 * part, 192)

        @pl.when(r != 0)
        def _():
            arrived(colpb.at[rows], colp_r.at[part])

            @pl.when(core == 0)
            def _():
                copy(colpb.at[rows], colpb.at[rows], fwd_s.at[part], colp_r.at[part], (r + 1, c)).start()

    def scatter(part):
        def to(k):
            dev = panel_owner(k) if part == 0 else other_owner(k)
            copy(chunk(k, part), chunk(k, part), sc_s, sc_r, (r, dev)).start()

        loop(1 - part, 16, to)

    when(r == 0, lambda: send_col(0))
    when(c == 0, lambda: scatter(0))

    @pl.when(r == 0)
    def _():
        loop(0, 3, lambda p: copy(gx.at[x], gx.at[x], g_s.at[0], g_r.at[0], (r, x_peer(p))).start())

        @pl.when(c == 0)
        def _():
            loop(0, 3, lambda p: copy(p1, p1, p1_s.at[0], p1_r, (r, x_peer(p))).start())

    when(c == 0, lambda: scatter(1))
    when(r == 0, lambda: send_col(1))

    wait_col(0)

    panel = jnp.concatenate([panel_cols(colpb, s) for s in range(3)], axis=1)
    for t in range(6):
        tile = jnp.concatenate([a_v[pl.ds(t * 384 + s, 128, stride=3), :] for s in range(3)], axis=1)
        zt = dot3(panel, tile, (1, 1))
        for g in range(8):
            zpart[g + 8 * (t % 2), t // 2] = zt[8 * g : 8 * g + 8, :]

    def reduce_to(p):
        k = lax.rem(z + spiral(lax.div(p, 2), 8), 8) * 2 + lax.rem(p, 2)
        dev = panel_owner(k)

        @pl.when(dev != c)
        def _():
            copy(zpart.at[k], zrecv.at[c], rs_s, rs_r, (r, dev)).start()

    loop(0, 16, reduce_to)

    @pl.when(r == 0)
    def _():
        arrived(gx.at[pl.ds(0, 3)], g_r.at[0])
        gz[z] = (gx[0] + gx[1]) + (gx[2] + gx[3])
        loop(0, 7, lambda p: copy(gz.at[z], gz.at[z], g_s.at[1], g_r.at[1], (r, z_peer(p))).start())

        @pl.when(z == 0)
        def _():
            when(x != 0, lambda: arrived(p1, p1_r))
            loop(0, 7, lambda p: copy(p1, p1, p1_s.at[1], p1_r, (r, z_peer(p))).start())

    def pass_on(part):
        when(c != 0, lambda: arrived(chunk(mine, part), sc_r))

        def to(p):
            dev = col_peer(p)

            @pl.when(dev != 0)
            def _():
                copy(chunk(mine, part), chunk(mine, part), ag_s, ag_r.at[part], (r, dev)).start()

        loop(0, 31, to)

    def wait_rows(part):
        holds = owner if part == 0 else plain
        when((c != 0) & holds, lambda: arrived(some(15), ag_r.at[part]))
        when((c != 0) & jnp.logical_not(holds), lambda: arrived(some(16), ag_r.at[part]))

    when(owner, lambda: pass_on(0))

    @pl.when(r == 0)
    def _():
        arrived(gz.at[pl.ds(0, 7)], g_r.at[1])
        gfin[...] = ((gz[0] + gz[1]) + (gz[2] + gz[3])) + ((gz[4] + gz[5]) + (gz[6] + gz[7]))
        loop(0, 15, lambda p: copy(gfin, gfin, g_s.at[2], g_r.at[2], (row_peer(p), c)).start())
        when(z != 0, lambda: arrived(p1, p1_r))
        loop(0, 15, lambda p: copy(p1, p1, p1_s.at[2], p1_r, (row_peer(p), c)).start())

    wait_col(1)

    @pl.when(owner)
    def _():
        arrived(some(31), rs_r)
        zrecv[c] = zpart[mine]
        zsum = lax.fori_loop(1, 32, lambda i, total: total + zrecv[i], zrecv[0])
        zrows[mine] = zsum
        wait_rows(0)
        rows = jnp.concatenate([rowpb[my_h, i, 0:NB, :] for i in range(3)], axis=1)
        total = dot_nt(
            jnp.concatenate([zsum[i] for i in range(3)], axis=1), jnp.concatenate([rows, jnp.zeros_like(rows)], axis=0)
        )
        lane8 = lax.broadcasted_iota(jnp.int32, (8, 128), 1)
        total = total + jnp.where((r == 0) & (my_h == 0) & (lane8 >= NB), zsum[0], 0.0)
        hsend[0] = total
        hrecv[r] = total
        loop(0, 15, lambda p: copy(hsend.at[0], hrecv.at[r], h_s, h_r, (row_peer(p), c)).start())
        there = r + 16 * my_h
        loop(0, 15, lambda p: copy(zrows.at[mine], zcols.at[my_g], zc_s, zc_r, (row_peer(p), there)).start())
        loop(0, 31, lambda p: copy(zrows.at[mine], zrows.at[mine], zr_s, zr_r, (r, col_peer(p))).start())
        arrived(hrecv.at[pl.ds(0, 15)], h_r)
        hall[mine] = lax.fori_loop(1, 16, lambda i, total: total + hrecv[i], hrecv[0])
        loop(0, 31, lambda p: copy(hall.at[mine], hall.at[mine], ha_s, ha_r, (r, col_peer(p))).start())
        wait_rows(1)

        @pl.when(r != 0)
        def _():
            arrived(gfin, g_r.at[2])
            arrived(p1, p1_r)

        arrived(c0, c0_r.at[0])
        arrived(om, c0_r.at[1])

    @pl.when(plain)
    def _():
        pass_on(1)
        when(r != 0, lambda: arrived(gfin, g_r.at[2]))
        packed = gfin[...]
        gram = jnp.concatenate([packed, pltpu.roll(packed, 64, 1)], axis=0)
        gram = jnp.where(lane < NB, gram, 0.0)
        ct[0:NB, :] = jnp.zeros((NB, 128), F32)
        factor_cholesky(gram, ct)
        c0[...] = jnp.transpose(ct[...])[0:NB, :]
        copy(c0, c0, c0_s.at[0], c0_r.at[0], (r, partner)).start()
        when(r != 0, lambda: arrived(p1, p1_r))
        corner = p1[...]
        product = dot_nn(pltpu.roll(c0[...], 64, 1), jnp.concatenate([corner, jnp.zeros_like(corner)], axis=0))
        om[...] = invert(gram + jnp.where(lane < NB, product, 0.0))
        copy(om, om, c0_s.at[1], c0_r.at[1], (r, partner)).start()
        wait_rows(0)
        wait_rows(1)

    sub = lax.broadcasted_iota(jnp.int32, (NB, 128), 0)
    c0v = c0[...]
    unit = jnp.where(sub == lane, 1.0, 0.0)
    pad = jnp.zeros((NB, 128), F32)
    s_mat = dot_nn(om[...], jnp.concatenate([unit + c0v, pad], axis=0))
    c_cols = jnp.where(c == 0, c0v, 0.0)
    c_rows = jnp.where(r == 0, c0v, 0.0)

    when(owner, lambda: arrived(some(15), zr_r))
    when(plain, lambda: arrived(some(16), zr_r))

    zb = []
    for t in range(6):
        h, i = t % 2, t // 2
        zb.append(
            jnp.concatenate([zrows[8 * h : 8 * h + 8, i].reshape(NB, 128), rowpb[h, i, NB:, :]], axis=0)
        )
        n_t = rowpb[h, i, 0:NB, :]
        if t == 0:
            n_t = n_t + c_rows
        left_o[t, NB:, :] = n_t
    w_rows = dot_nn(s_mat, jnp.concatenate(zb, axis=1))
    for t in range(6):
        left_o[t, 0:NB, :] = w_rows[:, 128 * t : 128 * t + 128]

    @pl.when(home)
    def _():
        zcols[...] = zrows[pl.ds(8 * lax.div(c, 16), 8)]

    when(jnp.logical_not(home), lambda: arrived(zcols, zc_r))

    zb = [
        jnp.concatenate([zcols[:, s].reshape(NB, 128), colpb[pl.ds(192 + s, NB, stride=3), :]], axis=0) for s in range(3)
    ]
    w_cols = dot_nn(s_mat, jnp.concatenate(zb, axis=1))
    n_cols = [panel_cols(colpb, s) for s in range(3)]
    n_cols = jnp.concatenate([n_cols[0] + c_cols] + n_cols[1:], axis=1)
    right_o[0:NB, :] = n_cols

    when(owner, lambda: arrived(hall.at[pl.ds(0, 15)], ha_r))
    when(plain, lambda: arrived(hall, ha_r))

    top = (hall[0:8] + hall[8:16]).reshape(NB, 128)
    turned = jnp.transpose(jnp.concatenate([top, pad], axis=0))
    bottom = jnp.where(lane < NB, turned[NB:, :], p1[...])
    x_mat = dot_nt(dot_nn(s_mat, jnp.concatenate([top, bottom], axis=0)), jnp.concatenate([s_mat, pad], axis=0))
    right_o[NB:, :] = w_cols - dot_nn(x_mat, jnp.concatenate([n_cols, jnp.zeros_like(n_cols)], axis=0))

    @pl.when(r == 0)
    def _():
        for part in range(2):
            sent(a_v.at[pl.ds(0, 1536)], colp_s.at[part])
        sent(gx.at[pl.ds(0, 3)], g_s.at[0])
        sent(gz.at[pl.ds(0, 7)], g_s.at[1])
        sent(a_v.at[pl.ds(0, 15 * 32)], g_s.at[2])
        when(c == 0, lambda: sent(a_v.at[pl.ds(0, 3 * NB)], p1_s.at[0]))
        when(z == 0, lambda: sent(a_v.at[pl.ds(0, 7 * NB)], p1_s.at[1]))
        sent(a_v.at[pl.ds(0, 15 * NB)], p1_s.at[2])

    @pl.when((r != 0) & (core == 0))
    def _():
        for part in range(2):
            sent(colpb.at[pl.ds(0, 192)], fwd_s.at[part])

    @pl.when(c == 0)
    def _():
        sent(some(31), sc_s)
        sent(some(31), ag_s)

    when(c != 0, lambda: sent(some(30), ag_s))

    @pl.when(owner)
    def _():
        sent(some(15), rs_s)
        sent(some(15), zc_s)
        sent(some(31), zr_s)
        sent(a_v.at[pl.ds(0, 15 * 8)], h_s)
        sent(a_v.at[pl.ds(0, 31 * 8)], ha_s)

    @pl.when(plain)
    def _():
        sent(some(16), rs_s)
        sent(c0, c0_s.at[0])
        sent(om, c0_s.at[1])


def update(a, left, right, out):
    high, low = split(right[...])
    columns = jnp.concatenate([high, low, high], axis=0)
    for t in range(6):
        high, low = split(jnp.transpose(left[t]))
        change = jnp.dot(jnp.concatenate([high, high, low], axis=1), columns, preferred_element_type=F32)
        for s in range(3):
            rows = pl.ds(t * 384 + s, 128, stride=3)
            out[rows, :] = a[rows, :] - change[:, 128 * s : 128 * s + 128]


def vmem(*shape):
    return pltpu.VMEM(shape, F32)


def dma(*shape):
    return pltpu.SemaphoreType.DMA(shape)


def body(hessian):
    flat = hessian.reshape(2304, 128)
    whole = pl.BlockSpec(memory_space=pltpu.VMEM)
    left, right = pl.pallas_call(
        kernel,
        out_shape=[jax.ShapeDtypeStruct((6, 128, 128), F32), jax.ShapeDtypeStruct((128, 384), F32)],
        in_specs=[pl.BlockSpec(memory_space=pltpu.HBM)],
        out_specs=[whole, whole],
        scratch_shapes=[
            vmem(2304, 128), vmem(384, 128), vmem(2, 3, 128, 128), vmem(16, 3, 8, 128), vmem(32, 3, 8, 128),
            vmem(16, 3, 8, 128), vmem(8, 3, 8, 128), vmem(4, 32, 128), vmem(8, 32, 128), vmem(32, 128),
            vmem(64, 128), vmem(1, 8, 128), vmem(16, 8, 128), vmem(16, 8, 128), vmem(128, 128), vmem(64, 128), vmem(64, 128),
            dma(), dma(2), dma(2), dma(2), dma(), dma(), dma(), dma(2), dma(), dma(), dma(), dma(), dma(), dma(),
            dma(3), dma(3), dma(3), dma(), dma(), dma(), dma(), dma(), dma(2), dma(2),
        ],
        compiler_params=pltpu.CompilerParams(collective_id=0, has_side_effects=True, vmem_limit_bytes=32 << 20),
        name="panel",
    )(flat)
    out = pl.pallas_call(
        update,
        out_shape=jax.ShapeDtypeStruct((2304, 128), F32),
        in_specs=[whole, whole, whole],
        out_specs=whole,
        compiler_params=pltpu.CompilerParams(vmem_limit_bytes=16 << 20),
        name="update",
    )(flat, left, right)
    return out.reshape(hessian.shape)


def solution(mesh):
    return jax.shard_map(
        body,
        mesh=mesh,
        in_specs=(P(None, "row", None, None, "col", None),),
        out_specs=P(None, "row", None, None, "col", None),
        check_vma=False,
    )
```

```python
import functools

import jax
import jax.numpy as jnp
from jax import lax
from jax.experimental import pallas as pl
from jax.experimental.pallas import tpu as pltpu
from jax.sharding import PartitionSpec as P

NB = 64
MESH = pl.DeviceIdType.MESH
HIGHEST = lax.Precision.HIGHEST
F32 = jnp.float32


def dot_nn(a, b):
    return lax.dot_general(a, b, (((1,), (0,)), ((), ())), precision=HIGHEST, preferred_element_type=F32)


def dot_nt(a, b):
    return lax.dot_general(a, b, (((1,), (1,)), ((), ())), precision=HIGHEST, preferred_element_type=F32)


def split(a):
    high = a.astype(jnp.bfloat16)
    return high, (a - high.astype(F32)).astype(jnp.bfloat16)


def dot3(a, b, dims):
    (ah, al), (bh, bl) = split(a), split(b)
    left = jnp.concatenate([ah, ah, al], axis=dims[0])
    right = jnp.concatenate([bh, bl, bh], axis=dims[1])
    return lax.dot_general(left, right, (((dims[0],), (dims[1],)), ((), ())), preferred_element_type=F32)


def split(a):
    high = a.astype(jnp.bfloat16)
    return high, (a - high.astype(F32)).astype(jnp.bfloat16)


def dot3(a, b, dims):
    (ah, al), (bh, bl) = split(a), split(b)
    left = jnp.concatenate([ah, ah, al], axis=dims[0])
    right = jnp.concatenate([bh, bl, bh], axis=dims[1])
    return lax.dot_general(left, right, (((dims[0],), (dims[1],)), ((), ())), preferred_element_type=F32)


def split(a):
    high = a.astype(jnp.bfloat16)
    return high, (a - high.astype(F32)).astype(jnp.bfloat16)


def dot3(a, b, dims):
    (ah, al), (bh, bl) = split(a), split(b)
    left = jnp.concatenate([ah, ah, al], axis=dims[0])
    right = jnp.concatenate([bh, bl, bh], axis=dims[1])
    return lax.dot_general(left, right, (((dims[0],), (dims[1],)), ((), ())), preferred_element_type=F32)


def spiral(q, n):
    return lax.rem(n // 2 + (1 - 2 * lax.rem(q, 2)) * lax.div(q + 1, 2), n)


def loop(lo, hi, f):
    def step(i, carry):
        f(i)
        return carry

    lax.fori_loop(lo, hi, step, 0)


def factor_cholesky(g, ct):
    lane1 = lax.broadcasted_iota(jnp.int32, (1, 128), 1)
    for k in range(NB):
        col = g[:, k : k + 1]
        row = g[k : k + 1, :]
        piv = g[k : k + 1, k : k + 1]
        ct[NB + k : NB + k + 1, :] = jnp.where((lane1 >= k) & (lane1 < NB), row * lax.rsqrt(piv), 0.0)
        if k < NB - 1:
            low = (k + 1) // 8 * 8
            part = g[low:, :] - col[low:, :] * (row / piv)
            g = part if low == 0 else jnp.concatenate([g[:low, :], part], axis=0)


def invert(m):
    lane1 = lax.broadcasted_iota(jnp.int32, (1, 128), 1)
    lane = lax.broadcasted_iota(jnp.int32, (NB, 128), 1)
    sub = lax.broadcasted_iota(jnp.int32, (NB, 128), 0)
    for k in range(NB):
        col = m[:, k : k + 1]
        row = m[k : k + 1, :]
        piv = m[k : k + 1, k : k + 1]
        scaled = jnp.where(lane1 == k, 1.0, row) / piv
        m = jnp.where(sub == k, scaled, jnp.where(lane == k, 0.0, m) - col * scaled)
    return m


def kernel(
    a_hbm, left_o, right_o, a_v, colpb, rowpb, zpart, zrecv, zrows, zcols, gx, gz, gfin, p1, hsend, hrecv, hall, ct, c0, om,
    load_s, colp_s, colp_r, fwd_s, sc_s, sc_r, ag_s, ag_r, rs_s, rs_r, zr_s, zr_r, zc_s, zc_r,
    g_s, g_r, p1_s, p1_r, h_s, h_r, ha_s, ha_r, c0_s, c0_r,
):
    r, c = lax.axis_index("row"), lax.axis_index("col")
    y, core = lax.div(r, 2), lax.rem(r, 2)
    z, x = lax.div(c, 4), lax.rem(c, 4)
    mine = lax.div(c, 2)
    owner = lax.rem(x + z, 2) == 0
    plain = jnp.logical_not(owner)
    my_g, my_h = lax.rem(mine, 8), lax.div(mine, 8)
    partner = c + 1 - 2 * lax.rem(c, 2)
    home = lax.rem(c, 16) == r
    lane = lax.broadcasted_iota(jnp.int32, (NB, 128), 1)

    def panel_owner(k):
        return 2 * k + lax.rem(lax.div(k, 2), 2)

    def other_owner(k):
        return 2 * k + 1 - lax.rem(lax.div(k, 2), 2)

    def col_peer(p):
        return lax.rem(z + spiral(lax.div(p, 4), 8), 8) * 4 + lax.rem(x + spiral(lax.rem(p, 4), 4), 4)

    def x_peer(p):
        return z * 4 + lax.rem(x + spiral(p, 4), 4)

    def z_peer(p):
        return lax.rem(z + spiral(p, 8), 8) * 4 + x

    def row_peer(p):
        return lax.rem(y + spiral(lax.div(p, 2), 8), 8) * 2 + lax.rem(core + 1 - lax.rem(p, 2), 2)

    def copy(src, dst, ssem, rsem, dev):
        return pltpu.make_async_remote_copy(
            src_ref=src, dst_ref=dst, send_sem=ssem, recv_sem=rsem, device_id=dev, device_id_type=MESH
        )

    def sent(ref, sem):
        copy(ref, ref, sem, sem, (r, partner)).wait_send()

    def arrived(ref, sem):
        copy(ref, ref, sem, sem, (r, partner)).wait_recv()

    def when(condition, f):
        pl.when(condition)(f)

    def chunk(k, part):
        rows = pl.multiple_of(lax.rem(k, 8) * 8 + part * NB, 8)
        return rowpb.at[lax.div(k, 8), :, pl.ds(rows, 8), :]

    def some(n):
        return zrecv.at[pl.ds(0, n)]

    load = pltpu.make_async_copy(a_hbm, a_v, load_s)
    load.start()
    barrier = pltpu.get_barrier_semaphore()

    def greet(dev):
        pl.semaphore_signal(barrier, inc=1, device_id=dev, device_id_type=MESH)

    loop(0, 15, lambda p: greet((row_peer(p), c)))
    loop(0, 31, lambda p: greet((r, col_peer(p))))

    @pl.when(jnp.logical_not(home))
    def _():
        loop(0, 8, lambda g: greet((lax.rem(c, 16), panel_owner(g + 8 * lax.div(c, 16)))))

    load.wait()

    def panel_cols(ref, s):
        return jnp.where((c == 0) & (s == 0) & (lane < NB), 0.0, ref[pl.ds(s, NB, stride=3), :])

    @pl.when(c == 0)
    def _():
        full = lax.broadcasted_iota(jnp.int32, (128, 128), 0)
        full_lane = lax.broadcasted_iota(jnp.int32, (128, 128), 1)
        for t in range(6):
            block = jnp.transpose(a_v[pl.ds(t * 384, 128, stride=3), :])
            if t == 0:
                block = jnp.where((r == 0) & (full < NB) & (full_lane < NB), 0.0, block)
            rowpb[t % 2, t // 2] = block

    @pl.when(r == 0)
    def _():
        panel = jnp.concatenate([panel_cols(a_v, s) for s in range(3)], axis=1)
        zero = jnp.zeros_like(panel)
        gx[x] = dot_nt(panel[:32], jnp.concatenate([panel, zero], axis=0)) + dot_nt(
            panel[32:], jnp.concatenate([zero, panel], axis=0)
        )

        @pl.when(c == 0)
        def _():
            p1[...] = a_v[pl.ds(3 * NB, NB, stride=3), :]

        colpb[...] = a_v[0:384, :]

    when(owner, lambda: pl.semaphore_wait(barrier, 61))
    when(plain, lambda: pl.semaphore_wait(barrier, 46))

    def send_col(part):
        rows = pl.ds(192 * part, 192)

        def to(q):
            other = 2 * spiral(q, 8) + jnp.where(q == 7, 1, 0)
            copy(a_v.at[rows], colpb.at[rows], colp_s.at[part], colp_r.at[part], (other, c)).start()

        loop(0, 8, to)

    def wait_col(part):
        rows = pl.ds(192 * part, 192)

        @pl.when(r != 0)
        def _():
            arrived(colpb.at[rows], colp_r.at[part])

            @pl.when(core == 0)
            def _():
                copy(colpb.at[rows], colpb.at[rows], fwd_s.at[part], colp_r.at[part], (r + 1, c)).start()

    def scatter(part):
        def to(k):
            dev = panel_owner(k) if part == 0 else other_owner(k)
            copy(chunk(k, part), chunk(k, part), sc_s, sc_r, (r, dev)).start()

        loop(1 - part, 16, to)

    when(r == 0, lambda: send_col(0))
    when(c == 0, lambda: scatter(0))

    @pl.when(r == 0)
    def _():
        loop(0, 3, lambda p: copy(gx.at[x], gx.at[x], g_s.at[0], g_r.at[0], (r, x_peer(p))).start())

        @pl.when(c == 0)
        def _():
            loop(0, 3, lambda p: copy(p1, p1, p1_s.at[0], p1_r, (r, x_peer(p))).start())

    when(c == 0, lambda: scatter(1))
    when(r == 0, lambda: send_col(1))

    wait_col(0)

    panel = jnp.concatenate([panel_cols(colpb, s) for s in range(3)], axis=1)
    for t in range(6):
        tile = jnp.concatenate([a_v[pl.ds(t * 384 + s, 128, stride=3), :] for s in range(3)], axis=1)
        zt = dot3(panel, tile, (1, 1))
        for g in range(8):
            zpart[g + 8 * (t % 2), t // 2] = zt[8 * g : 8 * g + 8, :]

    def reduce_to(p):
        k = lax.rem(z + spiral(lax.div(p, 2), 8), 8) * 2 + lax.rem(p, 2)
        dev = panel_owner(k)

        @pl.when(dev != c)
        def _():
            copy(zpart.at[k], zrecv.at[c], rs_s, rs_r, (r, dev)).start()

    loop(0, 16, reduce_to)

    @pl.when(r == 0)
    def _():
        arrived(gx.at[pl.ds(0, 3)], g_r.at[0])
        gz[z] = (gx[0] + gx[1]) + (gx[2] + gx[3])
        loop(0, 7, lambda p: copy(gz.at[z], gz.at[z], g_s.at[1], g_r.at[1], (r, z_peer(p))).start())

        @pl.when(z == 0)
        def _():
            when(x != 0, lambda: arrived(p1, p1_r))
            loop(0, 7, lambda p: copy(p1, p1, p1_s.at[1], p1_r, (r, z_peer(p))).start())

    def pass_to(k, part, dev, ssem, sem):
        copy(chunk(k, part), chunk(k, part), ag_s.at[ssem], ag_r.at[sem], (r, dev)).start()

    one = jnp.int32(1)
    n_first, n_across, n_b = jnp.int32(0), jnp.int32(0), jnp.int32(0)

    firsts = []
    for p in range(7):
        dev = panel_owner(8 * my_h + lax.rem(my_g + 4 + p + (1 if p > 3 else 0), 8))
        firsts.append((dev, owner & (dev != 0)))
    downs = []
    for p in range(7):
        dev = z_peer(p)
        dev_z = lax.div(dev, 4)
        first = (lax.rem(dev_z + x, 2) == 0) & (lax.div(dev_z, 4) == my_h)
        downs.append((dev, owner & (dev != 0) & jnp.logical_not(first), plain & (dev != 0)))
    acrosses = []
    for p in range(3):
        dev = x_peer(p)
        dev_owner = lax.rem(lax.rem(dev, 4) + z, 2) == 0
        for i in range(4):
            k = 4 * i + 2 * lax.rem(x, 2) + lax.div(x, 2)
            skip = dev_owner & (lax.div(z, 4) == i // 2)
            k_b = 4 * i + 2 * lax.rem(x + 1, 2) + lax.div(x, 2)
            acrosses.append((dev, k, (dev != 0) & jnp.logical_not(skip), k_b, dev != 0))

    @pl.when(owner)
    def _():
        when(c != 0, lambda: arrived(chunk(mine, 0), sc_r))

    for dev, go in firsts:
        when(go, functools.partial(pass_to, mine, 0, dev, 0, 2))
        n_first = n_first + jnp.where(go, one, 0)
    for dev, go, go_b in downs:
        when(go, functools.partial(pass_to, mine, 0, dev, 0, 0))
        n_first = n_first + jnp.where(go, one, 0)

    when(plain, lambda: arrived(chunk(mine, 1), sc_r))
    for dev, go, go_b in downs:
        when(go_b, functools.partial(pass_to, mine, 1, dev, 2, 1))
        n_b = n_b + jnp.where(go_b, one, 0)
    for dev, k, go, k_b, go_b in acrosses:
        n_across = n_across + jnp.where(go, one, 0)
        n_b = n_b + jnp.where(go_b, one, 0)

    def pass_across():
        for dev, k, go, k_b, go_b in acrosses:
            when(go, functools.partial(pass_to, k, 0, dev, 1, 3))
        for dev, k, go, k_b, go_b in acrosses:
            when(go_b, functools.partial(pass_to, k_b, 1, dev, 2, 4))

    def sent_some(n, sem, least, most):
        for count in range(least, most + 1):
            when(n == count, lambda count=count: sent(some(count), sem))

    @pl.when(r == 0)
    def _():
        arrived(gz.at[pl.ds(0, 7)], g_r.at[1])
        gfin[...] = ((gz[0] + gz[1]) + (gz[2] + gz[3])) + ((gz[4] + gz[5]) + (gz[6] + gz[7]))
        loop(0, 15, lambda p: copy(gfin, gfin, g_s.at[2], g_r.at[2], (row_peer(p), c)).start())
        when(z != 0, lambda: arrived(p1, p1_r))
        loop(0, 15, lambda p: copy(p1, p1, p1_s.at[2], p1_r, (row_peer(p), c)).start())

    wait_col(1)

    @pl.when(owner)
    def _():
        arrived(some(31), rs_r)
        zrecv[c] = zpart[mine]
        zsum = lax.fori_loop(1, 32, lambda i, total: total + zrecv[i], zrecv[0])
        zrows[mine] = zsum
        when(c != 0, lambda: arrived(some(7), ag_r.at[2]))
        rows = jnp.concatenate([rowpb[my_h, i, 0:NB, :] for i in range(3)], axis=1)
        total = dot_nt(
            jnp.concatenate([zsum[i] for i in range(3)], axis=1), jnp.concatenate([rows, jnp.zeros_like(rows)], axis=0)
        )
        lane8 = lax.broadcasted_iota(jnp.int32, (8, 128), 1)
        total = total + jnp.where((r == 0) & (my_h == 0) & (lane8 >= NB), zsum[0], 0.0)
        hsend[0] = total
        hrecv[r] = total
        loop(0, 15, lambda p: copy(hsend.at[0], hrecv.at[r], h_s, h_r, (row_peer(p), c)).start())
        there = r + 16 * my_h
        loop(0, 15, lambda p: copy(zrows.at[mine], zcols.at[my_g], zc_s, zc_r, (row_peer(p), there)).start())
        loop(0, 31, lambda p: copy(zrows.at[mine], zrows.at[mine], zr_s, zr_r, (r, col_peer(p))).start())
        @pl.when(c != 0)
        def _():
            arrived(some(2), ag_r.at[0])
            arrived(some(4), ag_r.at[1])

        pass_across()
        arrived(hrecv.at[pl.ds(0, 15)], h_r)
        hall[mine] = lax.fori_loop(1, 16, lambda i, total: total + hrecv[i], hrecv[0])
        loop(0, 31, lambda p: copy(hall.at[mine], hall.at[mine], ha_s, ha_r, (r, col_peer(p))).start())
        @pl.when(c != 0)
        def _():
            arrived(some(6), ag_r.at[3])
            arrived(some(12), ag_r.at[4])

        @pl.when(r != 0)
        def _():
            arrived(gfin, g_r.at[2])
            arrived(p1, p1_r)

        arrived(c0, c0_r.at[0])
        arrived(om, c0_r.at[1])

    @pl.when(plain)
    def _():
        when(r != 0, lambda: arrived(gfin, g_r.at[2]))
        packed = gfin[...]
        gram = jnp.concatenate([packed, pltpu.roll(packed, 64, 1)], axis=0)
        gram = jnp.where(lane < NB, gram, 0.0)
        ct[0:NB, :] = jnp.zeros((NB, 128), F32)
        factor_cholesky(gram, ct)
        c0[...] = jnp.transpose(ct[...])[0:NB, :]
        copy(c0, c0, c0_s.at[0], c0_r.at[0], (r, partner)).start()
        arrived(some(4), ag_r.at[0])
        arrived(some(3), ag_r.at[1])
        pass_across()
        when(r != 0, lambda: arrived(p1, p1_r))
        corner = p1[...]
        product = dot_nn(pltpu.roll(c0[...], 64, 1), jnp.concatenate([corner, jnp.zeros_like(corner)], axis=0))
        om[...] = invert(gram + jnp.where(lane < NB, product, 0.0))
        copy(om, om, c0_s.at[1], c0_r.at[1], (r, partner)).start()
        arrived(some(12), ag_r.at[3])
        arrived(some(12), ag_r.at[4])

    sub = lax.broadcasted_iota(jnp.int32, (NB, 128), 0)
    c0v = c0[...]
    unit = jnp.where(sub == lane, 1.0, 0.0)
    pad = jnp.zeros((NB, 128), F32)
    s_mat = dot_nn(om[...], jnp.concatenate([unit + c0v, pad], axis=0))
    c_cols = jnp.where(c == 0, c0v, 0.0)
    c_rows = jnp.where(r == 0, c0v, 0.0)

    when(owner, lambda: arrived(some(15), zr_r))
    when(plain, lambda: arrived(some(16), zr_r))

    zb = []
    for t in range(6):
        h, i = t % 2, t // 2
        zb.append(
            jnp.concatenate([zrows[8 * h : 8 * h + 8, i].reshape(NB, 128), rowpb[h, i, NB:, :]], axis=0)
        )
        n_t = rowpb[h, i, 0:NB, :]
        if t == 0:
            n_t = n_t + c_rows
        left_o[t, NB:, :] = n_t
    w_rows = dot_nn(s_mat, jnp.concatenate(zb, axis=1))
    for t in range(6):
        left_o[t, 0:NB, :] = w_rows[:, 128 * t : 128 * t + 128]

    @pl.when(home)
    def _():
        zcols[...] = zrows[pl.ds(8 * lax.div(c, 16), 8)]

    when(jnp.logical_not(home), lambda: arrived(zcols, zc_r))

    zb = [
        jnp.concatenate([zcols[:, s].reshape(NB, 128), colpb[pl.ds(192 + s, NB, stride=3), :]], axis=0) for s in range(3)
    ]
    w_cols = dot_nn(s_mat, jnp.concatenate(zb, axis=1))
    n_cols = [panel_cols(colpb, s) for s in range(3)]
    n_cols = jnp.concatenate([n_cols[0] + c_cols] + n_cols[1:], axis=1)
    right_o[0:NB, :] = n_cols

    when(owner, lambda: arrived(hall.at[pl.ds(0, 15)], ha_r))
    when(plain, lambda: arrived(hall, ha_r))

    top = (hall[0:8] + hall[8:16]).reshape(NB, 128)
    turned = jnp.transpose(jnp.concatenate([top, pad], axis=0))
    bottom = jnp.where(lane < NB, turned[NB:, :], p1[...])
    x_mat = dot_nt(dot_nn(s_mat, jnp.concatenate([top, bottom], axis=0)), jnp.concatenate([s_mat, pad], axis=0))
    right_o[NB:, :] = w_cols - dot_nn(x_mat, jnp.concatenate([n_cols, jnp.zeros_like(n_cols)], axis=0))

    @pl.when(r == 0)
    def _():
        for part in range(2):
            sent(a_v.at[pl.ds(0, 1536)], colp_s.at[part])
        sent(gx.at[pl.ds(0, 3)], g_s.at[0])
        sent(gz.at[pl.ds(0, 7)], g_s.at[1])
        sent(a_v.at[pl.ds(0, 15 * 32)], g_s.at[2])
        when(c == 0, lambda: sent(a_v.at[pl.ds(0, 3 * NB)], p1_s.at[0]))
        when(z == 0, lambda: sent(a_v.at[pl.ds(0, 7 * NB)], p1_s.at[1]))
        sent(a_v.at[pl.ds(0, 15 * NB)], p1_s.at[2])

    @pl.when((r != 0) & (core == 0))
    def _():
        for part in range(2):
            sent(colpb.at[pl.ds(0, 192)], fwd_s.at[part])

    @pl.when(c == 0)
    def _():
        sent(some(31), sc_s)

    when(owner, lambda: sent_some(n_first, ag_s.at[0], 10, 14))
    sent_some(n_across, ag_s.at[1], 4, 12)
    sent_some(n_b, ag_s.at[2], 8, 19)

    @pl.when(owner)
    def _():
        sent(some(15), rs_s)
        sent(some(15), zc_s)
        sent(some(31), zr_s)
        sent(a_v.at[pl.ds(0, 15 * 8)], h_s)
        sent(a_v.at[pl.ds(0, 31 * 8)], ha_s)

    @pl.when(plain)
    def _():
        sent(some(16), rs_s)
        sent(c0, c0_s.at[0])
        sent(om, c0_s.at[1])


def update(a, left, right, out):
    high, low = split(right[...])
    columns = jnp.concatenate([high, low, high], axis=0)
    for t in range(6):
        high, low = split(jnp.transpose(left[t]))
        change = jnp.dot(jnp.concatenate([high, high, low], axis=1), columns, preferred_element_type=F32)
        for s in range(3):
            rows = pl.ds(t * 384 + s, 128, stride=3)
            out[rows, :] = a[rows, :] - change[:, 128 * s : 128 * s + 128]


def vmem(*shape):
    return pltpu.VMEM(shape, F32)


def dma(*shape):
    return pltpu.SemaphoreType.DMA(shape)


def body(hessian):
    flat = hessian.reshape(2304, 128)
    whole = pl.BlockSpec(memory_space=pltpu.VMEM)
    left, right = pl.pallas_call(
        kernel,
        out_shape=[jax.ShapeDtypeStruct((6, 128, 128), F32), jax.ShapeDtypeStruct((128, 384), F32)],
        in_specs=[pl.BlockSpec(memory_space=pltpu.HBM)],
        out_specs=[whole, whole],
        scratch_shapes=[
            vmem(2304, 128), vmem(384, 128), vmem(2, 3, 128, 128), vmem(16, 3, 8, 128), vmem(32, 3, 8, 128),
            vmem(16, 3, 8, 128), vmem(8, 3, 8, 128), vmem(4, 32, 128), vmem(8, 32, 128), vmem(32, 128),
            vmem(64, 128), vmem(1, 8, 128), vmem(16, 8, 128), vmem(16, 8, 128), vmem(128, 128), vmem(64, 128), vmem(64, 128),
            dma(), dma(2), dma(2), dma(2), dma(), dma(), dma(3), dma(5), dma(), dma(), dma(), dma(), dma(), dma(),
            dma(3), dma(3), dma(3), dma(), dma(), dma(), dma(), dma(), dma(2), dma(2),
        ],
        compiler_params=pltpu.CompilerParams(collective_id=0, has_side_effects=True, vmem_limit_bytes=54208 << 10),
        name="panel",
    )(flat)
    out = pl.pallas_call(
        update,
        out_shape=jax.ShapeDtypeStruct((2304, 128), F32),
        in_specs=[whole, whole, whole],
        out_specs=whole,
        compiler_params=pltpu.CompilerParams(vmem_limit_bytes=16 << 20),
        name="update",
    )(flat, left, right)
    return out.reshape(hessian.shape)


def solution(mesh):
    return jax.shard_map(
        body,
        mesh=mesh,
        in_specs=(P(None, "row", None, None, "col", None),),
        out_specs=P(None, "row", None, None, "col", None),
        check_vma=False,
    )
```

```python
import functools

import jax
import jax.numpy as jnp
from jax import lax
from jax.experimental import pallas as pl
from jax.experimental.pallas import tpu as pltpu
from jax.sharding import PartitionSpec as P

NB = 64
MESH = pl.DeviceIdType.MESH
HIGHEST = lax.Precision.HIGHEST
F32 = jnp.float32


def dot_nn(a, b):
    return lax.dot_general(a, b, (((1,), (0,)), ((), ())), precision=HIGHEST, preferred_element_type=F32)


def dot_nt(a, b):
    return lax.dot_general(a, b, (((1,), (1,)), ((), ())), precision=HIGHEST, preferred_element_type=F32)


def split(a):
    high = a.astype(jnp.bfloat16)
    return high, (a - high.astype(F32)).astype(jnp.bfloat16)


def dot3(a, b, dims):
    (ah, al), (bh, bl) = split(a), split(b)
    left = jnp.concatenate([ah, ah, al], axis=dims[0])
    right = jnp.concatenate([bh, bl, bh], axis=dims[1])
    return lax.dot_general(left, right, (((dims[0],), (dims[1],)), ((), ())), preferred_element_type=F32)


def split(a):
    high = a.astype(jnp.bfloat16)
    return high, (a - high.astype(F32)).astype(jnp.bfloat16)


def dot3(a, b, dims):
    (ah, al), (bh, bl) = split(a), split(b)
    left = jnp.concatenate([ah, ah, al], axis=dims[0])
    right = jnp.concatenate([bh, bl, bh], axis=dims[1])
    return lax.dot_general(left, right, (((dims[0],), (dims[1],)), ((), ())), preferred_element_type=F32)


def split(a):
    high = a.astype(jnp.bfloat16)
    return high, (a - high.astype(F32)).astype(jnp.bfloat16)


def dot3(a, b, dims):
    (ah, al), (bh, bl) = split(a), split(b)
    left = jnp.concatenate([ah, ah, al], axis=dims[0])
    right = jnp.concatenate([bh, bl, bh], axis=dims[1])
    return lax.dot_general(left, right, (((dims[0],), (dims[1],)), ((), ())), preferred_element_type=F32)


def spiral(q, n):
    return lax.rem(n // 2 + (1 - 2 * lax.rem(q, 2)) * lax.div(q + 1, 2), n)


def loop(lo, hi, f):
    def step(i, carry):
        f(i)
        return carry

    lax.fori_loop(lo, hi, step, 0)


def factor_cholesky(g, ct, start, stop):
    lane1 = lax.broadcasted_iota(jnp.int32, (1, 128), 1)
    for k in range(start, stop):
        col = g[:, k : k + 1]
        row = g[k : k + 1, :]
        piv = g[k : k + 1, k : k + 1]
        ct[NB + k : NB + k + 1, :] = jnp.where((lane1 >= k) & (lane1 < NB), row * lax.rsqrt(piv), 0.0)
        if k < NB - 1:
            low = (k + 1) // 8 * 8
            part = g[low:, :] - col[low:, :] * (row / piv)
            g = part if low == 0 else jnp.concatenate([g[:low, :], part], axis=0)
    return g


def invert(m):
    lane1 = lax.broadcasted_iota(jnp.int32, (1, 128), 1)
    lane = lax.broadcasted_iota(jnp.int32, (NB, 128), 1)
    sub = lax.broadcasted_iota(jnp.int32, (NB, 128), 0)
    for k in range(NB):
        col = m[:, k : k + 1]
        row = m[k : k + 1, :]
        piv = m[k : k + 1, k : k + 1]
        scaled = jnp.where(lane1 == k, 1.0, row) / piv
        m = jnp.where(sub == k, scaled, jnp.where(lane == k, 0.0, m) - col * scaled)
    return m


def kernel(
    a_hbm, left_o, right_o, a_v, colpb, rowpb, zpart, zrecv, zrows, zcols, gx, gz, gfin, p1, hsend, hrecv, hall, ct, c0, om,
    load_s, colp_s, colp_r, fwd_s, sc_s, sc_r, ag_s, ag_r, rs_s, rs_r, zr_s, zr_r, zc_s, zc_r,
    g_s, g_r, p1_s, p1_r, h_s, h_r, ha_s, ha_r, c0_s, c0_r,
):
    r, c = lax.axis_index("row"), lax.axis_index("col")
    y, core = lax.div(r, 2), lax.rem(r, 2)
    z, x = lax.div(c, 4), lax.rem(c, 4)
    mine = lax.div(c, 2)
    owner = lax.rem(x + z, 2) == 0
    plain = jnp.logical_not(owner)
    my_g, my_h = lax.rem(mine, 8), lax.div(mine, 8)
    partner = c + 1 - 2 * lax.rem(c, 2)
    home = lax.rem(c, 16) == r
    lane = lax.broadcasted_iota(jnp.int32, (NB, 128), 1)

    def panel_owner(k):
        return 2 * k + lax.rem(lax.div(k, 2), 2)

    def other_owner(k):
        return 2 * k + 1 - lax.rem(lax.div(k, 2), 2)

    def col_peer(p):
        return lax.rem(z + spiral(lax.div(p, 4), 8), 8) * 4 + lax.rem(x + spiral(lax.rem(p, 4), 4), 4)

    def x_peer(p):
        return z * 4 + lax.rem(x + spiral(p, 4), 4)

    def z_peer(p):
        return lax.rem(z + spiral(p, 8), 8) * 4 + x

    def row_peer(p):
        return lax.rem(y + spiral(lax.div(p, 2), 8), 8) * 2 + lax.rem(core + 1 - lax.rem(p, 2), 2)

    def copy(src, dst, ssem, rsem, dev):
        return pltpu.make_async_remote_copy(
            src_ref=src, dst_ref=dst, send_sem=ssem, recv_sem=rsem, device_id=dev, device_id_type=MESH
        )

    def sent(ref, sem):
        copy(ref, ref, sem, sem, (r, partner)).wait_send()

    def arrived(ref, sem):
        copy(ref, ref, sem, sem, (r, partner)).wait_recv()

    def when(condition, f):
        pl.when(condition)(f)

    def chunk(k, part):
        rows = pl.multiple_of(lax.rem(k, 8) * 8 + part * NB, 8)
        return rowpb.at[lax.div(k, 8), :, pl.ds(rows, 8), :]

    def some(n):
        return zrecv.at[pl.ds(0, n)]

    load = pltpu.make_async_copy(a_hbm, a_v, load_s)
    load.start()
    barrier = pltpu.get_barrier_semaphore()

    def greet(dev):
        pl.semaphore_signal(barrier, inc=1, device_id=dev, device_id_type=MESH)

    loop(0, 15, lambda p: greet((row_peer(p), c)))

    @pl.when(jnp.logical_not(home))
    def _():
        loop(0, 8, lambda g: greet((lax.rem(c, 16), panel_owner(g + 8 * lax.div(c, 16)))))

    loop(0, 31, lambda p: greet((r, col_peer(p))))

    load.wait()

    def panel_cols(ref, s):
        return jnp.where((c == 0) & (s == 0) & (lane < NB), 0.0, ref[pl.ds(s, NB, stride=3), :])

    @pl.when(c == 0)
    def _():
        full = lax.broadcasted_iota(jnp.int32, (128, 128), 0)
        full_lane = lax.broadcasted_iota(jnp.int32, (128, 128), 1)
        for t in range(6):
            block = jnp.transpose(a_v[pl.ds(t * 384, 128, stride=3), :])
            if t == 0:
                block = jnp.where((r == 0) & (full < NB) & (full_lane < NB), 0.0, block)
            rowpb[t % 2, t // 2] = block

    @pl.when(r == 0)
    def _():
        panel = jnp.concatenate([panel_cols(a_v, s) for s in range(3)], axis=1)
        zero = jnp.zeros_like(panel)
        gx[x] = dot_nt(panel[:32], jnp.concatenate([panel, zero], axis=0)) + dot_nt(
            panel[32:], jnp.concatenate([zero, panel], axis=0)
        )

        @pl.when(c == 0)
        def _():
            p1[...] = a_v[pl.ds(3 * NB, NB, stride=3), :]

        colpb[...] = a_v[0:384, :]

    when(owner, lambda: pl.semaphore_wait(barrier, 61))
    when(plain, lambda: pl.semaphore_wait(barrier, 46))

    parts = ((0, 96), (96, 96), (192, 192))

    def send_col(part):
        rows = pl.ds(*parts[part])

        def to(q):
            other = 2 * spiral(q, 8) + jnp.where(q == 7, 1, 0)
            copy(a_v.at[rows], colpb.at[rows], colp_s.at[part], colp_r.at[part], (other, c)).start()

        loop(0, 8, to)

    def wait_col(part):
        rows = pl.ds(*parts[part])

        @pl.when(r != 0)
        def _():
            arrived(colpb.at[rows], colp_r.at[part])

            @pl.when(core == 0)
            def _():
                copy(colpb.at[rows], colpb.at[rows], fwd_s.at[part], colp_r.at[part], (r + 1, c)).start()

    def scatter(part):
        def to(k):
            dev = panel_owner(k) if part == 0 else other_owner(k)
            copy(chunk(k, part), chunk(k, part), sc_s, sc_r, (r, dev)).start()

        loop(1 - part, 16, to)

    when(c == 0, lambda: scatter(0))

    @pl.when(r == 0)
    def _():
        send_col(0)
        send_col(1)
        loop(0, 3, lambda p: copy(gx.at[x], gx.at[x], g_s.at[0], g_r.at[0], (r, x_peer(p))).start())

        @pl.when(c == 0)
        def _():
            loop(0, 3, lambda p: copy(p1, p1, p1_s.at[0], p1_r, (r, x_peer(p))).start())

    when(c == 0, lambda: scatter(1))
    when(r == 0, lambda: send_col(2))

    wait_col(0)
    wait_col(1)

    panel = jnp.concatenate([panel_cols(colpb, s) for s in range(3)], axis=1)
    for t in range(6):
        tile = jnp.concatenate([a_v[pl.ds(t * 384 + s, 128, stride=3), :] for s in range(3)], axis=1)
        zt = dot3(panel, tile, (1, 1))
        for g in range(8):
            zpart[g + 8 * (t % 2), t // 2] = zt[8 * g : 8 * g + 8, :]

    @pl.when(r == 0)
    def _():
        arrived(gx.at[pl.ds(0, 3)], g_r.at[0])
        gz[z] = (gx[0] + gx[1]) + (gx[2] + gx[3])
        loop(0, 7, lambda p: copy(gz.at[z], gz.at[z], g_s.at[1], g_r.at[1], (r, z_peer(p))).start())

        @pl.when(z == 0)
        def _():
            when(x != 0, lambda: arrived(p1, p1_r))
            loop(0, 7, lambda p: copy(p1, p1, p1_s.at[1], p1_r, (r, z_peer(p))).start())

    def reduce_to(p):
        k = lax.rem(z + spiral(lax.div(p, 2), 8), 8) * 2 + lax.rem(p, 2)
        dev = panel_owner(k)

        @pl.when(dev != c)
        def _():
            copy(zpart.at[k], zrecv.at[c], rs_s, rs_r, (r, dev)).start()

    loop(0, 16, reduce_to)

    def pass_to(k, part, dev, ssem, sem):
        copy(chunk(k, part), chunk(k, part), ag_s.at[ssem], ag_r.at[sem], (r, dev)).start()

    one = jnp.int32(1)
    n_first, n_across, n_b = jnp.int32(0), jnp.int32(0), jnp.int32(0)

    firsts = []
    for p in range(7):
        dev = panel_owner(8 * my_h + lax.rem(my_g + 4 + p + (1 if p > 3 else 0), 8))
        firsts.append((dev, owner & (dev != 0)))
    downs = []
    for p in range(7):
        dev = z_peer(p)
        dev_z = lax.div(dev, 4)
        first = (lax.rem(dev_z + x, 2) == 0) & (lax.div(dev_z, 4) == my_h)
        downs.append((dev, owner & (dev != 0) & jnp.logical_not(first), plain & (dev != 0)))
    acrosses = []
    for p in range(3):
        dev = x_peer(p)
        dev_owner = lax.rem(lax.rem(dev, 4) + z, 2) == 0
        for i in range(4):
            k = 4 * i + 2 * lax.rem(x, 2) + lax.div(x, 2)
            skip = dev_owner & (lax.div(z, 4) == i // 2)
            k_b = 4 * i + 2 * lax.rem(x + 1, 2) + lax.div(x, 2)
            acrosses.append((dev, k, (dev != 0) & jnp.logical_not(skip), k_b, dev != 0))

    @pl.when(owner)
    def _():
        when(c != 0, lambda: arrived(chunk(mine, 0), sc_r))

    for dev, go in firsts:
        when(go, functools.partial(pass_to, mine, 0, dev, 0, 2))
        n_first = n_first + jnp.where(go, one, 0)
    for dev, go, go_b in downs:
        when(go, functools.partial(pass_to, mine, 0, dev, 0, 0))
        n_first = n_first + jnp.where(go, one, 0)

    when(plain, lambda: arrived(chunk(mine, 1), sc_r))
    for dev, go, go_b in downs:
        when(go_b, functools.partial(pass_to, mine, 1, dev, 2, 1))
        n_b = n_b + jnp.where(go_b, one, 0)
    for dev, k, go, k_b, go_b in acrosses:
        n_across = n_across + jnp.where(go, one, 0)
        n_b = n_b + jnp.where(go_b, one, 0)

    def pass_across():
        for dev, k, go, k_b, go_b in acrosses:
            when(go, functools.partial(pass_to, k, 0, dev, 1, 3))
        for dev, k, go, k_b, go_b in acrosses:
            when(go_b, functools.partial(pass_to, k_b, 1, dev, 2, 4))

    def z_across():
        def to(p):
            k = 4 * lax.rem(p, 4) + 2 * lax.rem(x, 2) + lax.div(x, 2)
            copy(zrows.at[k], zrows.at[k], zr_s.at[1], zr_r.at[1], (r, x_peer(lax.div(p, 4)))).start()

        loop(0, 12, to)

    def sent_some(n, sem, least, most):
        for count in range(least, most + 1):
            when(n == count, lambda count=count: sent(some(count), sem))

    @pl.when(r == 0)
    def _():
        arrived(gz.at[pl.ds(0, 7)], g_r.at[1])
        gfin[...] = ((gz[0] + gz[1]) + (gz[2] + gz[3])) + ((gz[4] + gz[5]) + (gz[6] + gz[7]))
        loop(0, 15, lambda p: copy(gfin, gfin, g_s.at[2], g_r.at[2], (row_peer(p), c)).start())
        when(z != 0, lambda: arrived(p1, p1_r))
        loop(0, 15, lambda p: copy(p1, p1, p1_s.at[2], p1_r, (row_peer(p), c)).start())

    wait_col(2)

    @pl.when(owner)
    def _():
        arrived(some(31), rs_r)
        zrecv[c] = zpart[mine]
        zsum = lax.fori_loop(1, 32, lambda i, total: total + zrecv[i], zrecv[0])
        zrows[mine] = zsum
        when(c != 0, lambda: arrived(some(7), ag_r.at[2]))
        rows = jnp.concatenate([rowpb[my_h, i, 0:NB, :] for i in range(3)], axis=1)
        total = dot_nt(
            jnp.concatenate([zsum[i] for i in range(3)], axis=1), jnp.concatenate([rows, jnp.zeros_like(rows)], axis=0)
        )
        lane8 = lax.broadcasted_iota(jnp.int32, (8, 128), 1)
        total = total + jnp.where((r == 0) & (my_h == 0) & (lane8 >= NB), zsum[0], 0.0)
        hsend[0] = total
        hrecv[r] = total
        loop(0, 15, lambda p: copy(hsend.at[0], hrecv.at[r], h_s, h_r, (row_peer(p), c)).start())
        there = r + 16 * my_h
        loop(0, 15, lambda p: copy(zrows.at[mine], zcols.at[my_g], zc_s, zc_r, (row_peer(p), there)).start())
        loop(0, 7, lambda p: copy(zrows.at[mine], zrows.at[mine], zr_s.at[0], zr_r.at[0], (r, z_peer(p))).start())
        @pl.when(c != 0)
        def _():
            arrived(some(2), ag_r.at[0])
            arrived(some(4), ag_r.at[1])

        pass_across()
        arrived(hrecv.at[pl.ds(0, 15)], h_r)
        hall[mine] = lax.fori_loop(1, 16, lambda i, total: total + hrecv[i], hrecv[0])
        loop(0, 31, lambda p: copy(hall.at[mine], hall.at[mine], ha_s, ha_r, (r, col_peer(p))).start())
        arrived(some(3), zr_r.at[0])
        z_across()
        @pl.when(c != 0)
        def _():
            arrived(some(6), ag_r.at[3])
            arrived(some(12), ag_r.at[4])

        @pl.when(r != 0)
        def _():
            arrived(gfin, g_r.at[2])
            arrived(p1, p1_r)

        arrived(c0, c0_r.at[0])
        arrived(om, c0_r.at[1])

    @pl.when(plain)
    def _():
        when(r != 0, lambda: arrived(gfin, g_r.at[2]))
        packed = gfin[...]
        gram = jnp.concatenate([packed, pltpu.roll(packed, 64, 1)], axis=0)
        gram = jnp.where(lane < NB, gram, 0.0)
        ct[0:NB, :] = jnp.zeros((NB, 128), F32)
        rest = factor_cholesky(gram, ct, 0, 40)
        arrived(some(4), ag_r.at[0])
        arrived(some(3), ag_r.at[1])
        pass_across()
        factor_cholesky(rest, ct, 40, NB)
        c0[...] = jnp.transpose(ct[...])[0:NB, :]
        copy(c0, c0, c0_s.at[0], c0_r.at[0], (r, partner)).start()
        when(r != 0, lambda: arrived(p1, p1_r))
        corner = p1[...]
        product = dot_nn(pltpu.roll(c0[...], 64, 1), jnp.concatenate([corner, jnp.zeros_like(corner)], axis=0))
        om[...] = invert(gram + jnp.where(lane < NB, product, 0.0))
        copy(om, om, c0_s.at[1], c0_r.at[1], (r, partner)).start()
        arrived(some(4), zr_r.at[0])
        z_across()
        arrived(some(12), ag_r.at[3])
        arrived(some(12), ag_r.at[4])

    sub = lax.broadcasted_iota(jnp.int32, (NB, 128), 0)
    c0v = c0[...]
    unit = jnp.where(sub == lane, 1.0, 0.0)
    pad = jnp.zeros((NB, 128), F32)
    s_mat = dot_nn(om[...], jnp.concatenate([unit + c0v, pad], axis=0))
    c_cols = jnp.where(c == 0, c0v, 0.0)
    c_rows = jnp.where(r == 0, c0v, 0.0)

    arrived(some(12), zr_r.at[1])

    zb = []
    for t in range(6):
        h, i = t % 2, t // 2
        zb.append(
            jnp.concatenate([zrows[8 * h : 8 * h + 8, i].reshape(NB, 128), rowpb[h, i, NB:, :]], axis=0)
        )
        n_t = rowpb[h, i, 0:NB, :]
        if t == 0:
            n_t = n_t + c_rows
        left_o[t, NB:, :] = n_t
    w_rows = dot3(s_mat, jnp.concatenate(zb, axis=1), (1, 0))
    for t in range(6):
        left_o[t, 0:NB, :] = w_rows[:, 128 * t : 128 * t + 128]

    @pl.when(home)
    def _():
        zcols[...] = zrows[pl.ds(8 * lax.div(c, 16), 8)]

    when(jnp.logical_not(home), lambda: arrived(zcols, zc_r))

    zb = [
        jnp.concatenate([zcols[:, s].reshape(NB, 128), colpb[pl.ds(192 + s, NB, stride=3), :]], axis=0) for s in range(3)
    ]
    w_cols = dot3(s_mat, jnp.concatenate(zb, axis=1), (1, 0))
    n_cols = [panel_cols(colpb, s) for s in range(3)]
    n_cols = jnp.concatenate([n_cols[0] + c_cols] + n_cols[1:], axis=1)
    right_o[0:NB, :] = n_cols
    s_turned = jnp.transpose(jnp.concatenate([s_mat, pad], axis=0))
    sn_cols = dot3(s_turned[:, 0:NB], n_cols, (1, 0))

    when(owner, lambda: arrived(hall.at[pl.ds(0, 15)], ha_r))
    when(plain, lambda: arrived(hall, ha_r))

    top = (hall[0:8] + hall[8:16]).reshape(NB, 128)
    turned = jnp.transpose(jnp.concatenate([top, pad], axis=0))
    bottom = jnp.where(lane < NB, turned[NB:, :], p1[...])
    inner = dot3(jnp.concatenate([top, bottom], axis=0), sn_cols, (1, 0))
    right_o[NB:, :] = w_cols - dot3(s_mat, inner, (1, 0))

    @pl.when(r == 0)
    def _():
        for part in range(3):
            sent(a_v.at[pl.ds(0, 8 * parts[part][1])], colp_s.at[part])
        sent(gx.at[pl.ds(0, 3)], g_s.at[0])
        sent(gz.at[pl.ds(0, 7)], g_s.at[1])
        sent(a_v.at[pl.ds(0, 15 * 32)], g_s.at[2])
        when(c == 0, lambda: sent(a_v.at[pl.ds(0, 3 * NB)], p1_s.at[0]))
        when(z == 0, lambda: sent(a_v.at[pl.ds(0, 7 * NB)], p1_s.at[1]))
        sent(a_v.at[pl.ds(0, 15 * NB)], p1_s.at[2])

    @pl.when((r != 0) & (core == 0))
    def _():
        for part in range(3):
            sent(colpb.at[pl.ds(*parts[part])], fwd_s.at[part])

    @pl.when(c == 0)
    def _():
        sent(some(31), sc_s)

    when(owner, lambda: sent_some(n_first, ag_s.at[0], 10, 14))
    sent_some(n_across, ag_s.at[1], 4, 12)
    sent(some(12), zr_s.at[1])
    sent_some(n_b, ag_s.at[2], 8, 19)

    @pl.when(owner)
    def _():
        sent(some(15), rs_s)
        sent(some(15), zc_s)
        sent(some(7), zr_s.at[0])
        sent(a_v.at[pl.ds(0, 15 * 8)], h_s)
        sent(a_v.at[pl.ds(0, 31 * 8)], ha_s)

    @pl.when(plain)
    def _():
        sent(some(16), rs_s)
        sent(c0, c0_s.at[0])
        sent(om, c0_s.at[1])


def update(a, left, right, out, tiles, sems):
    high, low = split(right[...])
    columns = jnp.concatenate([high, low, high], axis=0)
    for t in range(6):
        high, low = split(jnp.transpose(left[t]))
        change = jnp.dot(jnp.concatenate([high, high, low], axis=1), columns, preferred_element_type=F32)
        for s in range(3):
            rows = pl.ds(t * 384 + s, 128, stride=3)
            tiles[rows, :] = a[rows, :] - change[:, 128 * s : 128 * s + 128]
        rows = pl.ds(t * 384, 384)
        pltpu.make_async_copy(tiles.at[rows], out.at[rows], sems.at[t]).start()
    for t in range(6):
        rows = pl.ds(t * 384, 384)
        pltpu.make_async_copy(tiles.at[rows], out.at[rows], sems.at[t]).wait()


def vmem(*shape):
    return pltpu.VMEM(shape, F32)


def dma(*shape):
    return pltpu.SemaphoreType.DMA(shape)


def body(hessian):
    flat = hessian.reshape(2304, 128)
    whole = pl.BlockSpec(memory_space=pltpu.VMEM)
    left, right = pl.pallas_call(
        kernel,
        out_shape=[jax.ShapeDtypeStruct((6, 128, 128), F32), jax.ShapeDtypeStruct((128, 384), F32)],
        in_specs=[pl.BlockSpec(memory_space=pltpu.HBM)],
        out_specs=[whole, whole],
        scratch_shapes=[
            vmem(2304, 128), vmem(384, 128), vmem(2, 3, 128, 128), vmem(16, 3, 8, 128), vmem(32, 3, 8, 128),
            vmem(16, 3, 8, 128), vmem(8, 3, 8, 128), vmem(4, 32, 128), vmem(8, 32, 128), vmem(32, 128),
            vmem(64, 128), vmem(1, 8, 128), vmem(16, 8, 128), vmem(16, 8, 128), vmem(128, 128), vmem(64, 128), vmem(64, 128),
            dma(), dma(3), dma(3), dma(3), dma(), dma(), dma(3), dma(5), dma(), dma(), dma(2), dma(2), dma(), dma(),
            dma(3), dma(3), dma(3), dma(), dma(), dma(), dma(), dma(), dma(2), dma(2),
        ],
        compiler_params=pltpu.CompilerParams(collective_id=0, has_side_effects=True, vmem_limit_bytes=54208 << 10),
        name="panel",
    )(flat)
    out = pl.pallas_call(
        update,
        out_shape=jax.ShapeDtypeStruct((2304, 128), F32),
        in_specs=[whole, whole, whole],
        out_specs=pl.BlockSpec(memory_space=pltpu.HBM),
        scratch_shapes=[vmem(2304, 128), dma(6)],
        compiler_params=pltpu.CompilerParams(vmem_limit_bytes=16 << 20),
        name="update",
    )(flat, left, right)
    return out.reshape(hessian.shape)


def solution(mesh):
    return jax.shard_map(
        body,
        mesh=mesh,
        in_specs=(P(None, "row", None, None, "col", None),),
        out_specs=P(None, "row", None, None, "col", None),
        check_vma=False,
    )
```

```python
import functools

import jax
import jax.numpy as jnp
from jax import lax
from jax.experimental import pallas as pl
from jax.experimental.pallas import tpu as pltpu
from jax.sharding import PartitionSpec as P

NB = 64
MESH = pl.DeviceIdType.MESH
HIGHEST = lax.Precision.HIGHEST
F32 = jnp.float32


def dot_nn(a, b):
    return lax.dot_general(a, b, (((1,), (0,)), ((), ())), precision=HIGHEST, preferred_element_type=F32)


def dot_nt(a, b):
    return lax.dot_general(a, b, (((1,), (1,)), ((), ())), precision=HIGHEST, preferred_element_type=F32)


def split(a):
    high = a.astype(jnp.bfloat16)
    return high, (a - high.astype(F32)).astype(jnp.bfloat16)


def dot3(a, b, dims):
    (ah, al), (bh, bl) = split(a), split(b)
    left = jnp.concatenate([ah, ah, al], axis=dims[0])
    right = jnp.concatenate([bh, bl, bh], axis=dims[1])
    return lax.dot_general(left, right, (((dims[0],), (dims[1],)), ((), ())), preferred_element_type=F32)


def split(a):
    high = a.astype(jnp.bfloat16)
    return high, (a - high.astype(F32)).astype(jnp.bfloat16)


def dot3(a, b, dims):
    (ah, al), (bh, bl) = split(a), split(b)
    left = jnp.concatenate([ah, ah, al], axis=dims[0])
    right = jnp.concatenate([bh, bl, bh], axis=dims[1])
    return lax.dot_general(left, right, (((dims[0],), (dims[1],)), ((), ())), preferred_element_type=F32)


def split(a):
    high = a.astype(jnp.bfloat16)
    return high, (a - high.astype(F32)).astype(jnp.bfloat16)


def dot3(a, b, dims):
    (ah, al), (bh, bl) = split(a), split(b)
    left = jnp.concatenate([ah, ah, al], axis=dims[0])
    right = jnp.concatenate([bh, bl, bh], axis=dims[1])
    return lax.dot_general(left, right, (((dims[0],), (dims[1],)), ((), ())), preferred_element_type=F32)


def spiral(q, n):
    return lax.rem(n // 2 + (1 - 2 * lax.rem(q, 2)) * lax.div(q + 1, 2), n)


def loop(lo, hi, f):
    def step(i, carry):
        f(i)
        return carry

    lax.fori_loop(lo, hi, step, 0)


def factor_cholesky(g, ct):
    lane1 = lax.broadcasted_iota(jnp.int32, (1, 128), 1)
    for first in range(0, NB, 8):
        rest = g[first:, :]
        cols = [jnp.broadcast_to(rest[:, first + j : first + j + 1], rest.shape) for j in range(8)]
        rows = [rest[j : j + 1, :] for j in range(8)]
        for j in range(8):
            k = first + j
            pivot = cols[j][j : j + 1, :]
            inverse = 1.0 / pivot
            scaled = rows[j] * inverse
            ct[NB + k : NB + k + 1, :] = jnp.where((lane1 >= k) & (lane1 < NB), rows[j] * lax.rsqrt(pivot), 0.0)
            for i in range(j + 1, 8):
                factor = cols[i][j : j + 1, :] * inverse
                rows[i] = rows[i] - cols[j][i : i + 1, :] * scaled
                cols[i] = cols[i] - cols[j] * factor
            rest = rest - cols[j] * scaled
        g = rest if first == 0 else jnp.concatenate([g[:first, :], rest], axis=0)


def invert(m):
    lane1 = lax.broadcasted_iota(jnp.int32, (1, 128), 1)
    lane = lax.broadcasted_iota(jnp.int32, (NB, 128), 1)
    sub = lax.broadcasted_iota(jnp.int32, (NB, 128), 0)
    for first in range(0, NB, 8):
        cols = [jnp.broadcast_to(m[:, first + j : first + j + 1], (NB, 128)) for j in range(8)]
        rows = [m[first + j : first + j + 1, :] for j in range(8)]
        for j in range(8):
            k = first + j
            inverse = 1.0 / cols[j][k : k + 1, :]
            scaled = jnp.where(lane1 == k, 1.0, rows[j]) * inverse
            for i in range(j + 1, 8):
                factor = cols[i][k : k + 1, :] * inverse
                rows[i] = jnp.where(lane1 == k, 0.0, rows[i]) - cols[j][first + i : first + i + 1, :] * scaled
                cols[i] = jnp.where(sub == k, factor, cols[i] - cols[j] * factor)
            m = jnp.where(sub == k, scaled, jnp.where(lane == k, 0.0, m) - cols[j] * scaled)
    return m


def kernel(
    a_hbm, left_o, right_o, a_v, colpb, rowpb, zpart, zrecv, zrows, zcols, gx, gz, gfin, p1, hsend, hrecv, hall, ct, c0, om,
    load_s, colp_s, colp_r, fwd_s, sc_s, sc_r, ag_s, ag_r, rs_s, rs_r, zr_s, zr_r, zc_s, zc_r,
    g_s, g_r, p1_s, p1_r, h_s, h_r, ha_s, ha_r, c0_s, c0_r,
):
    r, c = lax.axis_index("row"), lax.axis_index("col")
    y, core = lax.div(r, 2), lax.rem(r, 2)
    z, x = lax.div(c, 4), lax.rem(c, 4)
    mine = lax.div(c, 2)
    owner = lax.rem(x + z, 2) == 0
    plain = jnp.logical_not(owner)
    my_g, my_h = lax.rem(mine, 8), lax.div(mine, 8)
    partner = c + 1 - 2 * lax.rem(c, 2)
    home = lax.rem(c, 16) == r
    lane = lax.broadcasted_iota(jnp.int32, (NB, 128), 1)

    def panel_owner(k):
        return 2 * k + lax.rem(lax.div(k, 2), 2)

    def other_owner(k):
        return 2 * k + 1 - lax.rem(lax.div(k, 2), 2)

    def col_peer(p):
        return lax.rem(z + spiral(lax.div(p, 4), 8), 8) * 4 + lax.rem(x + spiral(lax.rem(p, 4), 4), 4)

    def early_peer(p):
        place = z * 4 + x
        return p + jnp.where(p >= place, 1, 0)

    def x_peer(p):
        return z * 4 + lax.rem(x + spiral(p, 4), 4)

    def z_peer(p):
        return lax.rem(z + spiral(p, 8), 8) * 4 + x

    def row_peer(p):
        return lax.rem(y + spiral(lax.div(p, 2), 8), 8) * 2 + lax.rem(core + 1 - lax.rem(p, 2), 2)

    def copy(src, dst, ssem, rsem, dev):
        return pltpu.make_async_remote_copy(
            src_ref=src, dst_ref=dst, send_sem=ssem, recv_sem=rsem, device_id=dev, device_id_type=MESH
        )

    def sent(ref, sem):
        copy(ref, ref, sem, sem, (r, partner)).wait_send()

    def arrived(ref, sem):
        copy(ref, ref, sem, sem, (r, partner)).wait_recv()

    def when(condition, f):
        pl.when(condition)(f)

    def chunk(k, part):
        rows = pl.multiple_of(lax.rem(k, 8) * 8 + part * NB, 8)
        return rowpb.at[lax.div(k, 8), :, pl.ds(rows, 8), :]

    def some(n):
        return zrecv.at[pl.ds(0, n)]

    load = pltpu.make_async_copy(a_hbm, a_v, load_s)
    load.start()
    barrier = pltpu.get_barrier_semaphore()

    def greet(dev):
        pl.semaphore_signal(barrier, inc=1, device_id=dev, device_id_type=MESH)

    loop(0, 15, lambda p: greet((row_peer(p), c)))

    @pl.when(jnp.logical_not(home))
    def _():
        loop(0, 8, lambda g: greet((lax.rem(c, 16), panel_owner(g + 8 * lax.div(c, 16)))))

    loop(0, 31, lambda p: greet((r, col_peer(p))))

    load.wait()

    def panel_cols(ref, s):
        return jnp.where((c == 0) & (s == 0) & (lane < NB), 0.0, ref[pl.ds(s, NB, stride=3), :])

    @pl.when(c == 0)
    def _():
        full = lax.broadcasted_iota(jnp.int32, (128, 128), 0)
        full_lane = lax.broadcasted_iota(jnp.int32, (128, 128), 1)
        for t in range(6):
            block = jnp.transpose(a_v[pl.ds(t * 384, 128, stride=3), :])
            if t == 0:
                block = jnp.where((r == 0) & (full < NB) & (full_lane < NB), 0.0, block)
            rowpb[t % 2, t // 2] = block

    @pl.when(r == 0)
    def _():
        panel = jnp.concatenate([panel_cols(a_v, s) for s in range(3)], axis=1)
        zero = jnp.zeros_like(panel)
        gx[x] = dot_nt(panel[:32], jnp.concatenate([panel, zero], axis=0)) + dot_nt(
            panel[32:], jnp.concatenate([zero, panel], axis=0)
        )

        @pl.when(c == 0)
        def _():
            p1[...] = a_v[pl.ds(3 * NB, NB, stride=3), :]

        colpb[...] = a_v[0:384, :]

    when(owner, lambda: pl.semaphore_wait(barrier, 61))
    when(plain, lambda: pl.semaphore_wait(barrier, 46))

    parts = ((0, 192), (192, 192))

    def send_col(part):
        rows = pl.ds(*parts[part])

        def to(q):
            other = 2 * spiral(q, 8) + jnp.where(q == 7, 1, 0)
            copy(a_v.at[rows], colpb.at[rows], colp_s.at[part], colp_r.at[part], (other, c)).start()

        loop(0, 8, to)

    def wait_col(part):
        rows = pl.ds(*parts[part])

        @pl.when(r != 0)
        def _():
            arrived(colpb.at[rows], colp_r.at[part])

            @pl.when(core == 0)
            def _():
                copy(colpb.at[rows], colpb.at[rows], fwd_s.at[part], colp_r.at[part], (r + 1, c)).start()

    def scatter(part):
        def to(p):
            k = 2 * spiral(lax.div(p, 2), 8) + 1 - lax.rem(p, 2)
            dev = panel_owner(k) if part == 0 else other_owner(k)
            copy(chunk(k, part), chunk(k, part), sc_s, sc_r, (r, dev)).start()

        loop(0, 15 + part, to)

    when(c == 0, lambda: scatter(0))

    @pl.when(r == 0)
    def _():
        send_col(0)
        loop(0, 3, lambda p: copy(gx.at[x], gx.at[x], g_s.at[0], g_r.at[0], (r, x_peer(p))).start())

        @pl.when(c == 0)
        def _():
            loop(0, 3, lambda p: copy(p1, p1, p1_s.at[0], p1_r, (r, x_peer(p))).start())

    when(c == 0, lambda: scatter(1))

    wait_col(0)

    def pass_to(k, part, dev, ssem, sem):
        copy(chunk(k, part), chunk(k, part), ag_s.at[ssem], ag_r.at[sem], (r, dev)).start()

    one = jnp.int32(1)
    n_first, n_across, n_b = jnp.int32(0), jnp.int32(0), jnp.int32(0)

    firsts = []
    for p in range(7):
        dev = panel_owner(8 * my_h + lax.rem(my_g + 4 + p + (1 if p > 3 else 0), 8))
        firsts.append((dev, owner & (dev != 0)))
    downs = []
    for p in range(7):
        dev = z_peer(p)
        dev_z = lax.div(dev, 4)
        first = (lax.rem(dev_z + x, 2) == 0) & (lax.div(dev_z, 4) == my_h)
        downs.append((dev, owner & (dev != 0) & jnp.logical_not(first), plain & (dev != 0)))
    acrosses = []
    for p in range(3):
        dev = x_peer(p)
        dev_owner = lax.rem(lax.rem(dev, 4) + z, 2) == 0
        for i in range(4):
            k = 4 * i + 2 * lax.rem(x, 2) + lax.div(x, 2)
            skip = dev_owner & (lax.div(z, 4) == i // 2)
            k_b = 4 * i + 2 * lax.rem(x + 1, 2) + lax.div(x, 2)
            acrosses.append((dev, k, (dev != 0) & jnp.logical_not(skip), k_b, dev != 0))

    panel = jnp.concatenate([panel_cols(colpb, s) for s in range(3)], axis=1)
    def share(t):
        tile = jnp.concatenate([a_v[pl.ds(t * 384 + s, 128, stride=3), :] for s in range(3)], axis=1)
        zt = dot3(panel, tile, (1, 1))
        for g in range(8):
            zpart[g + 8 * (t % 2), t // 2] = zt[8 * g : 8 * g + 8, :]

    def reduce_to(k):
        dev = panel_owner(k)

        @pl.when(dev != c)
        def _():
            copy(zpart.at[k], zrecv.at[c], rs_s, rs_r, (r, dev)).start()

    for t in (0, 2, 4):
        share(t)
    @pl.when(r == 0)
    def _():
        arrived(gx.at[pl.ds(0, 3)], g_r.at[0])
        gz[z] = (gx[0] + gx[1]) + (gx[2] + gx[3])
        loop(0, 7, lambda p: copy(gz.at[z], gz.at[z], g_s.at[1], g_r.at[1], (r, z_peer(p))).start())

        @pl.when(z == 0)
        def _():
            when(x != 0, lambda: arrived(p1, p1_r))
            loop(0, 7, lambda p: copy(p1, p1, p1_s.at[1], p1_r, (r, z_peer(p))).start())

    @pl.when(owner)
    def _():
        when(c != 0, lambda: arrived(chunk(mine, 0), sc_r))

    for dev, go in firsts:
        when(go, functools.partial(pass_to, mine, 0, dev, 0, 2))
        n_first = n_first + jnp.where(go, one, 0)
    loop(0, 8, reduce_to)
    for t in (1, 3, 5):
        share(t)
    loop(8, 16, reduce_to)

    when(r == 0, lambda: send_col(1))

    for dev, go, go_b in downs:
        when(go, functools.partial(pass_to, mine, 0, dev, 0, 0))
        n_first = n_first + jnp.where(go, one, 0)

    for dev, k, go, k_b, go_b in acrosses:
        n_across = n_across + jnp.where(go, one, 0)
        n_b = n_b + jnp.where(go_b, one, 0)

    def pass_across():
        for dev, k, go, k_b, go_b in acrosses:
            when(go, functools.partial(pass_to, k, 0, dev, 1, 3))
        for dev, k, go, k_b, go_b in acrosses:
            when(go_b, functools.partial(pass_to, k_b, 1, dev, 2, 4))

    def z_across():
        def to(p):
            k = 4 * lax.rem(p, 4) + 2 * lax.rem(x, 2) + lax.div(x, 2)
            copy(zrows.at[k], zrows.at[k], zr_s.at[1], zr_r.at[1], (r, x_peer(lax.div(p, 4)))).start()

        loop(0, 12, to)

    def sent_some(n, sem, least, most):
        for count in range(least, most + 1):
            when(n == count, lambda count=count: sent(some(count), sem))

    for dev, go, go_b in downs:
        n_b = n_b + jnp.where(go_b, one, 0)

    @pl.when(r == 0)
    def _():
        arrived(gz.at[pl.ds(0, 7)], g_r.at[1])
        gfin[...] = ((gz[0] + gz[1]) + (gz[2] + gz[3])) + ((gz[4] + gz[5]) + (gz[6] + gz[7]))
        loop(0, 15, lambda p: copy(gfin, gfin, g_s.at[2], g_r.at[2], (row_peer(p), c)).start())
        when(z != 0, lambda: arrived(p1, p1_r))
        loop(0, 15, lambda p: copy(p1, p1, p1_s.at[2], p1_r, (row_peer(p), c)).start())


    @pl.when(owner)
    def _():
        arrived(some(31), rs_r)
        zrecv[c] = zpart[mine]
        zsum = lax.fori_loop(1, 32, lambda i, total: total + zrecv[i], zrecv[0])
        zrows[mine] = zsum
        when(c != 0, lambda: arrived(some(7), ag_r.at[2]))
        rows = jnp.concatenate([rowpb[my_h, i, 0:NB, :] for i in range(3)], axis=1)
        total = dot3(
            jnp.concatenate([zsum[i] for i in range(3)], axis=1),
            jnp.concatenate([rows, jnp.zeros_like(rows)], axis=0),
            (1, 1),
        )
        lane8 = lax.broadcasted_iota(jnp.int32, (8, 128), 1)
        total = total + jnp.where((r == 0) & (my_h == 0) & (lane8 >= NB), zsum[0], 0.0)
        hsend[0] = total
        hrecv[r] = total
        loop(0, 15, lambda p: copy(hsend.at[0], hrecv.at[r], h_s, h_r, (row_peer(p), c)).start())
        there = r + 16 * my_h
        loop(0, 15, lambda p: copy(zrows.at[mine], zcols.at[my_g], zc_s, zc_r, (row_peer(p), there)).start())
        loop(0, 7, lambda p: copy(zrows.at[mine], zrows.at[mine], zr_s.at[0], zr_r.at[0], (r, z_peer(p))).start())
        wait_col(1)
        @pl.when(c != 0)
        def _():
            arrived(some(2), ag_r.at[0])
            arrived(some(4), ag_r.at[1])

        pass_across()
        arrived(hrecv.at[pl.ds(0, 15)], h_r)
        hall[mine] = lax.fori_loop(1, 16, lambda i, total: total + hrecv[i], hrecv[0])
        loop(0, 31, lambda p: copy(hall.at[mine], hall.at[mine], ha_s, ha_r, (r, early_peer(p))).start())
        arrived(some(3), zr_r.at[0])
        z_across()
        @pl.when(c != 0)
        def _():
            arrived(some(6), ag_r.at[3])
            arrived(some(12), ag_r.at[4])

        @pl.when(r != 0)
        def _():
            arrived(gfin, g_r.at[2])
            arrived(p1, p1_r)

        arrived(c0, c0_r.at[0])
        arrived(om, c0_r.at[1])

    @pl.when(plain)
    def _():
        when(r != 0, lambda: arrived(gfin, g_r.at[2]))
        arrived(chunk(mine, 1), sc_r)
        for dev, go, go_b in downs:
            when(go_b, functools.partial(pass_to, mine, 1, dev, 2, 1))
        packed = gfin[...]
        gram = jnp.concatenate([packed, pltpu.roll(packed, 64, 1)], axis=0)
        gram = jnp.where(lane < NB, gram, 0.0)
        ct[0:NB, :] = jnp.zeros((NB, 128), F32)
        factor_cholesky(gram, ct)
        c0[...] = jnp.transpose(ct[...])[0:NB, :]
        copy(c0, c0, c0_s.at[0], c0_r.at[0], (r, partner)).start()
        when(r != 0, lambda: arrived(p1, p1_r))
        corner = p1[...]
        product = dot_nn(pltpu.roll(c0[...], 64, 1), jnp.concatenate([corner, jnp.zeros_like(corner)], axis=0))
        whole = invert(gram + jnp.where(lane < NB, product, 0.0))
        om[...] = whole[0:32, :] + pltpu.roll(whole[32:, :], 64, 1)
        copy(om, om, c0_s.at[1], c0_r.at[1], (r, partner)).start()
        wait_col(1)
        arrived(some(4), ag_r.at[0])
        arrived(some(3), ag_r.at[1])
        pass_across()
        arrived(some(4), zr_r.at[0])
        z_across()
        arrived(some(12), ag_r.at[3])
        arrived(some(12), ag_r.at[4])

    sub = lax.broadcasted_iota(jnp.int32, (NB, 128), 0)
    c0v = c0[...]
    unit = jnp.where(sub == lane, 1.0, 0.0)
    pad = jnp.zeros((NB, 128), F32)
    packed_om = om[...]
    inverse = jnp.where(lane < NB, jnp.concatenate([packed_om, pltpu.roll(packed_om, 64, 1)], axis=0), 0.0)
    s_mat = dot_nn(inverse, jnp.concatenate([unit + c0v, pad], axis=0))
    c_cols = jnp.where(c == 0, c0v, 0.0)
    c_rows = jnp.where(r == 0, c0v, 0.0)

    arrived(some(12), zr_r.at[1])

    zb, n_rows = [], []
    for t in range(6):
        h, i = t % 2, t // 2
        zb.append(
            jnp.concatenate([zrows[8 * h : 8 * h + 8, i].reshape(NB, 128), rowpb[h, i, NB:, :]], axis=0)
        )
        n_t = rowpb[h, i, 0:NB, :]
        if t == 0:
            n_t = n_t + c_rows
        n_rows.append(n_t)
    w_rows = dot3(s_mat, jnp.concatenate(zb, axis=1), (1, 0))
    for t in range(6):
        rows = jnp.concatenate([w_rows[:, 128 * t : 128 * t + 128], n_rows[t]], axis=0)
        high, low = split(jnp.transpose(rows))
        left_o[t] = jnp.concatenate([high, high, low], axis=1)

    @pl.when(home)
    def _():
        zcols[...] = zrows[pl.ds(8 * lax.div(c, 16), 8)]

    when(jnp.logical_not(home), lambda: arrived(zcols, zc_r))

    zb = [
        jnp.concatenate([zcols[:, s].reshape(NB, 128), colpb[pl.ds(192 + s, NB, stride=3), :]], axis=0) for s in range(3)
    ]
    w_cols = dot3(s_mat, jnp.concatenate(zb, axis=1), (1, 0))
    n_cols = [panel_cols(colpb, s) for s in range(3)]
    n_cols = jnp.concatenate([n_cols[0] + c_cols] + n_cols[1:], axis=1)
    right_o[0:NB, :] = n_cols
    s_turned = jnp.transpose(jnp.concatenate([s_mat, pad], axis=0))
    sn_cols = dot3(s_turned[:, 0:NB], n_cols, (1, 0))

    when(owner, lambda: arrived(hall.at[pl.ds(0, 15)], ha_r))
    when(plain, lambda: arrived(hall, ha_r))

    top = (hall[0:8] + hall[8:16]).reshape(NB, 128)
    turned = jnp.transpose(jnp.concatenate([top, pad], axis=0))
    bottom = jnp.where(lane < NB, turned[NB:, :], p1[...])
    inner = dot3(jnp.concatenate([top, bottom], axis=0), sn_cols, (1, 0))
    right_o[NB:, :] = w_cols - dot3(s_mat, inner, (1, 0))

    @pl.when(r == 0)
    def _():
        for part in range(2):
            sent(a_v.at[pl.ds(0, 8 * parts[part][1])], colp_s.at[part])
        sent(gx.at[pl.ds(0, 3)], g_s.at[0])
        sent(gz.at[pl.ds(0, 7)], g_s.at[1])
        sent(a_v.at[pl.ds(0, 15 * 32)], g_s.at[2])
        when(c == 0, lambda: sent(a_v.at[pl.ds(0, 3 * NB)], p1_s.at[0]))
        when(z == 0, lambda: sent(a_v.at[pl.ds(0, 7 * NB)], p1_s.at[1]))
        sent(a_v.at[pl.ds(0, 15 * NB)], p1_s.at[2])

    @pl.when((r != 0) & (core == 0))
    def _():
        for part in range(2):
            sent(colpb.at[pl.ds(*parts[part])], fwd_s.at[part])

    @pl.when(c == 0)
    def _():
        sent(some(31), sc_s)

    when(owner, lambda: sent_some(n_first, ag_s.at[0], 10, 14))
    sent_some(n_across, ag_s.at[1], 4, 12)
    sent(some(12), zr_s.at[1])
    sent_some(n_b, ag_s.at[2], 8, 19)

    @pl.when(owner)
    def _():
        sent(some(15), rs_s)
        sent(some(15), zc_s)
        sent(some(7), zr_s.at[0])
        sent(a_v.at[pl.ds(0, 15 * 8)], h_s)
        sent(a_v.at[pl.ds(0, 31 * 8)], ha_s)

    @pl.when(plain)
    def _():
        sent(some(16), rs_s)
        sent(c0, c0_s.at[0])
        sent(om, c0_s.at[1])


def update(a, left, right, out, tiles, sems):
    high, low = split(right[...])
    columns = jnp.concatenate([high, low, high], axis=0)
    for t in range(6):
        change = jnp.dot(left[t], columns, preferred_element_type=F32)
        for s in range(3):
            rows = pl.ds(t * 384 + s, 128, stride=3)
            tiles[rows, :] = a[rows, :] - change[:, 128 * s : 128 * s + 128]
        rows = pl.ds(t * 384, 384)
        pltpu.make_async_copy(tiles.at[rows], out.at[rows], sems.at[t]).start()
    for t in range(6):
        rows = pl.ds(t * 384, 384)
        pltpu.make_async_copy(tiles.at[rows], out.at[rows], sems.at[t]).wait()


def vmem(*shape):
    return pltpu.VMEM(shape, F32)


def dma(*shape):
    return pltpu.SemaphoreType.DMA(shape)


def body(hessian):
    flat = hessian.reshape(2304, 128)
    whole = pl.BlockSpec(memory_space=pltpu.VMEM)
    left, right = pl.pallas_call(
        kernel,
        out_shape=[jax.ShapeDtypeStruct((6, 128, 384), jnp.bfloat16), jax.ShapeDtypeStruct((128, 384), F32)],
        in_specs=[pl.BlockSpec(memory_space=pltpu.HBM)],
        out_specs=[whole, whole],
        scratch_shapes=[
            vmem(2304, 128), vmem(384, 128), vmem(2, 3, 128, 128), vmem(16, 3, 8, 128), vmem(32, 3, 8, 128),
            vmem(16, 3, 8, 128), vmem(8, 3, 8, 128), vmem(4, 32, 128), vmem(8, 32, 128), vmem(32, 128),
            vmem(64, 128), vmem(1, 8, 128), vmem(16, 8, 128), vmem(16, 8, 128), vmem(128, 128), vmem(64, 128), vmem(32, 128),
            dma(), dma(2), dma(2), dma(2), dma(), dma(), dma(3), dma(5), dma(), dma(), dma(2), dma(2), dma(), dma(),
            dma(3), dma(3), dma(3), dma(), dma(), dma(), dma(), dma(), dma(2), dma(2),
        ],
        compiler_params=pltpu.CompilerParams(collective_id=0, has_side_effects=True, vmem_limit_bytes=54208 << 10),
        name="panel",
    )(flat)
    out = pl.pallas_call(
        update,
        out_shape=jax.ShapeDtypeStruct((2304, 128), F32),
        in_specs=[whole, whole, whole],
        out_specs=pl.BlockSpec(memory_space=pltpu.HBM),
        scratch_shapes=[vmem(2304, 128), dma(6)],
        compiler_params=pltpu.CompilerParams(vmem_limit_bytes=16 << 20),
        name="update",
    )(flat, left, right)
    return out.reshape(hessian.shape)


def solution(mesh):
    return jax.shard_map(
        body,
        mesh=mesh,
        in_specs=(P(None, "row", None, None, "col", None),),
        out_specs=P(None, "row", None, None, "col", None),
        check_vma=False,
    )
```

```python
import functools

import jax
import jax.numpy as jnp
from jax import lax
from jax.experimental import pallas as pl
from jax.experimental.pallas import tpu as pltpu
from jax.sharding import PartitionSpec as P

NB = 64
MESH = pl.DeviceIdType.MESH
HIGHEST = lax.Precision.HIGHEST
F32 = jnp.float32


def dot_nn(a, b):
    return lax.dot_general(a, b, (((1,), (0,)), ((), ())), precision=HIGHEST, preferred_element_type=F32)


def dot_nt(a, b):
    return lax.dot_general(a, b, (((1,), (1,)), ((), ())), precision=HIGHEST, preferred_element_type=F32)


def split(a):
    high = a.astype(jnp.bfloat16)
    return high, (a - high.astype(F32)).astype(jnp.bfloat16)


def dot3(a, b, dims):
    (ah, al), (bh, bl) = split(a), split(b)
    left = jnp.concatenate([ah, ah, al], axis=dims[0])
    right = jnp.concatenate([bh, bl, bh], axis=dims[1])
    return lax.dot_general(left, right, (((dims[0],), (dims[1],)), ((), ())), preferred_element_type=F32)


def split(a):
    high = a.astype(jnp.bfloat16)
    return high, (a - high.astype(F32)).astype(jnp.bfloat16)


def dot3(a, b, dims):
    (ah, al), (bh, bl) = split(a), split(b)
    left = jnp.concatenate([ah, ah, al], axis=dims[0])
    right = jnp.concatenate([bh, bl, bh], axis=dims[1])
    return lax.dot_general(left, right, (((dims[0],), (dims[1],)), ((), ())), preferred_element_type=F32)


def split(a):
    high = a.astype(jnp.bfloat16)
    return high, (a - high.astype(F32)).astype(jnp.bfloat16)


def dot3(a, b, dims):
    (ah, al), (bh, bl) = split(a), split(b)
    left = jnp.concatenate([ah, ah, al], axis=dims[0])
    right = jnp.concatenate([bh, bl, bh], axis=dims[1])
    return lax.dot_general(left, right, (((dims[0],), (dims[1],)), ((), ())), preferred_element_type=F32)


def spiral(q, n):
    return lax.rem(n // 2 + (1 - 2 * lax.rem(q, 2)) * lax.div(q + 1, 2), n)


def loop(lo, hi, f):
    def step(i, carry):
        f(i)
        return carry

    lax.fori_loop(lo, hi, step, 0)


def factor_cholesky(g, ct):
    lane1 = lax.broadcasted_iota(jnp.int32, (1, 128), 1)
    for first in range(0, NB, 8):
        rest = g[first:, :]
        cols = [jnp.broadcast_to(rest[:, first + j : first + j + 1], rest.shape) for j in range(8)]
        rows = [rest[j : j + 1, :] for j in range(8)]
        for j in range(8):
            k = first + j
            pivot = cols[j][j : j + 1, :]
            inverse = 1.0 / pivot
            scaled = rows[j] * inverse
            ct[NB + k : NB + k + 1, :] = jnp.where((lane1 >= k) & (lane1 < NB), rows[j] * lax.rsqrt(pivot), 0.0)
            for i in range(j + 1, 8):
                factor = cols[i][j : j + 1, :] * inverse
                rows[i] = rows[i] - cols[j][i : i + 1, :] * scaled
                cols[i] = cols[i] - cols[j] * factor
            rest = rest - cols[j] * scaled
        g = rest if first == 0 else jnp.concatenate([g[:first, :], rest], axis=0)


def invert(m):
    lane1 = lax.broadcasted_iota(jnp.int32, (1, 128), 1)
    lane = lax.broadcasted_iota(jnp.int32, (NB, 128), 1)
    sub = lax.broadcasted_iota(jnp.int32, (NB, 128), 0)
    for first in range(0, NB, 8):
        cols = [jnp.broadcast_to(m[:, first + j : first + j + 1], (NB, 128)) for j in range(8)]
        rows = [m[first + j : first + j + 1, :] for j in range(8)]
        for j in range(8):
            k = first + j
            inverse = 1.0 / cols[j][k : k + 1, :]
            scaled = jnp.where(lane1 == k, 1.0, rows[j]) * inverse
            for i in range(j + 1, 8):
                factor = cols[i][k : k + 1, :] * inverse
                rows[i] = jnp.where(lane1 == k, 0.0, rows[i]) - cols[j][first + i : first + i + 1, :] * scaled
                cols[i] = jnp.where(sub == k, factor, cols[i] - cols[j] * factor)
            m = jnp.where(sub == k, scaled, jnp.where(lane == k, 0.0, m) - cols[j] * scaled)
    return m


def kernel(
    a_hbm, left_o, right_o, a_v, colpb, rowpb, zpart, zrecv, zrows, zcols, gx, gz, gfin, p1, hsend, hrecv, hall, ct, c0, om,
    load_s, colp_s, colp_r, fwd_s, sc_s, sc_r, ag_s, ag_r, rs_s, rs_r, zr_s, zr_r, zc_s, zc_r,
    g_s, g_r, p1_s, p1_r, h_s, h_r, ha_s, ha_r,
):
    r, c = lax.axis_index("row"), lax.axis_index("col")
    y, core = lax.div(r, 2), lax.rem(r, 2)
    z, x = lax.div(c, 4), lax.rem(c, 4)
    mine = lax.div(c, 2)
    owner = lax.rem(x + z, 2) == 0
    plain = jnp.logical_not(owner)
    my_g, my_h = lax.rem(mine, 8), lax.div(mine, 8)
    partner = c + 1 - 2 * lax.rem(c, 2)
    home = lax.rem(c, 16) == r
    lane = lax.broadcasted_iota(jnp.int32, (NB, 128), 1)

    def panel_owner(k):
        return 2 * k + lax.rem(lax.div(k, 2), 2)

    def other_owner(k):
        return 2 * k + 1 - lax.rem(lax.div(k, 2), 2)

    def col_peer(p):
        return lax.rem(z + spiral(lax.div(p, 4), 8), 8) * 4 + lax.rem(x + spiral(lax.rem(p, 4), 4), 4)

    def early_peer(p):
        place = z * 4 + x
        return p + jnp.where(p >= place, 1, 0)

    def x_peer(p):
        return z * 4 + lax.rem(x + spiral(p, 4), 4)

    def far_peer(p):
        return lax.rem(z + spiral(p, 8), 8) * 4 + lax.rem(x + 2, 4)

    def z_peer(p):
        return lax.rem(z + spiral(p, 8), 8) * 4 + x

    def row_peer(p):
        return lax.rem(y + spiral(lax.div(p, 2), 8), 8) * 2 + lax.rem(core + 1 - lax.rem(p, 2), 2)

    def copy(src, dst, ssem, rsem, dev):
        return pltpu.make_async_remote_copy(
            src_ref=src, dst_ref=dst, send_sem=ssem, recv_sem=rsem, device_id=dev, device_id_type=MESH
        )

    def sent(ref, sem):
        copy(ref, ref, sem, sem, (r, partner)).wait_send()

    def arrived(ref, sem):
        copy(ref, ref, sem, sem, (r, partner)).wait_recv()

    def when(condition, f):
        pl.when(condition)(f)

    def chunk(k, part):
        rows = pl.multiple_of(lax.rem(k, 8) * 8 + part * NB, 8)
        return rowpb.at[lax.div(k, 8), :, pl.ds(rows, 8), :]

    def some(n):
        return zrecv.at[pl.ds(0, n)]

    load = pltpu.make_async_copy(a_hbm, a_v, load_s)
    load.start()
    barrier = pltpu.get_barrier_semaphore()

    def greet(dev):
        pl.semaphore_signal(barrier, inc=1, device_id=dev, device_id_type=MESH)

    loop(0, 15, lambda p: greet((row_peer(p), c)))

    @pl.when(jnp.logical_not(home) & (core == 0))
    def _():
        loop(0, 8, lambda g: greet((lax.rem(c, 16), panel_owner(g + 8 * lax.div(c, 16)))))

    loop(0, 31, lambda p: greet((r, col_peer(p))))

    load.wait()

    def panel_cols(ref, s):
        return jnp.where((c == 0) & (s == 0) & (lane < NB), 0.0, ref[pl.ds(s, NB, stride=3), :])

    @pl.when(c == 0)
    def _():
        full = lax.broadcasted_iota(jnp.int32, (128, 128), 0)
        full_lane = lax.broadcasted_iota(jnp.int32, (128, 128), 1)
        for t in range(6):
            block = jnp.transpose(a_v[pl.ds(t * 384, 128, stride=3), :])
            if t == 0:
                block = jnp.where((r == 0) & (full < NB) & (full_lane < NB), 0.0, block)
            rowpb[t % 2, t // 2] = block

    @pl.when(r == 0)
    def _():
        panel = jnp.concatenate([panel_cols(a_v, s) for s in range(3)], axis=1)
        zero = jnp.zeros_like(panel)
        gx[x] = dot_nt(panel[:32], jnp.concatenate([panel, zero], axis=0)) + dot_nt(
            panel[32:], jnp.concatenate([zero, panel], axis=0)
        )

        @pl.when(c == 0)
        def _():
            p1[...] = a_v[pl.ds(3 * NB, NB, stride=3), :]

        colpb[...] = a_v[0:192, :]

    when(owner & (core == 0), lambda: pl.semaphore_wait(barrier, 53))
    when(owner & (core == 1), lambda: pl.semaphore_wait(barrier, 54))
    when(plain, lambda: pl.semaphore_wait(barrier, 46))

    columns = pl.ds(0, 192)

    def send_col(q):
        other = 2 * spiral(q, 8) + jnp.where(q == 7, 1, 0)
        copy(a_v.at[columns], colpb, colp_s, colp_r, (other, c)).start()

    def wait_col():
        @pl.when(r != 0)
        def _():
            arrived(colpb, colp_r)

            @pl.when(core == 0)
            def _():
                copy(colpb, colpb, fwd_s.at[0], colp_r, (r + 1, c)).start()

    def scatter(part):
        def to(p):
            k = 2 * spiral(lax.div(p, 2), 8) + 1 - lax.rem(p, 2)
            dev = panel_owner(k) if part == 0 else other_owner(k)
            copy(chunk(k, part), chunk(k, part), sc_s, sc_r, (r, dev)).start()

        loop(0, 15 + part, to)

    when(c == 0, lambda: scatter(0))

    @pl.when(r == 0)
    def _():
        loop(0, 8, send_col)
        loop(0, 3, lambda p: copy(gx.at[x], gx.at[x], g_s.at[0], g_r.at[0], (r, x_peer(p))).start())

        @pl.when(c == 0)
        def _():
            loop(0, 3, lambda p: copy(p1, p1, p1_s.at[0], p1_r, (r, x_peer(p))).start())

    when(c == 0, lambda: scatter(1))

    wait_col()

    def pass_to(k, part, dev, ssem, sem):
        copy(chunk(k, part), chunk(k, part), ag_s.at[ssem], ag_r.at[sem], (r, dev)).start()

    one = jnp.int32(1)
    n_first, n_across, n_b = jnp.int32(0), jnp.int32(0), jnp.int32(0)

    firsts = []
    for p in range(7):
        dev = panel_owner(8 * my_h + lax.rem(my_g + 4 + p + (1 if p > 3 else 0), 8))
        firsts.append((dev, owner & (dev != 0)))
    downs = []
    for p in range(7):
        dev = z_peer(p)
        dev_z = lax.div(dev, 4)
        first = (lax.rem(dev_z + x, 2) == 0) & (lax.div(dev_z, 4) == my_h)
        downs.append((dev, owner & (dev != 0) & jnp.logical_not(first)))
    acrosses = []
    for p in range(3):
        dev = x_peer(p)
        dev_owner = lax.rem(lax.rem(dev, 4) + z, 2) == 0
        for i in range(4):
            k = 4 * i + 2 * lax.rem(x, 2) + lax.div(x, 2)
            skip = dev_owner & (lax.div(z, 4) == i // 2)
            acrosses.append((dev, k, (dev != 0) & jnp.logical_not(skip)))

    panel = jnp.concatenate([panel_cols(colpb, s) for s in range(3)], axis=1)
    def share(t):
        tile = jnp.concatenate([a_v[pl.ds(t * 384 + s, 128, stride=3), :] for s in range(3)], axis=1)
        zt = dot3(panel, tile, (1, 1))
        for g in range(8):
            zpart[g + 8 * (t % 2), t // 2] = zt[8 * g : 8 * g + 8, :]

    def reduce_to(k):
        dev = panel_owner(k)

        @pl.when(dev != c)
        def _():
            copy(zpart.at[k], zrecv.at[c], rs_s, rs_r, (r, dev)).start()

    for t in (0, 2, 4):
        share(t)
    @pl.when(r == 0)
    def _():
        arrived(gx.at[pl.ds(0, 3)], g_r.at[0])
        gz[z] = (gx[0] + gx[1]) + (gx[2] + gx[3])
        loop(0, 7, lambda p: copy(gz.at[z], gz.at[z], g_s.at[1], g_r.at[1], (r, z_peer(p))).start())

        @pl.when(z == 0)
        def _():
            when(x != 0, lambda: arrived(p1, p1_r))
            loop(0, 7, lambda p: copy(p1, p1, p1_s.at[1], p1_r, (r, z_peer(p))).start())

    @pl.when(owner)
    def _():
        when(c != 0, lambda: arrived(chunk(mine, 0), sc_r))

    for dev, go in firsts:
        when(go, functools.partial(pass_to, mine, 0, dev, 0, 2))
        n_first = n_first + jnp.where(go, one, 0)
    loop(0, 8, lambda p: reduce_to(7 - p))
    for t in (1, 3, 5):
        share(t)
    loop(8, 16, reduce_to)

    for dev, go in downs:
        when(go, functools.partial(pass_to, mine, 0, dev, 0, 0))
        n_first = n_first + jnp.where(go, one, 0)

    for dev, k, go in acrosses:
        n_across = n_across + jnp.where(go, one, 0)

    when(plain, lambda: arrived(chunk(mine, 1), sc_r))
    for p in range(8):
        dev = panel_owner(8 * my_h + lax.rem(my_g + 4 + p, 8))
        when(plain & (dev != 0), functools.partial(pass_to, mine, 1, dev, 2, 1))
        n_b = n_b + jnp.where(plain & (dev != 0), one, 0)

    def pass_across():
        for dev, k, go in acrosses:
            when(go, functools.partial(pass_to, k, 0, dev, 1, 3))

    def z_across():
        def to(p):
            k = 4 * lax.rem(p, 4) + 2 * lax.rem(x, 2) + lax.div(x, 2)
            copy(zrows.at[k], zrows.at[k], zr_s.at[1], zr_r.at[1], (r, x_peer(1 + lax.div(p, 4)))).start()

        loop(0, 8, to)

    def sent_some(n, sem, least, most):
        for count in range(least, most + 1):
            when(n == count, lambda count=count: sent(some(count), sem))

    @pl.when(r == 0)
    def _():
        arrived(gz.at[pl.ds(0, 7)], g_r.at[1])
        gfin[...] = ((gz[0] + gz[1]) + (gz[2] + gz[3])) + ((gz[4] + gz[5]) + (gz[6] + gz[7]))
        loop(0, 15, lambda p: copy(gfin, gfin, g_s.at[2], g_r.at[2], (row_peer(p), c)).start())
        when(z != 0, lambda: arrived(p1, p1_r))
        loop(0, 15, lambda p: copy(p1, p1, p1_s.at[2], p1_r, (row_peer(p), c)).start())


    def gram_matrix():
        packed = gfin[...]
        gram = jnp.concatenate([packed, pltpu.roll(packed, 64, 1)], axis=0)
        return jnp.where(lane < NB, gram, 0.0)

    def cholesky():
        when(r != 0, lambda: arrived(gfin, g_r.at[2]))
        ct[0:NB, :] = jnp.zeros((NB, 128), F32)
        factor_cholesky(gram_matrix(), ct)
        c0[...] = jnp.transpose(ct[...])[0:NB, :]

    def inverse():
        when(r != 0, lambda: arrived(p1, p1_r))
        corner = p1[...]
        product = dot_nn(pltpu.roll(c0[...], 64, 1), jnp.concatenate([corner, jnp.zeros_like(corner)], axis=0))
        whole = invert(gram_matrix() + jnp.where(lane < NB, product, 0.0))
        om[...] = whole

    @pl.when(owner)
    def _():
        cholesky()
        when(c != 0, lambda: arrived(some(7), ag_r.at[2]))
        rows = jnp.concatenate([rowpb[my_h, i, 0:NB, :] for i in range(3)], axis=1)
        high, low = split(jnp.concatenate([rows, jnp.zeros_like(rows)], axis=0))
        arrived(some(31), rs_r)
        zrecv[c] = zpart[mine]
        zsum = lax.fori_loop(1, 32, lambda i, total: total + zrecv[i], zrecv[0])
        z_rows = jnp.concatenate([zsum[i] for i in range(3)], axis=1)
        z_high, z_low = split(z_rows)
        total = lax.dot_general(
            jnp.concatenate([z_high, z_high, z_low], axis=1),
            jnp.concatenate([high, low, high], axis=1),
            (((1,), (1,)), ((), ())),
            preferred_element_type=F32,
        )
        lane8 = lax.broadcasted_iota(jnp.int32, (8, 128), 1)
        total = total + jnp.where((r == 0) & (my_h == 0) & (lane8 >= NB), zsum[0], 0.0)
        hsend[0] = total
        hrecv[r] = total
        loop(0, 15, lambda p: copy(hsend.at[0], hrecv.at[r], h_s, h_r, (row_peer(p), c)).start())
        when(c != 0, lambda: arrived(some(8), ag_r.at[1]))
        mine_c = c0[pl.ds(pl.multiple_of(8 * my_g, 8), 8), :]
        y_rows = z_rows + dot3(mine_c, jnp.concatenate([rowpb[my_h, i] for i in range(3)], axis=1), (1, 0))
        for i in range(3):
            zrows[mine, i] = y_rows[:, 128 * i : 128 * i + 128]
        there = r + 16 * my_h

        loop(0, 7, lambda p: copy(zrows.at[mine], zrows.at[mine], zr_s.at[0], zr_r.at[0], (r, z_peer(p))).start())
        loop(0, 8, lambda p: copy(zrows.at[mine], zrows.at[mine], zr_s.at[0], zr_r.at[2], (r, far_peer(p))).start())
        def to_cols(p):
            dev = 2 * lax.rem(y + spiral(p, 8), 8)
            when(dev != r, lambda: copy(zrows.at[mine], zcols.at[my_g], zc_s, zc_r, (dev, there)).start())

        loop(0, 8, to_cols)
        inverse()
        when(c != 0, lambda: arrived(some(2), ag_r.at[0]))
        pass_across()
        arrived(hrecv.at[pl.ds(0, 15)], h_r)
        hall[mine] = lax.fori_loop(1, 16, lambda i, total: total + hrecv[i], hrecv[0])
        loop(0, 31, lambda p: copy(hall.at[mine], hall.at[mine], ha_s, ha_r, (r, early_peer(p))).start())
        arrived(some(3), zr_r.at[0])
        z_across()
        @pl.when(c != 0)
        def _():
            arrived(some(6), ag_r.at[3])


    @pl.when(plain)
    def _():
        cholesky()
        inverse()
        arrived(some(4), ag_r.at[0])
        pass_across()
        arrived(some(4), zr_r.at[0])
        z_across()
        arrived(some(12), ag_r.at[3])

    def forward_cols():
        copy(zcols, zcols, fwd_s.at[1], zc_r, (r + 1, c)).start()

    home_next = lax.rem(c, 16) == r + 1

    @pl.when(jnp.logical_not(home) & (core == 0))
    def _():
        arrived(zcols, zc_r)
        when(jnp.logical_not(home_next), forward_cols)

    inverse_t = om[:, 0:NB]
    pad = jnp.zeros((NB, 128), F32)
    sub = lax.broadcasted_iota(jnp.int32, (NB, 128), 0)
    unit = jnp.where(sub == lane, 1.0, 0.0)
    s_mat = dot_nn(inverse_t, unit + c0[...])
    turned = jnp.transpose(jnp.concatenate([s_mat, pad], axis=0))
    c_cols = jnp.where(c == 0, c0[...], 0.0)
    c_rows = jnp.where(r == 0, c0[...], 0.0)
    n_cols = [panel_cols(colpb, s) for s in range(3)]
    n_cols = jnp.concatenate([n_cols[0] + c_cols] + n_cols[1:], axis=1)
    right_o[0:NB, :] = n_cols
    sn_cols = dot3(turned[:, 0:NB], n_cols, (1, 0))

    arrived(some(4), zr_r.at[2])
    arrived(some(8), zr_r.at[1])

    y_rows, n_rows = [], []
    for t in range(6):
        h, i = t % 2, t // 2
        y_rows.append(zrows[8 * h : 8 * h + 8, i].reshape(NB, 128))
        n_t = rowpb[h, i, 0:NB, :]
        if t == 0:
            n_t = n_t + c_rows
        n_rows.append(n_t)
    w_rows = dot3(inverse_t, jnp.concatenate(y_rows, axis=1), (1, 0))
    for t in range(6):
        rows = jnp.concatenate([w_rows[:, 128 * t : 128 * t + 128], n_rows[t]], axis=0)
        high, low = split(jnp.transpose(rows))
        left_o[t] = jnp.concatenate([high, high, low], axis=1)

    @pl.when(home)
    def _():
        zcols[...] = zrows[pl.ds(8 * lax.div(c, 16), 8)]

    when(home & (core == 0), forward_cols)
    when(jnp.logical_not(home) & (core == 1), lambda: arrived(zcols, zc_r))

    y_cols = jnp.concatenate([zcols[:, s].reshape(NB, 128) for s in range(3)], axis=1)
    w_cols = dot3(inverse_t, y_cols, (1, 0))

    when(owner, lambda: arrived(hall.at[pl.ds(0, 15)], ha_r))
    when(plain, lambda: arrived(hall, ha_r))

    top = (hall[0:8] + hall[8:16]).reshape(NB, 128)
    turned = jnp.transpose(jnp.concatenate([top, pad], axis=0))
    bottom = jnp.where(lane < NB, turned[NB:, :], p1[...])
    inner = dot3(jnp.concatenate([top, bottom], axis=0), sn_cols, (1, 0))
    right_o[NB:, :] = w_cols - dot3(s_mat, inner, (1, 0))

    @pl.when(r == 0)
    def _():
        sent(a_v.at[pl.ds(0, 8 * 192)], colp_s)
        sent(gx.at[pl.ds(0, 3)], g_s.at[0])
        sent(gz.at[pl.ds(0, 7)], g_s.at[1])
        sent(a_v.at[pl.ds(0, 15 * 32)], g_s.at[2])
        when(c == 0, lambda: sent(a_v.at[pl.ds(0, 3 * NB)], p1_s.at[0]))
        when(z == 0, lambda: sent(a_v.at[pl.ds(0, 7 * NB)], p1_s.at[1]))
        sent(a_v.at[pl.ds(0, 15 * NB)], p1_s.at[2])

    @pl.when((r != 0) & (core == 0))
    def _():
        sent(colpb, fwd_s.at[0])

    @pl.when(c == 0)
    def _():
        sent(some(31), sc_s)

    when(owner, lambda: sent_some(n_first, ag_s.at[0], 10, 14))
    sent_some(n_across, ag_s.at[1], 4, 12)
    sent(some(8), zr_s.at[1])
    when(plain, lambda: sent_some(n_b, ag_s.at[2], 7, 8))

    @pl.when(owner)
    def _():
        sent(some(15), rs_s)
        when(core == 0, lambda: sent(some(7), zc_s))
        when(core == 1, lambda: sent(some(8), zc_s))
        sent(some(15), zr_s.at[0])
        sent(a_v.at[pl.ds(0, 15 * 8)], h_s)
        sent(a_v.at[pl.ds(0, 31 * 8)], ha_s)

    when((core == 0) & jnp.logical_not(home_next), lambda: sent(zcols, fwd_s.at[1]))

    @pl.when(plain)
    def _():
        sent(some(16), rs_s)


def update(a, left, right, out, tiles, sems):
    high, low = split(right[...])
    columns = jnp.concatenate([high, low, high], axis=0)
    for t in range(6):
        change = jnp.dot(left[t], columns, preferred_element_type=F32)
        for s in range(3):
            rows = pl.ds(t * 384 + s, 128, stride=3)
            tiles[rows, :] = a[rows, :] - change[:, 128 * s : 128 * s + 128]
        rows = pl.ds(t * 384, 384)
        pltpu.make_async_copy(tiles.at[rows], out.at[rows], sems.at[t]).start()
    for t in range(6):
        rows = pl.ds(t * 384, 384)
        pltpu.make_async_copy(tiles.at[rows], out.at[rows], sems.at[t]).wait()


def vmem(*shape):
    return pltpu.VMEM(shape, F32)


def dma(*shape):
    return pltpu.SemaphoreType.DMA(shape)


def body(hessian):
    flat = hessian.reshape(2304, 128)
    whole = pl.BlockSpec(memory_space=pltpu.VMEM)
    left, right = pl.pallas_call(
        kernel,
        out_shape=[jax.ShapeDtypeStruct((6, 128, 384), jnp.bfloat16), jax.ShapeDtypeStruct((128, 384), F32)],
        in_specs=[pl.BlockSpec(memory_space=pltpu.HBM)],
        out_specs=[whole, whole],
        scratch_shapes=[
            vmem(2304, 128), vmem(192, 128), vmem(2, 3, 128, 128), vmem(16, 3, 8, 128), vmem(32, 3, 8, 128),
            vmem(16, 3, 8, 128), vmem(8, 3, 8, 128), vmem(4, 32, 128), vmem(8, 32, 128), vmem(32, 128),
            vmem(64, 128), vmem(1, 8, 128), vmem(16, 8, 128), vmem(16, 8, 128), vmem(128, 128), vmem(64, 128), vmem(64, 128),
            dma(), dma(), dma(), dma(2), dma(), dma(), dma(3), dma(4), dma(), dma(), dma(2), dma(3), dma(), dma(),
            dma(3), dma(3), dma(3), dma(), dma(), dma(), dma(), dma(),
        ],
        compiler_params=pltpu.CompilerParams(collective_id=0, has_side_effects=True, vmem_limit_bytes=54208 << 10),
        name="panel",
    )(flat)
    out = pl.pallas_call(
        update,
        out_shape=jax.ShapeDtypeStruct((2304, 128), F32),
        in_specs=[whole, whole, whole],
        out_specs=pl.BlockSpec(memory_space=pltpu.HBM),
        scratch_shapes=[vmem(2304, 128), dma(6)],
        compiler_params=pltpu.CompilerParams(vmem_limit_bytes=16 << 20),
        name="update",
    )(flat, left, right)
    return out.reshape(hessian.shape)


def solution(mesh):
    return jax.shard_map(
        body,
        mesh=mesh,
        in_specs=(P(None, "row", None, None, "col", None),),
        out_specs=P(None, "row", None, None, "col", None),
        check_vma=False,
    )
```

```python
import functools

import jax
import jax.numpy as jnp
from jax import lax
from jax.experimental import pallas as pl
from jax.experimental.pallas import tpu as pltpu
from jax.sharding import PartitionSpec as P

NB = 64
MESH = pl.DeviceIdType.MESH
HIGHEST = lax.Precision.HIGHEST
F32 = jnp.float32


def dot_nn(a, b):
    return lax.dot_general(a, b, (((1,), (0,)), ((), ())), precision=HIGHEST, preferred_element_type=F32)


def dot_nt(a, b):
    return lax.dot_general(a, b, (((1,), (1,)), ((), ())), precision=HIGHEST, preferred_element_type=F32)


def split(a):
    high = a.astype(jnp.bfloat16)
    return high, (a - high.astype(F32)).astype(jnp.bfloat16)


def dot3(a, b, dims):
    (ah, al), (bh, bl) = split(a), split(b)
    left = jnp.concatenate([ah, ah, al], axis=dims[0])
    right = jnp.concatenate([bh, bl, bh], axis=dims[1])
    return lax.dot_general(left, right, (((dims[0],), (dims[1],)), ((), ())), preferred_element_type=F32)


def split(a):
    high = a.astype(jnp.bfloat16)
    return high, (a - high.astype(F32)).astype(jnp.bfloat16)


def dot3(a, b, dims):
    (ah, al), (bh, bl) = split(a), split(b)
    left = jnp.concatenate([ah, ah, al], axis=dims[0])
    right = jnp.concatenate([bh, bl, bh], axis=dims[1])
    return lax.dot_general(left, right, (((dims[0],), (dims[1],)), ((), ())), preferred_element_type=F32)


def split(a):
    high = a.astype(jnp.bfloat16)
    return high, (a - high.astype(F32)).astype(jnp.bfloat16)


def dot3(a, b, dims):
    (ah, al), (bh, bl) = split(a), split(b)
    left = jnp.concatenate([ah, ah, al], axis=dims[0])
    right = jnp.concatenate([bh, bl, bh], axis=dims[1])
    return lax.dot_general(left, right, (((dims[0],), (dims[1],)), ((), ())), preferred_element_type=F32)


def spiral(q, n):
    return lax.rem(n // 2 + (1 - 2 * lax.rem(q, 2)) * lax.div(q + 1, 2), n)


def loop(lo, hi, f):
    def step(i, carry):
        f(i)
        return carry

    lax.fori_loop(lo, hi, step, 0)


def factor_cholesky(g, ct):
    lane1 = lax.broadcasted_iota(jnp.int32, (1, 128), 1)
    for first in range(0, NB, 8):
        rest = g[first:, :]
        cols = [jnp.broadcast_to(rest[:, first + j : first + j + 1], rest.shape) for j in range(8)]
        rows = [rest[j : j + 1, :] for j in range(8)]
        for j in range(8):
            k = first + j
            pivot = cols[j][j : j + 1, :]
            inverse = 1.0 / pivot
            scaled = rows[j] * inverse
            ct[NB + k : NB + k + 1, :] = jnp.where((lane1 >= k) & (lane1 < NB), rows[j] * lax.rsqrt(pivot), 0.0)
            for i in range(j + 1, 8):
                factor = cols[i][j : j + 1, :] * inverse
                rows[i] = rows[i] - cols[j][i : i + 1, :] * scaled
                cols[i] = cols[i] - cols[j] * factor
            rest = rest - cols[j] * scaled
        g = rest if first == 0 else jnp.concatenate([g[:first, :], rest], axis=0)


def invert(m):
    lane1 = lax.broadcasted_iota(jnp.int32, (1, 128), 1)
    lane = lax.broadcasted_iota(jnp.int32, (NB, 128), 1)
    sub = lax.broadcasted_iota(jnp.int32, (NB, 128), 0)
    for first in range(0, NB, 8):
        cols = [jnp.broadcast_to(m[:, first + j : first + j + 1], (NB, 128)) for j in range(8)]
        rows = [m[first + j : first + j + 1, :] for j in range(8)]
        for j in range(8):
            k = first + j
            inverse = 1.0 / cols[j][k : k + 1, :]
            scaled = jnp.where(lane1 == k, 1.0, rows[j]) * inverse
            for i in range(j + 1, 8):
                factor = cols[i][k : k + 1, :] * inverse
                rows[i] = jnp.where(lane1 == k, 0.0, rows[i]) - cols[j][first + i : first + i + 1, :] * scaled
                cols[i] = jnp.where(sub == k, factor, cols[i] - cols[j] * factor)
            m = jnp.where(sub == k, scaled, jnp.where(lane == k, 0.0, m) - cols[j] * scaled)
    return m


def kernel(
    a_hbm, left_o, right_o, a_v, colpb, rowpb, zpart, zrecv, zrows, zcols, gx, gz, gfin, p1, hsend, hrecv, hall, ct, c0, om,
    load_s, colp_s, colp_r, fwd_s, sc_s, sc_r, ag_s, ag_r, rs_s, rs_r, zr_s, zr_r, zc_s, zc_r,
    g_s, g_r, p1_s, p1_r, h_s, h_r, ha_s, ha_r,
):
    r, c = lax.axis_index("row"), lax.axis_index("col")
    y, core = lax.div(r, 2), lax.rem(r, 2)
    z, x = lax.div(c, 4), lax.rem(c, 4)
    mine = lax.div(c, 2)
    owner = lax.rem(x + z, 2) == 0
    plain = jnp.logical_not(owner)
    my_g, my_h = lax.rem(mine, 8), lax.div(mine, 8)
    partner = c + 1 - 2 * lax.rem(c, 2)
    home = lax.rem(c, 16) == r
    lane = lax.broadcasted_iota(jnp.int32, (NB, 128), 1)

    def panel_owner(k):
        return 2 * k + lax.rem(lax.div(k, 2), 2)

    def other_owner(k):
        return 2 * k + 1 - lax.rem(lax.div(k, 2), 2)

    def col_peer(p):
        return lax.rem(z + spiral(lax.div(p, 4), 8), 8) * 4 + lax.rem(x + spiral(lax.rem(p, 4), 4), 4)

    def early_peer(p):
        place = z * 4 + x
        return p + jnp.where(p >= place, 1, 0)

    def x_peer(p):
        return z * 4 + lax.rem(x + spiral(p, 4), 4)

    def far_peer(p):
        return lax.rem(z + spiral(p, 8), 8) * 4 + lax.rem(x + 2, 4)

    def z_peer(p):
        return lax.rem(z + spiral(p, 8), 8) * 4 + x

    def row_peer(p):
        return lax.rem(y + spiral(lax.div(p, 2), 8), 8) * 2 + lax.rem(core + 1 - lax.rem(p, 2), 2)

    def copy(src, dst, ssem, rsem, dev):
        return pltpu.make_async_remote_copy(
            src_ref=src, dst_ref=dst, send_sem=ssem, recv_sem=rsem, device_id=dev, device_id_type=MESH
        )

    def sent(ref, sem):
        copy(ref, ref, sem, sem, (r, partner)).wait_send()

    def arrived(ref, sem):
        copy(ref, ref, sem, sem, (r, partner)).wait_recv()

    def when(condition, f):
        pl.when(condition)(f)

    def chunk(k, part):
        rows = pl.multiple_of(lax.rem(k, 8) * 8 + part * NB, 8)
        return rowpb.at[lax.div(k, 8), :, pl.ds(rows, 8), :]

    def some(n):
        return zrecv.at[pl.ds(0, n)]

    load = pltpu.make_async_copy(a_hbm, a_v, load_s)
    load.start()
    barrier = pltpu.get_barrier_semaphore()

    def greet(dev):
        pl.semaphore_signal(barrier, inc=1, device_id=dev, device_id_type=MESH)

    loop(0, 15, lambda p: greet((row_peer(p), c)))

    @pl.when(jnp.logical_not(home) & (core == 0))
    def _():
        loop(0, 8, lambda g: greet((lax.rem(c, 16), panel_owner(g + 8 * lax.div(c, 16)))))

    loop(0, 31, lambda p: greet((r, col_peer(p))))

    load.wait()

    def panel_cols(ref, s):
        return jnp.where((c == 0) & (s == 0) & (lane < NB), 0.0, ref[pl.ds(s, NB, stride=3), :])

    @pl.when(c == 0)
    def _():
        full = lax.broadcasted_iota(jnp.int32, (128, 128), 0)
        full_lane = lax.broadcasted_iota(jnp.int32, (128, 128), 1)
        for t in range(6):
            block = jnp.transpose(a_v[pl.ds(t * 384, 128, stride=3), :])
            if t == 0:
                block = jnp.where((r == 0) & (full < NB) & (full_lane < NB), 0.0, block)
            rowpb[t % 2, t // 2] = block

    @pl.when(r == 0)
    def _():
        panel = jnp.concatenate([panel_cols(a_v, s) for s in range(3)], axis=1)
        zero = jnp.zeros_like(panel)
        gx[x] = dot_nt(panel[:32], jnp.concatenate([panel, zero], axis=0)) + dot_nt(
            panel[32:], jnp.concatenate([zero, panel], axis=0)
        )

        @pl.when(c == 0)
        def _():
            p1[...] = a_v[pl.ds(3 * NB, NB, stride=3), :]

        colpb[...] = a_v[0:192, :]

    when(owner & (core == 0), lambda: pl.semaphore_wait(barrier, 53))
    when(owner & (core == 1), lambda: pl.semaphore_wait(barrier, 54))
    when(plain, lambda: pl.semaphore_wait(barrier, 46))

    columns = pl.ds(0, 192)

    def send_col(q):
        other = 2 * spiral(q, 8) + jnp.where(q == 7, 1, 0)
        copy(a_v.at[columns], colpb, colp_s, colp_r, (other, c)).start()

    def wait_col():
        @pl.when(r != 0)
        def _():
            arrived(colpb, colp_r)

            @pl.when(core == 0)
            def _():
                copy(colpb, colpb, fwd_s.at[0], colp_r, (r + 1, c)).start()

    def scatter(part):
        def to(p):
            k = 2 * spiral(lax.div(p, 2), 8) + 1 - lax.rem(p, 2)
            dev = panel_owner(k) if part == 0 else other_owner(k)
            copy(chunk(k, part), chunk(k, part), sc_s, sc_r, (r, dev)).start()

        loop(0, 15 + part, to)

    when(c == 0, lambda: scatter(0))

    @pl.when(r == 0)
    def _():
        loop(0, 8, send_col)
        loop(0, 3, lambda p: copy(gx.at[x], gx.at[x], g_s.at[0], g_r.at[0], (r, x_peer(p))).start())

        @pl.when(c == 0)
        def _():
            loop(0, 3, lambda p: copy(p1, p1, p1_s.at[0], p1_r, (r, x_peer(p))).start())

    when(c == 0, lambda: scatter(1))

    wait_col()

    def pass_to(k, part, dev, ssem, sem):
        copy(chunk(k, part), chunk(k, part), ag_s.at[ssem], ag_r.at[sem], (r, dev)).start()

    one = jnp.int32(1)
    n_first, n_across, n_b = jnp.int32(0), jnp.int32(0), jnp.int32(0)

    firsts = []
    for p in range(7):
        dev = panel_owner(8 * my_h + lax.rem(my_g + 4 + p + (1 if p > 3 else 0), 8))
        firsts.append((dev, owner & (dev != 0)))
    downs = []
    for p in range(7):
        dev = z_peer(p)
        dev_z = lax.div(dev, 4)
        first = (lax.rem(dev_z + x, 2) == 0) & (lax.div(dev_z, 4) == my_h)
        downs.append((dev, owner & (dev != 0) & jnp.logical_not(first)))
    acrosses = []
    for p in range(3):
        dev = x_peer(p)
        dev_owner = lax.rem(lax.rem(dev, 4) + z, 2) == 0
        for i in range(4):
            k = 4 * i + 2 * lax.rem(x, 2) + lax.div(x, 2)
            skip = dev_owner & (lax.div(z, 4) == i // 2)
            acrosses.append((dev, k, (dev != 0) & jnp.logical_not(skip)))

    panel = jnp.concatenate([panel_cols(colpb, s) for s in range(3)], axis=1)
    def share(t):
        tile = jnp.concatenate([a_v[pl.ds(t * 384 + s, 128, stride=3), :] for s in range(3)], axis=1)
        zt = dot3(panel, tile, (1, 1))
        for g in range(8):
            zpart[g + 8 * (t % 2), t // 2] = zt[8 * g : 8 * g + 8, :]

    def reduce_to(k):
        dev = panel_owner(k)

        @pl.when(dev != c)
        def _():
            copy(zpart.at[k], zrecv.at[c], rs_s, rs_r, (r, dev)).start()

    for t in (0, 2, 4):
        share(t)
    @pl.when(r == 0)
    def _():
        arrived(gx.at[pl.ds(0, 3)], g_r.at[0])
        gz[z] = (gx[0] + gx[1]) + (gx[2] + gx[3])
        loop(0, 7, lambda p: copy(gz.at[z], gz.at[z], g_s.at[1], g_r.at[1], (r, z_peer(p))).start())

        @pl.when(z == 0)
        def _():
            when(x != 0, lambda: arrived(p1, p1_r))
            loop(0, 7, lambda p: copy(p1, p1, p1_s.at[1], p1_r, (r, z_peer(p))).start())

    @pl.when(owner)
    def _():
        when(c != 0, lambda: arrived(chunk(mine, 0), sc_r))

    for dev, go in firsts:
        when(go, functools.partial(pass_to, mine, 0, dev, 0, 2))
        n_first = n_first + jnp.where(go, one, 0)
    loop(0, 8, lambda p: reduce_to(7 - p))
    for t in (1, 3, 5):
        share(t)
    loop(8, 16, reduce_to)

    for dev, go in downs:
        when(go, functools.partial(pass_to, mine, 0, dev, 0, 0))
        n_first = n_first + jnp.where(go, one, 0)

    for dev, k, go in acrosses:
        n_across = n_across + jnp.where(go, one, 0)

    when(plain, lambda: arrived(chunk(mine, 1), sc_r))
    for p in range(8):
        dev = panel_owner(8 * my_h + lax.rem(my_g + 4 + p, 8))
        when(plain & (dev != 0), functools.partial(pass_to, mine, 1, dev, 2, 1))
        n_b = n_b + jnp.where(plain & (dev != 0), one, 0)

    def pass_across():
        for dev, k, go in acrosses:
            when(go, functools.partial(pass_to, k, 0, dev, 1, 3))

    def z_across():
        def to(p):
            k = 4 * lax.rem(p, 4) + 2 * lax.rem(x, 2) + lax.div(x, 2)
            copy(zrows.at[k], zrows.at[k], zr_s.at[1], zr_r.at[1], (r, x_peer(1 + lax.div(p, 4)))).start()

        loop(0, 8, to)

    def sent_some(n, sem, least, most):
        for count in range(least, most + 1):
            when(n == count, lambda count=count: sent(some(count), sem))

    @pl.when(r == 0)
    def _():
        arrived(gz.at[pl.ds(0, 7)], g_r.at[1])
        gfin[...] = ((gz[0] + gz[1]) + (gz[2] + gz[3])) + ((gz[4] + gz[5]) + (gz[6] + gz[7]))
        loop(0, 15, lambda p: copy(gfin, gfin, g_s.at[2], g_r.at[2], (row_peer(p), c)).start())
        when(z != 0, lambda: arrived(p1, p1_r))
        loop(0, 15, lambda p: copy(p1, p1, p1_s.at[2], p1_r, (row_peer(p), c)).start())


    def gram_matrix():
        packed = gfin[...]
        gram = jnp.concatenate([packed, pltpu.roll(packed, 64, 1)], axis=0)
        return jnp.where(lane < NB, gram, 0.0)

    def cholesky():
        when(r != 0, lambda: arrived(gfin, g_r.at[2]))
        ct[0:NB, :] = jnp.zeros((NB, 128), F32)
        factor_cholesky(gram_matrix(), ct)
        c0[...] = jnp.transpose(ct[...])[0:NB, :]

    def inverse():
        when(r != 0, lambda: arrived(p1, p1_r))
        corner = p1[...]
        product = dot_nn(pltpu.roll(c0[...], 64, 1), jnp.concatenate([corner, jnp.zeros_like(corner)], axis=0))
        whole = invert(gram_matrix() + jnp.where(lane < NB, product, 0.0))
        om[...] = whole

    @pl.when(owner)
    def _():
        cholesky()
        when(c != 0, lambda: arrived(some(7), ag_r.at[2]))
        rows = jnp.concatenate([rowpb[my_h, i, 0:NB, :] for i in range(3)], axis=1)
        high, low = split(jnp.concatenate([rows, jnp.zeros_like(rows)], axis=0))
        arrived(some(31), rs_r)
        zrecv[c] = zpart[mine]
        zsum = lax.fori_loop(1, 32, lambda i, total: total + zrecv[i], zrecv[0])
        z_rows = jnp.concatenate([zsum[i] for i in range(3)], axis=1)
        z_high, z_low = split(z_rows)
        total = lax.dot_general(
            jnp.concatenate([z_high, z_high, z_low], axis=1),
            jnp.concatenate([high, low, high], axis=1),
            (((1,), (1,)), ((), ())),
            preferred_element_type=F32,
        )
        lane8 = lax.broadcasted_iota(jnp.int32, (8, 128), 1)
        total = total + jnp.where((r == 0) & (my_h == 0) & (lane8 >= NB), zsum[0], 0.0)
        hsend[0] = total
        hrecv[r] = total
        loop(0, 15, lambda p: copy(hsend.at[0], hrecv.at[r], h_s, h_r, (row_peer(p), c)).start())
        when(c != 0, lambda: arrived(some(8), ag_r.at[1]))
        mine_c = c0[pl.ds(pl.multiple_of(8 * my_g, 8), 8), :]
        y_rows = z_rows + dot3(mine_c, jnp.concatenate([rowpb[my_h, i] for i in range(3)], axis=1), (1, 0))
        for i in range(3):
            zrows[mine, i] = y_rows[:, 128 * i : 128 * i + 128]
        there = r + 16 * my_h

        loop(0, 7, lambda p: copy(zrows.at[mine], zrows.at[mine], zr_s.at[0], zr_r.at[0], (r, z_peer(p))).start())
        loop(0, 8, lambda p: copy(zrows.at[mine], zrows.at[mine], zr_s.at[0], zr_r.at[2], (r, far_peer(p))).start())
        def to_cols(p):
            dev = 2 * lax.rem(y + spiral(p, 8), 8)
            when(dev != r, lambda: copy(zrows.at[mine], zcols.at[my_g], zc_s, zc_r, (dev, there)).start())

        loop(0, 8, to_cols)
        when(c != 0, lambda: arrived(some(2), ag_r.at[0]))
        pass_across()
        inverse()
        arrived(hrecv.at[pl.ds(0, 15)], h_r)
        hall[mine] = lax.fori_loop(1, 16, lambda i, total: total + hrecv[i], hrecv[0])
        loop(0, 31, lambda p: copy(hall.at[mine], hall.at[mine], ha_s, ha_r, (r, early_peer(p))).start())
        arrived(some(3), zr_r.at[0])
        z_across()
        @pl.when(c != 0)
        def _():
            arrived(some(6), ag_r.at[3])


    @pl.when(plain)
    def _():
        arrived(some(4), ag_r.at[0])
        pass_across()
        cholesky()
        inverse()
        arrived(some(4), zr_r.at[0])
        z_across()
        arrived(some(12), ag_r.at[3])

    def forward_cols():
        copy(zcols, zcols, fwd_s.at[1], zc_r, (r + 1, c)).start()

    home_next = lax.rem(c, 16) == r + 1

    @pl.when(jnp.logical_not(home) & (core == 0))
    def _():
        arrived(zcols, zc_r)
        when(jnp.logical_not(home_next), forward_cols)

    inverse_t = om[:, 0:NB]
    pad = jnp.zeros((NB, 128), F32)
    sub = lax.broadcasted_iota(jnp.int32, (NB, 128), 0)
    unit = jnp.where(sub == lane, 1.0, 0.0)
    s_mat = dot_nn(inverse_t, unit + c0[...])
    turned = jnp.transpose(jnp.concatenate([s_mat, pad], axis=0))
    c_cols = jnp.where(c == 0, c0[...], 0.0)
    c_rows = jnp.where(r == 0, c0[...], 0.0)
    n_cols = [panel_cols(colpb, s) for s in range(3)]
    n_cols = jnp.concatenate([n_cols[0] + c_cols] + n_cols[1:], axis=1)
    right_o[0:NB, :] = n_cols
    sn_cols = dot3(turned[:, 0:NB], n_cols, (1, 0))

    arrived(some(4), zr_r.at[2])
    arrived(some(8), zr_r.at[1])

    y_rows, n_rows = [], []
    for t in range(6):
        h, i = t % 2, t // 2
        y_rows.append(zrows[8 * h : 8 * h + 8, i].reshape(NB, 128))
        n_t = rowpb[h, i, 0:NB, :]
        if t == 0:
            n_t = n_t + c_rows
        n_rows.append(n_t)
    w_rows = dot3(inverse_t, jnp.concatenate(y_rows, axis=1), (1, 0))
    for t in range(6):
        rows = jnp.concatenate([w_rows[:, 128 * t : 128 * t + 128], n_rows[t]], axis=0)
        high, low = split(jnp.transpose(rows))
        left_o[t] = jnp.concatenate([high, high, low], axis=1)

    @pl.when(home)
    def _():
        zcols[...] = zrows[pl.ds(8 * lax.div(c, 16), 8)]

    when(home & (core == 0), forward_cols)
    when(jnp.logical_not(home) & (core == 1), lambda: arrived(zcols, zc_r))

    y_cols = jnp.concatenate([zcols[:, s].reshape(NB, 128) for s in range(3)], axis=1)
    w_cols = dot3(inverse_t, y_cols, (1, 0))

    when(owner, lambda: arrived(hall.at[pl.ds(0, 15)], ha_r))
    when(plain, lambda: arrived(hall, ha_r))

    top = (hall[0:8] + hall[8:16]).reshape(NB, 128)
    turned = jnp.transpose(jnp.concatenate([top, pad], axis=0))
    bottom = jnp.where(lane < NB, turned[NB:, :], p1[...])
    inner = dot3(jnp.concatenate([top, bottom], axis=0), sn_cols, (1, 0))
    right_o[NB:, :] = w_cols - dot3(s_mat, inner, (1, 0))

    @pl.when(r == 0)
    def _():
        sent(a_v.at[pl.ds(0, 8 * 192)], colp_s)
        sent(gx.at[pl.ds(0, 3)], g_s.at[0])
        sent(gz.at[pl.ds(0, 7)], g_s.at[1])
        sent(a_v.at[pl.ds(0, 15 * 32)], g_s.at[2])
        when(c == 0, lambda: sent(a_v.at[pl.ds(0, 3 * NB)], p1_s.at[0]))
        when(z == 0, lambda: sent(a_v.at[pl.ds(0, 7 * NB)], p1_s.at[1]))
        sent(a_v.at[pl.ds(0, 15 * NB)], p1_s.at[2])

    @pl.when((r != 0) & (core == 0))
    def _():
        sent(colpb, fwd_s.at[0])

    @pl.when(c == 0)
    def _():
        sent(some(31), sc_s)

    when(owner, lambda: sent_some(n_first, ag_s.at[0], 10, 14))
    sent_some(n_across, ag_s.at[1], 4, 12)
    sent(some(8), zr_s.at[1])
    when(plain, lambda: sent_some(n_b, ag_s.at[2], 7, 8))

    @pl.when(owner)
    def _():
        sent(some(15), rs_s)
        when(core == 0, lambda: sent(some(7), zc_s))
        when(core == 1, lambda: sent(some(8), zc_s))
        sent(some(15), zr_s.at[0])
        sent(a_v.at[pl.ds(0, 15 * 8)], h_s)
        sent(a_v.at[pl.ds(0, 31 * 8)], ha_s)

    when((core == 0) & jnp.logical_not(home_next), lambda: sent(zcols, fwd_s.at[1]))

    @pl.when(plain)
    def _():
        sent(some(16), rs_s)


def update(a, left, right, out, tiles, sems):
    high, low = split(right[...])
    columns = jnp.concatenate([high, low, high], axis=0)
    for t in range(6):
        change = jnp.dot(left[t], columns, preferred_element_type=F32)
        for s in range(3):
            rows = pl.ds(t * 384 + s, 128, stride=3)
            tiles[rows, :] = a[rows, :] - change[:, 128 * s : 128 * s + 128]
        rows = pl.ds(t * 384, 384)
        pltpu.make_async_copy(tiles.at[rows], out.at[rows], sems.at[t]).start()
    for t in range(6):
        rows = pl.ds(t * 384, 384)
        pltpu.make_async_copy(tiles.at[rows], out.at[rows], sems.at[t]).wait()


def vmem(*shape):
    return pltpu.VMEM(shape, F32)


def dma(*shape):
    return pltpu.SemaphoreType.DMA(shape)


def body(hessian):
    flat = hessian.reshape(2304, 128)
    whole = pl.BlockSpec(memory_space=pltpu.VMEM)
    left, right = pl.pallas_call(
        kernel,
        out_shape=[jax.ShapeDtypeStruct((6, 128, 384), jnp.bfloat16), jax.ShapeDtypeStruct((128, 384), F32)],
        in_specs=[pl.BlockSpec(memory_space=pltpu.HBM)],
        out_specs=[whole, whole],
        scratch_shapes=[
            vmem(2304, 128), vmem(192, 128), vmem(2, 3, 128, 128), vmem(16, 3, 8, 128), vmem(32, 3, 8, 128),
            vmem(16, 3, 8, 128), vmem(8, 3, 8, 128), vmem(4, 32, 128), vmem(8, 32, 128), vmem(32, 128),
            vmem(64, 128), vmem(1, 8, 128), vmem(16, 8, 128), vmem(16, 8, 128), vmem(128, 128), vmem(64, 128), vmem(64, 128),
            dma(), dma(), dma(), dma(2), dma(), dma(), dma(3), dma(4), dma(), dma(), dma(2), dma(3), dma(), dma(),
            dma(3), dma(3), dma(3), dma(), dma(), dma(), dma(), dma(),
        ],
        compiler_params=pltpu.CompilerParams(collective_id=0, has_side_effects=True, vmem_limit_bytes=54208 << 10),
        name="panel",
    )(flat)
    out = pl.pallas_call(
        update,
        out_shape=jax.ShapeDtypeStruct((2304, 128), F32),
        in_specs=[whole, whole, whole],
        out_specs=pl.BlockSpec(memory_space=pltpu.HBM),
        scratch_shapes=[vmem(2304, 128), dma(6)],
        compiler_params=pltpu.CompilerParams(vmem_limit_bytes=16 << 20),
        name="update",
    )(flat, left, right)
    return out.reshape(hessian.shape)


def solution(mesh):
    return jax.shard_map(
        body,
        mesh=mesh,
        in_specs=(P(None, "row", None, None, "col", None),),
        out_specs=P(None, "row", None, None, "col", None),
        check_vma=False,
    )
```

```python
import functools

import jax
import jax.numpy as jnp
from jax import lax
from jax.experimental import pallas as pl
from jax.experimental.pallas import tpu as pltpu
from jax.sharding import PartitionSpec as P

NB = 64
MESH = pl.DeviceIdType.MESH
HIGHEST = lax.Precision.HIGHEST
F32 = jnp.float32


def dot_nn(a, b):
    return lax.dot_general(a, b, (((1,), (0,)), ((), ())), precision=HIGHEST, preferred_element_type=F32)


def dot_nt(a, b):
    return lax.dot_general(a, b, (((1,), (1,)), ((), ())), precision=HIGHEST, preferred_element_type=F32)


def split(a):
    high = a.astype(jnp.bfloat16)
    return high, (a - high.astype(F32)).astype(jnp.bfloat16)


def dot3(a, b, dims):
    (ah, al), (bh, bl) = split(a), split(b)
    left = jnp.concatenate([ah, ah, al], axis=dims[0])
    right = jnp.concatenate([bh, bl, bh], axis=dims[1])
    return lax.dot_general(left, right, (((dims[0],), (dims[1],)), ((), ())), preferred_element_type=F32)


def split(a):
    high = a.astype(jnp.bfloat16)
    return high, (a - high.astype(F32)).astype(jnp.bfloat16)


def dot3(a, b, dims):
    (ah, al), (bh, bl) = split(a), split(b)
    left = jnp.concatenate([ah, ah, al], axis=dims[0])
    right = jnp.concatenate([bh, bl, bh], axis=dims[1])
    return lax.dot_general(left, right, (((dims[0],), (dims[1],)), ((), ())), preferred_element_type=F32)


def split(a):
    high = a.astype(jnp.bfloat16)
    return high, (a - high.astype(F32)).astype(jnp.bfloat16)


def dot3(a, b, dims):
    (ah, al), (bh, bl) = split(a), split(b)
    left = jnp.concatenate([ah, ah, al], axis=dims[0])
    right = jnp.concatenate([bh, bl, bh], axis=dims[1])
    return lax.dot_general(left, right, (((dims[0],), (dims[1],)), ((), ())), preferred_element_type=F32)


def spiral(q, n):
    return lax.rem(n // 2 + (1 - 2 * lax.rem(q, 2)) * lax.div(q + 1, 2), n)


def tree_sum(terms):
    while len(terms) > 1:
        terms = [a + b for a, b in zip(terms[0::2], terms[1::2])]
    return terms[0]


def loop(lo, hi, f):
    def step(i, carry):
        f(i)
        return carry

    lax.fori_loop(lo, hi, step, 0)


def factor_cholesky(g, ct):
    lane1 = lax.broadcasted_iota(jnp.int32, (1, 128), 1)
    for first in range(0, NB, 8):
        rest = g[first:, :]
        cols = [jnp.broadcast_to(rest[:, first + j : first + j + 1], rest.shape) for j in range(8)]
        rows = [rest[j : j + 1, :] for j in range(8)]
        for j in range(8):
            k = first + j
            pivot = cols[j][j : j + 1, :]
            inverse = 1.0 / pivot
            scaled = rows[j] * inverse
            ct[NB + k : NB + k + 1, :] = jnp.where((lane1 >= k) & (lane1 < NB), rows[j] * lax.rsqrt(pivot), 0.0)
            for i in range(j + 1, 8):
                factor = cols[i][j : j + 1, :] * inverse
                rows[i] = rows[i] - cols[j][i : i + 1, :] * scaled
                cols[i] = cols[i] - cols[j] * factor
            rest = rest - cols[j] * scaled
        g = rest if first == 0 else jnp.concatenate([g[:first, :], rest], axis=0)


def invert(m):
    lane1 = lax.broadcasted_iota(jnp.int32, (1, 128), 1)
    lane = lax.broadcasted_iota(jnp.int32, (NB, 128), 1)
    sub = lax.broadcasted_iota(jnp.int32, (NB, 128), 0)
    for first in range(0, NB, 8):
        cols = [jnp.broadcast_to(m[:, first + j : first + j + 1], (NB, 128)) for j in range(8)]
        rows = [m[first + j : first + j + 1, :] for j in range(8)]
        for j in range(8):
            k = first + j
            inverse = 1.0 / cols[j][k : k + 1, :]
            scaled = jnp.where(lane1 == k, 1.0, rows[j]) * inverse
            for i in range(j + 1, 8):
                factor = cols[i][k : k + 1, :] * inverse
                rows[i] = jnp.where(lane1 == k, 0.0, rows[i]) - cols[j][first + i : first + i + 1, :] * scaled
                cols[i] = jnp.where(sub == k, factor, cols[i] - cols[j] * factor)
            m = jnp.where(sub == k, scaled, jnp.where(lane == k, 0.0, m) - cols[j] * scaled)
    return m


def kernel(
    a_hbm, left_o, right_o, a_v, colpb, rowpb, zpart, zrecv, zrows, zcols, gx, gz, gfin, p1, hsend, hrecv, hall, ct, c0, om,
    load_s, colp_s, colp_r, fwd_s, sc_s, sc_r, ag_s, ag_r, rs_s, rs_r, zr_s, zr_r, zc_s, zc_r,
    g_s, g_r, p1_s, p1_r, h_s, h_r, ha_s, ha_r,
):
    r, c = lax.axis_index("row"), lax.axis_index("col")
    y, core = lax.div(r, 2), lax.rem(r, 2)
    z, x = lax.div(c, 4), lax.rem(c, 4)
    mine = lax.div(c, 2)
    owner = lax.rem(x + z, 2) == 0
    plain = jnp.logical_not(owner)
    my_g, my_h = lax.rem(mine, 8), lax.div(mine, 8)
    partner = c + 1 - 2 * lax.rem(c, 2)
    home = lax.rem(c, 16) == r
    lane = lax.broadcasted_iota(jnp.int32, (NB, 128), 1)

    def panel_owner(k):
        return 2 * k + lax.rem(lax.div(k, 2), 2)

    def other_owner(k):
        return 2 * k + 1 - lax.rem(lax.div(k, 2), 2)

    def col_peer(p):
        return lax.rem(z + spiral(lax.div(p, 4), 8), 8) * 4 + lax.rem(x + spiral(lax.rem(p, 4), 4), 4)

    def early_peer(p):
        place = z * 4 + x
        return p + jnp.where(p >= place, 1, 0)

    def x_peer(p):
        return z * 4 + lax.rem(x + spiral(p, 4), 4)

    def far_peer(p):
        return lax.rem(z + spiral(p, 8), 8) * 4 + lax.rem(x + 2, 4)

    def z_peer(p):
        return lax.rem(z + spiral(p, 8), 8) * 4 + x

    def row_peer(p):
        return lax.rem(y + spiral(lax.div(p, 2), 8), 8) * 2 + lax.rem(core + 1 - lax.rem(p, 2), 2)

    def copy(src, dst, ssem, rsem, dev):
        return pltpu.make_async_remote_copy(
            src_ref=src, dst_ref=dst, send_sem=ssem, recv_sem=rsem, device_id=dev, device_id_type=MESH
        )

    def sent(ref, sem):
        copy(ref, ref, sem, sem, (r, partner)).wait_send()

    def arrived(ref, sem):
        copy(ref, ref, sem, sem, (r, partner)).wait_recv()

    def when(condition, f):
        pl.when(condition)(f)

    def chunk(k, part):
        rows = pl.multiple_of(lax.rem(k, 8) * 8 + part * NB, 8)
        return rowpb.at[lax.div(k, 8), :, pl.ds(rows, 8), :]

    def some(n):
        return zrecv.at[pl.ds(0, n)]

    load = pltpu.make_async_copy(a_hbm, a_v, load_s)
    load.start()
    barrier = pltpu.get_barrier_semaphore()

    def greet(dev):
        pl.semaphore_signal(barrier, inc=1, device_id=dev, device_id_type=MESH)

    loop(0, 15, lambda p: greet((row_peer(p), c)))

    @pl.when(jnp.logical_not(home) & (core == 0))
    def _():
        loop(0, 8, lambda g: greet((lax.rem(c, 16), panel_owner(g + 8 * lax.div(c, 16)))))

    loop(0, 31, lambda p: greet((r, col_peer(p))))

    load.wait()

    def panel_cols(ref, s):
        return jnp.where((c == 0) & (s == 0) & (lane < NB), 0.0, ref[pl.ds(s, NB, stride=3), :])

    @pl.when(c == 0)
    def _():
        full = lax.broadcasted_iota(jnp.int32, (128, 128), 0)
        full_lane = lax.broadcasted_iota(jnp.int32, (128, 128), 1)
        for t in range(6):
            block = jnp.transpose(a_v[pl.ds(t * 384, 128, stride=3), :])
            if t == 0:
                block = jnp.where((r == 0) & (full < NB) & (full_lane < NB), 0.0, block)
            rowpb[t % 2, t // 2] = block

    @pl.when(r == 0)
    def _():
        panel = jnp.concatenate([panel_cols(a_v, s) for s in range(3)], axis=1)
        zero = jnp.zeros_like(panel)
        gx[x] = dot_nt(panel[:32], jnp.concatenate([panel, zero], axis=0)) + dot_nt(
            panel[32:], jnp.concatenate([zero, panel], axis=0)
        )

        @pl.when(c == 0)
        def _():
            p1[...] = a_v[pl.ds(3 * NB, NB, stride=3), :]

        colpb[...] = a_v[0:192, :]

    when(owner & (core == 0), lambda: pl.semaphore_wait(barrier, 53))
    when(owner & (core == 1), lambda: pl.semaphore_wait(barrier, 54))
    when(plain, lambda: pl.semaphore_wait(barrier, 46))

    columns = pl.ds(0, 192)

    def send_col(q):
        other = 2 * spiral(q, 8) + jnp.where(q == 7, 1, 0)
        copy(a_v.at[columns], colpb, colp_s, colp_r, (other, c)).start()

    def wait_col():
        @pl.when(r != 0)
        def _():
            arrived(colpb, colp_r)

            @pl.when(core == 0)
            def _():
                copy(colpb, colpb, fwd_s.at[0], colp_r, (r + 1, c)).start()

    def scatter(part):
        def to(p):
            k = 2 * spiral(lax.div(p, 2), 8) + 1 - lax.rem(p, 2)
            dev = panel_owner(k) if part == 0 else other_owner(k)
            copy(chunk(k, part), chunk(k, part), sc_s, sc_r, (r, dev)).start()

        loop(0, 15 + part, to)

    when(c == 0, lambda: scatter(0))

    @pl.when(r == 0)
    def _():
        loop(0, 8, send_col)
        loop(0, 3, lambda p: copy(gx.at[x], gx.at[x], g_s.at[0], g_r.at[0], (r, x_peer(p))).start())

        @pl.when(c == 0)
        def _():
            loop(0, 3, lambda p: copy(p1, p1, p1_s.at[0], p1_r, (r, x_peer(p))).start())

    when(c == 0, lambda: scatter(1))

    wait_col()

    def pass_to(k, part, dev, ssem, sem):
        copy(chunk(k, part), chunk(k, part), ag_s.at[ssem], ag_r.at[sem], (r, dev)).start()

    one = jnp.int32(1)
    n_first, n_across, n_b = jnp.int32(0), jnp.int32(0), jnp.int32(0)

    firsts = []
    for p in range(7):
        dev = panel_owner(8 * my_h + lax.rem(my_g + 4 + p + (1 if p > 3 else 0), 8))
        firsts.append((dev, owner & (dev != 0)))
    downs = []
    for p in range(7):
        dev = z_peer(p)
        dev_z = lax.div(dev, 4)
        first = (lax.rem(dev_z + x, 2) == 0) & (lax.div(dev_z, 4) == my_h)
        downs.append((dev, owner & (dev != 0) & jnp.logical_not(first)))
    acrosses = []
    for p in range(3):
        dev = x_peer(p)
        dev_owner = lax.rem(lax.rem(dev, 4) + z, 2) == 0
        for i in range(4):
            k = 4 * i + 2 * lax.rem(x, 2) + lax.div(x, 2)
            skip = dev_owner & (lax.div(z, 4) == i // 2)
            acrosses.append((dev, k, (dev != 0) & jnp.logical_not(skip)))

    panel = jnp.concatenate([panel_cols(colpb, s) for s in range(3)], axis=1)
    def share(t):
        tile = jnp.concatenate([a_v[pl.ds(t * 384 + s, 128, stride=3), :] for s in range(3)], axis=1)
        zt = dot3(panel, tile, (1, 1))
        for g in range(8):
            zpart[g + 8 * (t % 2), t // 2] = zt[8 * g : 8 * g + 8, :]

    def reduce_to(k):
        dev = panel_owner(k)

        @pl.when(dev != c)
        def _():
            copy(zpart.at[k], zrecv.at[c], rs_s, rs_r, (r, dev)).start()

    for t in (0, 2, 4):
        share(t)
    @pl.when(r == 0)
    def _():
        arrived(gx.at[pl.ds(0, 3)], g_r.at[0])
        gz[z] = (gx[0] + gx[1]) + (gx[2] + gx[3])
        loop(0, 7, lambda p: copy(gz.at[z], gz.at[z], g_s.at[1], g_r.at[1], (r, z_peer(p))).start())

        @pl.when(z == 0)
        def _():
            when(x != 0, lambda: arrived(p1, p1_r))
            loop(0, 7, lambda p: copy(p1, p1, p1_s.at[1], p1_r, (r, z_peer(p))).start())

    @pl.when(owner)
    def _():
        when(c != 0, lambda: arrived(chunk(mine, 0), sc_r))

    for dev, go in firsts:
        when(go, functools.partial(pass_to, mine, 0, dev, 0, 2))
        n_first = n_first + jnp.where(go, one, 0)
    loop(0, 8, lambda p: reduce_to(7 - p))
    for t in (1, 3, 5):
        share(t)
    loop(8, 16, reduce_to)

    for dev, go in downs:
        when(go, functools.partial(pass_to, mine, 0, dev, 0, 0))
        n_first = n_first + jnp.where(go, one, 0)

    for dev, k, go in acrosses:
        n_across = n_across + jnp.where(go, one, 0)

    when(plain, lambda: arrived(chunk(mine, 1), sc_r))
    for p in range(8):
        dev = panel_owner(8 * my_h + lax.rem(my_g + 4 + p, 8))
        when(plain & (dev != 0), functools.partial(pass_to, mine, 1, dev, 2, 1))
        n_b = n_b + jnp.where(plain & (dev != 0), one, 0)

    def pass_across():
        for dev, k, go in acrosses:
            when(go, functools.partial(pass_to, k, 0, dev, 1, 3))

    def z_across():
        def to(p):
            k = 4 * lax.rem(p, 4) + 2 * lax.rem(x, 2) + lax.div(x, 2)
            copy(zrows.at[k], zrows.at[k], zr_s.at[1], zr_r.at[1], (r, x_peer(1 + lax.div(p, 4)))).start()

        loop(0, 8, to)

    def sent_some(n, sem, least, most):
        for count in range(least, most + 1):
            when(n == count, lambda count=count: sent(some(count), sem))

    @pl.when(r == 0)
    def _():
        arrived(gz.at[pl.ds(0, 7)], g_r.at[1])
        gfin[...] = ((gz[0] + gz[1]) + (gz[2] + gz[3])) + ((gz[4] + gz[5]) + (gz[6] + gz[7]))
        loop(0, 15, lambda p: copy(gfin, gfin, g_s.at[2], g_r.at[2], (row_peer(p), c)).start())
        when(z != 0, lambda: arrived(p1, p1_r))
        loop(0, 15, lambda p: copy(p1, p1, p1_s.at[2], p1_r, (row_peer(p), c)).start())


    def gram_matrix():
        packed = gfin[...]
        gram = jnp.concatenate([packed, pltpu.roll(packed, 64, 1)], axis=0)
        return jnp.where(lane < NB, gram, 0.0)

    def cholesky():
        when(r != 0, lambda: arrived(gfin, g_r.at[2]))
        ct[0:NB, :] = jnp.zeros((NB, 128), F32)
        factor_cholesky(gram_matrix(), ct)
        c0[...] = jnp.transpose(ct[...])[0:NB, :]

    def inverse():
        when(r != 0, lambda: arrived(p1, p1_r))
        corner = p1[...]
        product = dot_nn(pltpu.roll(c0[...], 64, 1), jnp.concatenate([corner, jnp.zeros_like(corner)], axis=0))
        whole = invert(gram_matrix() + jnp.where(lane < NB, product, 0.0))
        om[...] = whole

    @pl.when(owner)
    def _():
        cholesky()
        when(c != 0, lambda: arrived(some(7), ag_r.at[2]))
        rows = jnp.concatenate([rowpb[my_h, i, 0:NB, :] for i in range(3)], axis=1)
        high, low = split(jnp.concatenate([rows, jnp.zeros_like(rows)], axis=0))
        arrived(some(31), rs_r)
        zrecv[c] = zpart[mine]
        zsum = tree_sum([zrecv[i] for i in range(32)])
        z_rows = jnp.concatenate([zsum[i] for i in range(3)], axis=1)
        z_high, z_low = split(z_rows)
        total = lax.dot_general(
            jnp.concatenate([z_high, z_high, z_low], axis=1),
            jnp.concatenate([high, low, high], axis=1),
            (((1,), (1,)), ((), ())),
            preferred_element_type=F32,
        )
        lane8 = lax.broadcasted_iota(jnp.int32, (8, 128), 1)
        total = total + jnp.where((r == 0) & (my_h == 0) & (lane8 >= NB), zsum[0], 0.0)
        hsend[0] = total
        hrecv[r] = total
        loop(0, 15, lambda p: copy(hsend.at[0], hrecv.at[r], h_s, h_r, (row_peer(p), c)).start())
        when(c != 0, lambda: arrived(some(8), ag_r.at[1]))
        mine_c = c0[pl.ds(pl.multiple_of(8 * my_g, 8), 8), :]
        y_rows = z_rows + dot3(mine_c, jnp.concatenate([rowpb[my_h, i] for i in range(3)], axis=1), (1, 0))
        for i in range(3):
            zrows[mine, i] = y_rows[:, 128 * i : 128 * i + 128]
        there = r + 16 * my_h

        loop(0, 7, lambda p: copy(zrows.at[mine], zrows.at[mine], zr_s.at[0], zr_r.at[0], (r, z_peer(p))).start())
        loop(0, 8, lambda p: copy(zrows.at[mine], zrows.at[mine], zr_s.at[0], zr_r.at[2], (r, far_peer(p))).start())
        def to_cols(p):
            dev = 2 * lax.rem(y + spiral(p, 8), 8)
            when(dev != r, lambda: copy(zrows.at[mine], zcols.at[my_g], zc_s, zc_r, (dev, there)).start())

        loop(0, 8, to_cols)
        when(c != 0, lambda: arrived(some(2), ag_r.at[0]))
        pass_across()
        inverse()
        arrived(hrecv.at[pl.ds(0, 15)], h_r)
        hall[mine] = tree_sum([hrecv[i] for i in range(16)])
        loop(0, 31, lambda p: copy(hall.at[mine], hall.at[mine], ha_s, ha_r, (r, early_peer(p))).start())
        arrived(some(3), zr_r.at[0])
        z_across()
        @pl.when(c != 0)
        def _():
            arrived(some(6), ag_r.at[3])


    @pl.when(plain)
    def _():
        arrived(some(4), ag_r.at[0])
        pass_across()
        cholesky()
        inverse()
        arrived(some(4), zr_r.at[0])
        z_across()
        arrived(some(12), ag_r.at[3])

    def forward_cols():
        copy(zcols, zcols, fwd_s.at[1], zc_r, (r + 1, c)).start()

    home_next = lax.rem(c, 16) == r + 1

    @pl.when(jnp.logical_not(home) & (core == 0))
    def _():
        arrived(zcols, zc_r)
        when(jnp.logical_not(home_next), forward_cols)

    inverse_t = om[:, 0:NB]
    pad = jnp.zeros((NB, 128), F32)
    sub = lax.broadcasted_iota(jnp.int32, (NB, 128), 0)
    unit = jnp.where(sub == lane, 1.0, 0.0)
    s_mat = dot_nn(inverse_t, unit + c0[...])
    turned = jnp.transpose(jnp.concatenate([s_mat, pad], axis=0))
    c_cols = jnp.where(c == 0, c0[...], 0.0)
    c_rows = jnp.where(r == 0, c0[...], 0.0)
    n_cols = [panel_cols(colpb, s) for s in range(3)]
    n_cols = jnp.concatenate([n_cols[0] + c_cols] + n_cols[1:], axis=1)
    right_o[0:NB, :] = n_cols
    sn_cols = dot3(turned[:, 0:NB], n_cols, (1, 0))

    arrived(some(4), zr_r.at[2])
    arrived(some(8), zr_r.at[1])

    y_rows, n_rows = [], []
    for t in range(6):
        h, i = t % 2, t // 2
        y_rows.append(zrows[8 * h : 8 * h + 8, i].reshape(NB, 128))
        n_t = rowpb[h, i, 0:NB, :]
        if t == 0:
            n_t = n_t + c_rows
        n_rows.append(n_t)
    w_rows = dot3(inverse_t, jnp.concatenate(y_rows, axis=1), (1, 0))
    for t in range(6):
        rows = jnp.concatenate([w_rows[:, 128 * t : 128 * t + 128], n_rows[t]], axis=0)
        high, low = split(jnp.transpose(rows))
        left_o[t] = jnp.concatenate([high, high, low], axis=1)

    @pl.when(home)
    def _():
        zcols[...] = zrows[pl.ds(8 * lax.div(c, 16), 8)]

    when(home & (core == 0), forward_cols)
    when(jnp.logical_not(home) & (core == 1), lambda: arrived(zcols, zc_r))

    y_cols = jnp.concatenate([zcols[:, s].reshape(NB, 128) for s in range(3)], axis=1)
    w_cols = dot3(inverse_t, y_cols, (1, 0))

    when(owner, lambda: arrived(hall.at[pl.ds(0, 15)], ha_r))
    when(plain, lambda: arrived(hall, ha_r))

    top = (hall[0:8] + hall[8:16]).reshape(NB, 128)
    turned = jnp.transpose(jnp.concatenate([top, pad], axis=0))
    bottom = jnp.where(lane < NB, turned[NB:, :], p1[...])
    inner = dot3(jnp.concatenate([top, bottom], axis=0), sn_cols, (1, 0))
    right_o[NB:, :] = w_cols - dot3(s_mat, inner, (1, 0))

    @pl.when(r == 0)
    def _():
        sent(a_v.at[pl.ds(0, 8 * 192)], colp_s)
        sent(gx.at[pl.ds(0, 3)], g_s.at[0])
        sent(gz.at[pl.ds(0, 7)], g_s.at[1])
        sent(a_v.at[pl.ds(0, 15 * 32)], g_s.at[2])
        when(c == 0, lambda: sent(a_v.at[pl.ds(0, 3 * NB)], p1_s.at[0]))
        when(z == 0, lambda: sent(a_v.at[pl.ds(0, 7 * NB)], p1_s.at[1]))
        sent(a_v.at[pl.ds(0, 15 * NB)], p1_s.at[2])

    @pl.when((r != 0) & (core == 0))
    def _():
        sent(colpb, fwd_s.at[0])

    @pl.when(c == 0)
    def _():
        sent(some(31), sc_s)

    when(owner, lambda: sent_some(n_first, ag_s.at[0], 10, 14))
    sent_some(n_across, ag_s.at[1], 4, 12)
    sent(some(8), zr_s.at[1])
    when(plain, lambda: sent_some(n_b, ag_s.at[2], 7, 8))

    @pl.when(owner)
    def _():
        sent(some(15), rs_s)
        when(core == 0, lambda: sent(some(7), zc_s))
        when(core == 1, lambda: sent(some(8), zc_s))
        sent(some(15), zr_s.at[0])
        sent(a_v.at[pl.ds(0, 15 * 8)], h_s)
        sent(a_v.at[pl.ds(0, 31 * 8)], ha_s)

    when((core == 0) & jnp.logical_not(home_next), lambda: sent(zcols, fwd_s.at[1]))

    @pl.when(plain)
    def _():
        sent(some(16), rs_s)


def update(a, left, right, out, tiles, sems):
    high, low = split(right[...])
    columns = jnp.concatenate([high, low, high], axis=0)
    for t in range(6):
        change = jnp.dot(left[t], columns, preferred_element_type=F32)
        for s in range(3):
            rows = pl.ds(t * 384 + s, 128, stride=3)
            tiles[rows, :] = a[rows, :] - change[:, 128 * s : 128 * s + 128]
        rows = pl.ds(t * 384, 384)
        pltpu.make_async_copy(tiles.at[rows], out.at[rows], sems.at[t]).start()
    for t in range(6):
        rows = pl.ds(t * 384, 384)
        pltpu.make_async_copy(tiles.at[rows], out.at[rows], sems.at[t]).wait()


def vmem(*shape):
    return pltpu.VMEM(shape, F32)


def dma(*shape):
    return pltpu.SemaphoreType.DMA(shape)


def body(hessian):
    flat = hessian.reshape(2304, 128)
    whole = pl.BlockSpec(memory_space=pltpu.VMEM)
    left, right = pl.pallas_call(
        kernel,
        out_shape=[jax.ShapeDtypeStruct((6, 128, 384), jnp.bfloat16), jax.ShapeDtypeStruct((128, 384), F32)],
        in_specs=[pl.BlockSpec(memory_space=pltpu.HBM)],
        out_specs=[whole, whole],
        scratch_shapes=[
            vmem(2304, 128), vmem(192, 128), vmem(2, 3, 128, 128), vmem(16, 3, 8, 128), vmem(32, 3, 8, 128),
            vmem(16, 3, 8, 128), vmem(8, 3, 8, 128), vmem(4, 32, 128), vmem(8, 32, 128), vmem(32, 128),
            vmem(64, 128), vmem(1, 8, 128), vmem(16, 8, 128), vmem(16, 8, 128), vmem(128, 128), vmem(64, 128), vmem(64, 128),
            dma(), dma(), dma(), dma(2), dma(), dma(), dma(3), dma(4), dma(), dma(), dma(2), dma(3), dma(), dma(),
            dma(3), dma(3), dma(3), dma(), dma(), dma(), dma(), dma(),
        ],
        compiler_params=pltpu.CompilerParams(collective_id=0, has_side_effects=True, vmem_limit_bytes=54208 << 10),
        name="panel",
    )(flat)
    out = pl.pallas_call(
        update,
        out_shape=jax.ShapeDtypeStruct((2304, 128), F32),
        in_specs=[whole, whole, whole],
        out_specs=pl.BlockSpec(memory_space=pltpu.HBM),
        scratch_shapes=[vmem(2304, 128), dma(6)],
        compiler_params=pltpu.CompilerParams(vmem_limit_bytes=16 << 20),
        name="update",
    )(flat, left, right)
    return out.reshape(hessian.shape)


def solution(mesh):
    return jax.shard_map(
        body,
        mesh=mesh,
        in_specs=(P(None, "row", None, None, "col", None),),
        out_specs=P(None, "row", None, None, "col", None),
        check_vma=False,
    )
```

```python
import functools

import jax
import jax.numpy as jnp
from jax import lax
from jax.experimental import pallas as pl
from jax.experimental.pallas import tpu as pltpu
from jax.sharding import PartitionSpec as P

NB = 64
MESH = pl.DeviceIdType.MESH
HIGHEST = lax.Precision.HIGHEST
F32 = jnp.float32


def dot_nn(a, b):
    return lax.dot_general(a, b, (((1,), (0,)), ((), ())), precision=HIGHEST, preferred_element_type=F32)


def dot_nt(a, b):
    return lax.dot_general(a, b, (((1,), (1,)), ((), ())), precision=HIGHEST, preferred_element_type=F32)


def split(a):
    high = a.astype(jnp.bfloat16)
    return high, (a - high.astype(F32)).astype(jnp.bfloat16)


def dot3(a, b, dims):
    (ah, al), (bh, bl) = split(a), split(b)
    left = jnp.concatenate([ah, ah, al], axis=dims[0])
    right = jnp.concatenate([bh, bl, bh], axis=dims[1])
    return lax.dot_general(left, right, (((dims[0],), (dims[1],)), ((), ())), preferred_element_type=F32)


def split(a):
    high = a.astype(jnp.bfloat16)
    return high, (a - high.astype(F32)).astype(jnp.bfloat16)


def dot3(a, b, dims):
    (ah, al), (bh, bl) = split(a), split(b)
    left = jnp.concatenate([ah, ah, al], axis=dims[0])
    right = jnp.concatenate([bh, bl, bh], axis=dims[1])
    return lax.dot_general(left, right, (((dims[0],), (dims[1],)), ((), ())), preferred_element_type=F32)


def split(a):
    high = a.astype(jnp.bfloat16)
    return high, (a - high.astype(F32)).astype(jnp.bfloat16)


def dot3(a, b, dims):
    (ah, al), (bh, bl) = split(a), split(b)
    left = jnp.concatenate([ah, ah, al], axis=dims[0])
    right = jnp.concatenate([bh, bl, bh], axis=dims[1])
    return lax.dot_general(left, right, (((dims[0],), (dims[1],)), ((), ())), preferred_element_type=F32)


def spiral(q, n):
    return lax.rem(n // 2 + (1 - 2 * lax.rem(q, 2)) * lax.div(q + 1, 2), n)


def tree_sum(terms):
    while len(terms) > 1:
        terms = [a + b for a, b in zip(terms[0::2], terms[1::2])]
    return terms[0]


def loop(lo, hi, f):
    def step(i, carry):
        f(i)
        return carry

    lax.fori_loop(lo, hi, step, 0)


def factor_cholesky(g, ct):
    lane1 = lax.broadcasted_iota(jnp.int32, (1, 128), 1)
    for first in range(0, NB, 8):
        rest = g[first:, :]
        cols = [jnp.broadcast_to(rest[:, first + j : first + j + 1], rest.shape) for j in range(8)]
        rows = [rest[j : j + 1, :] for j in range(8)]
        for j in range(8):
            k = first + j
            pivot = cols[j][j : j + 1, :]
            inverse = 1.0 / pivot
            scaled = rows[j] * inverse
            ct[NB + k : NB + k + 1, :] = jnp.where((lane1 >= k) & (lane1 < NB), rows[j] * lax.rsqrt(pivot), 0.0)
            for i in range(j + 1, 8):
                factor = cols[i][j : j + 1, :] * inverse
                rows[i] = rows[i] - cols[j][i : i + 1, :] * scaled
                cols[i] = cols[i] - cols[j] * factor
            rest = rest - cols[j] * scaled
        g = rest if first == 0 else jnp.concatenate([g[:first, :], rest], axis=0)


def invert(m):
    lane1 = lax.broadcasted_iota(jnp.int32, (1, 128), 1)
    lane = lax.broadcasted_iota(jnp.int32, (NB, 128), 1)
    sub = lax.broadcasted_iota(jnp.int32, (NB, 128), 0)
    for first in range(0, NB, 8):
        cols = [jnp.broadcast_to(m[:, first + j : first + j + 1], (NB, 128)) for j in range(8)]
        rows = [m[first + j : first + j + 1, :] for j in range(8)]
        for j in range(8):
            k = first + j
            inverse = 1.0 / cols[j][k : k + 1, :]
            scaled = jnp.where(lane1 == k, 1.0, rows[j]) * inverse
            for i in range(j + 1, 8):
                factor = cols[i][k : k + 1, :] * inverse
                rows[i] = jnp.where(lane1 == k, 0.0, rows[i]) - cols[j][first + i : first + i + 1, :] * scaled
                cols[i] = jnp.where(sub == k, factor, cols[i] - cols[j] * factor)
            m = jnp.where(sub == k, scaled, jnp.where(lane == k, 0.0, m) - cols[j] * scaled)
    return m


def kernel(
    a_hbm, left_o, right_o, a_v, colpb, rowpb, zpart, zrecv, zrows, zcols, gx, gz, gfin, p1, hsend, hrecv, hall, ct, c0, om,
    load_s, colp_s, colp_r, fwd_s, sc_s, sc_r, ag_s, ag_r, rs_s, rs_r, zr_s, zr_r, zc_s, zc_r,
    g_s, g_r, p1_s, p1_r, h_s, h_r, ha_s, ha_r,
):
    r, c = lax.axis_index("row"), lax.axis_index("col")
    y, core = lax.div(r, 2), lax.rem(r, 2)
    z, x = lax.div(c, 4), lax.rem(c, 4)
    mine = lax.div(c, 2)
    owner = lax.rem(x + z, 2) == 0
    plain = jnp.logical_not(owner)
    my_g, my_h = lax.rem(mine, 8), lax.div(mine, 8)
    partner = c + 1 - 2 * lax.rem(c, 2)
    home = lax.rem(c, 16) == r
    lane = lax.broadcasted_iota(jnp.int32, (NB, 128), 1)

    def panel_owner(k):
        return 2 * k + lax.rem(lax.div(k, 2), 2)

    def other_owner(k):
        return 2 * k + 1 - lax.rem(lax.div(k, 2), 2)

    def col_peer(p):
        return lax.rem(z + spiral(lax.div(p, 4), 8), 8) * 4 + lax.rem(x + spiral(lax.rem(p, 4), 4), 4)

    def early_peer(p):
        place = z * 4 + x
        return p + jnp.where(p >= place, 1, 0)

    def x_peer(p):
        return z * 4 + lax.rem(x + spiral(p, 4), 4)

    def far_peer(p):
        return lax.rem(z + spiral(p, 8), 8) * 4 + lax.rem(x + 2, 4)

    def z_peer(p):
        return lax.rem(z + spiral(p, 8), 8) * 4 + x

    def row_peer(p):
        return lax.rem(y + spiral(lax.div(p, 2), 8), 8) * 2 + lax.rem(core + 1 - lax.rem(p, 2), 2)

    def copy(src, dst, ssem, rsem, dev):
        return pltpu.make_async_remote_copy(
            src_ref=src, dst_ref=dst, send_sem=ssem, recv_sem=rsem, device_id=dev, device_id_type=MESH
        )

    def sent(ref, sem):
        copy(ref, ref, sem, sem, (r, partner)).wait_send()

    def arrived(ref, sem):
        copy(ref, ref, sem, sem, (r, partner)).wait_recv()

    def when(condition, f):
        pl.when(condition)(f)

    def chunk(k, part):
        rows = pl.multiple_of(lax.rem(k, 8) * 8 + part * NB, 8)
        return rowpb.at[lax.div(k, 8), :, pl.ds(rows, 8), :]

    def some(n):
        return zrecv.at[pl.ds(0, n)]

    load = pltpu.make_async_copy(a_hbm, a_v, load_s)
    load.start()
    barrier = pltpu.get_barrier_semaphore()

    def greet(dev):
        pl.semaphore_signal(barrier, inc=1, device_id=dev, device_id_type=MESH)

    loop(0, 15, lambda p: greet((row_peer(p), c)))

    @pl.when(jnp.logical_not(home) & (core == 0))
    def _():
        loop(0, 8, lambda g: greet((lax.rem(c, 16), panel_owner(g + 8 * lax.div(c, 16)))))

    loop(0, 31, lambda p: greet((r, col_peer(p))))

    load.wait()

    def panel_cols(ref, s):
        return jnp.where((c == 0) & (s == 0) & (lane < NB), 0.0, ref[pl.ds(s, NB, stride=3), :])

    @pl.when(c == 0)
    def _():
        full = lax.broadcasted_iota(jnp.int32, (128, 128), 0)
        full_lane = lax.broadcasted_iota(jnp.int32, (128, 128), 1)
        for t in range(6):
            block = jnp.transpose(a_v[pl.ds(t * 384, 128, stride=3), :])
            if t == 0:
                block = jnp.where((r == 0) & (full < NB) & (full_lane < NB), 0.0, block)
            rowpb[t % 2, t // 2] = block

    @pl.when(r == 0)
    def _():
        panel = jnp.concatenate([panel_cols(a_v, s) for s in range(3)], axis=1)
        zero = jnp.zeros_like(panel)
        gx[x] = dot_nt(panel[:32], jnp.concatenate([panel, zero], axis=0)) + dot_nt(
            panel[32:], jnp.concatenate([zero, panel], axis=0)
        )

        @pl.when(c == 0)
        def _():
            p1[...] = a_v[pl.ds(3 * NB, NB, stride=3), :]

        colpb[...] = a_v[0:192, :]

    when(owner & (core == 0), lambda: pl.semaphore_wait(barrier, 53))
    when(owner & (core == 1), lambda: pl.semaphore_wait(barrier, 54))
    when(plain, lambda: pl.semaphore_wait(barrier, 46))

    columns = pl.ds(0, 192)

    def send_col(q):
        other = 2 * spiral(q, 8) + jnp.where(q == 7, 1, 0)
        copy(a_v.at[columns], colpb, colp_s, colp_r, (other, c)).start()

    def wait_col():
        @pl.when(r != 0)
        def _():
            arrived(colpb, colp_r)

            @pl.when(core == 0)
            def _():
                copy(colpb, colpb, fwd_s.at[0], colp_r, (r + 1, c)).start()

    def scatter(part):
        def to(p):
            k = 2 * spiral(lax.div(p, 2), 8) + 1 - lax.rem(p, 2)
            dev = panel_owner(k) if part == 0 else other_owner(k)
            copy(chunk(k, part), chunk(k, part), sc_s, sc_r, (r, dev)).start()

        loop(0, 15 + part, to)

    when(c == 0, lambda: scatter(0))

    @pl.when(r == 0)
    def _():
        loop(0, 8, send_col)
        loop(0, 3, lambda p: copy(gx.at[x], gx.at[x], g_s.at[0], g_r.at[0], (r, x_peer(p))).start())

        @pl.when(c == 0)
        def _():
            loop(0, 3, lambda p: copy(p1, p1, p1_s.at[0], p1_r, (r, x_peer(p))).start())

    when(c == 0, lambda: scatter(1))

    wait_col()

    def pass_to(k, part, dev, ssem, sem):
        copy(chunk(k, part), chunk(k, part), ag_s.at[ssem], ag_r.at[sem], (r, dev)).start()

    one = jnp.int32(1)
    n_first, n_across, n_b = jnp.int32(0), jnp.int32(0), jnp.int32(0)

    firsts = []
    for p in range(7):
        dev = panel_owner(8 * my_h + lax.rem(my_g + 4 + p + (1 if p > 3 else 0), 8))
        firsts.append((dev, owner & (dev != 0)))
    downs = []
    for p in range(7):
        dev = z_peer(p)
        dev_z = lax.div(dev, 4)
        first = (lax.rem(dev_z + x, 2) == 0) & (lax.div(dev_z, 4) == my_h)
        downs.append((dev, owner & (dev != 0) & jnp.logical_not(first)))
    acrosses = []
    for p in range(3):
        dev = x_peer(p)
        dev_owner = lax.rem(lax.rem(dev, 4) + z, 2) == 0
        for i in range(4):
            k = 4 * i + 2 * lax.rem(x, 2) + lax.div(x, 2)
            skip = dev_owner & (lax.div(z, 4) == i // 2)
            acrosses.append((dev, k, (dev != 0) & jnp.logical_not(skip)))

    panel = jnp.concatenate([panel_cols(colpb, s) for s in range(3)], axis=1)
    def share(t):
        tile = jnp.concatenate([a_v[pl.ds(t * 384 + s, 128, stride=3), :] for s in range(3)], axis=1)
        zt = dot3(panel, tile, (1, 1))
        for g in range(8):
            zpart[g + 8 * (t % 2), t // 2] = zt[8 * g : 8 * g + 8, :]

    def reduce_to(k):
        dev = panel_owner(k)

        @pl.when(dev != c)
        def _():
            copy(zpart.at[k], zrecv.at[c], rs_s, rs_r, (r, dev)).start()

    for t in (0, 2, 4):
        share(t)
    @pl.when(r == 0)
    def _():
        arrived(gx.at[pl.ds(0, 3)], g_r.at[0])
        gz[z] = (gx[0] + gx[1]) + (gx[2] + gx[3])
        loop(0, 7, lambda p: copy(gz.at[z], gz.at[z], g_s.at[1], g_r.at[1], (r, z_peer(p))).start())

        @pl.when(z == 0)
        def _():
            when(x != 0, lambda: arrived(p1, p1_r))
            loop(0, 7, lambda p: copy(p1, p1, p1_s.at[1], p1_r, (r, z_peer(p))).start())

    @pl.when(owner)
    def _():
        when(c != 0, lambda: arrived(chunk(mine, 0), sc_r))

    for dev, go in firsts:
        when(go, functools.partial(pass_to, mine, 0, dev, 0, 2))
        n_first = n_first + jnp.where(go, one, 0)
    loop(0, 8, lambda p: reduce_to(7 - p))
    for t in (1, 3, 5):
        share(t)
    loop(8, 16, reduce_to)

    for dev, go in downs:
        when(go, functools.partial(pass_to, mine, 0, dev, 0, 0))
        n_first = n_first + jnp.where(go, one, 0)

    for dev, k, go in acrosses:
        n_across = n_across + jnp.where(go, one, 0)

    when(plain, lambda: arrived(chunk(mine, 1), sc_r))
    for p in range(8):
        dev = panel_owner(8 * my_h + lax.rem(my_g + 4 + p, 8))
        when(plain & (dev != 0), functools.partial(pass_to, mine, 1, dev, 2, 1))
        n_b = n_b + jnp.where(plain & (dev != 0), one, 0)

    def pass_across():
        for dev, k, go in acrosses:
            when(go, functools.partial(pass_to, k, 0, dev, 1, 3))

    def z_across():
        def to(p):
            k = 4 * lax.rem(p, 4) + 2 * lax.rem(x, 2) + lax.div(x, 2)
            copy(zrows.at[k], zrows.at[k], zr_s.at[1], zr_r.at[1], (r, x_peer(1 + lax.div(p, 4)))).start()

        loop(0, 8, to)

    def sent_some(n, sem, least, most):
        for count in range(least, most + 1):
            when(n == count, lambda count=count: sent(some(count), sem))

    @pl.when(r == 0)
    def _():
        arrived(gz.at[pl.ds(0, 7)], g_r.at[1])
        gfin[...] = ((gz[0] + gz[1]) + (gz[2] + gz[3])) + ((gz[4] + gz[5]) + (gz[6] + gz[7]))
        loop(0, 15, lambda p: copy(gfin, gfin, g_s.at[2], g_r.at[2], (row_peer(p), c)).start())
        when(z != 0, lambda: arrived(p1, p1_r))
        loop(0, 15, lambda p: copy(p1, p1, p1_s.at[2], p1_r, (row_peer(p), c)).start())


    def gram_matrix():
        packed = gfin[...]
        gram = jnp.concatenate([packed, pltpu.roll(packed, 64, 1)], axis=0)
        return jnp.where(lane < NB, gram, 0.0)

    def cholesky():
        when(r != 0, lambda: arrived(gfin, g_r.at[2]))
        ct[0:NB, :] = jnp.zeros((NB, 128), F32)
        factor_cholesky(gram_matrix(), ct)
        c0[...] = jnp.transpose(ct[...])[0:NB, :]

    def inverse():
        when(r != 0, lambda: arrived(p1, p1_r))
        corner = p1[...]
        product = dot_nn(pltpu.roll(c0[...], 64, 1), jnp.concatenate([corner, jnp.zeros_like(corner)], axis=0))
        whole = invert(gram_matrix() + jnp.where(lane < NB, product, 0.0))
        om[...] = whole

    @pl.when(owner)
    def _():
        cholesky()
        when(c != 0, lambda: arrived(some(7), ag_r.at[2]))
        rows = jnp.concatenate([rowpb[my_h, i, 0:NB, :] for i in range(3)], axis=1)
        high, low = split(jnp.concatenate([rows, jnp.zeros_like(rows)], axis=0))
        arrived(some(31), rs_r)
        zrecv[c] = zpart[mine]
        zsum = tree_sum([zrecv[i] for i in range(32)])
        z_rows = jnp.concatenate([zsum[i] for i in range(3)], axis=1)
        z_high, z_low = split(z_rows)
        total = lax.dot_general(
            jnp.concatenate([z_high, z_high, z_low], axis=1),
            jnp.concatenate([high, low, high], axis=1),
            (((1,), (1,)), ((), ())),
            preferred_element_type=F32,
        )
        lane8 = lax.broadcasted_iota(jnp.int32, (8, 128), 1)
        total = total + jnp.where((r == 0) & (my_h == 0) & (lane8 >= NB), zsum[0], 0.0)
        hsend[0] = total
        hrecv[r] = total
        loop(0, 15, lambda p: copy(hsend.at[0], hrecv.at[r], h_s, h_r, (row_peer(p), c)).start())
        when(c != 0, lambda: arrived(some(8), ag_r.at[1]))
        mine_c = c0[pl.ds(pl.multiple_of(8 * my_g, 8), 8), :]
        y_rows = z_rows + dot3(mine_c, jnp.concatenate([rowpb[my_h, i] for i in range(3)], axis=1), (1, 0))
        for i in range(3):
            zrows[mine, i] = y_rows[:, 128 * i : 128 * i + 128]
        there = r + 16 * my_h

        loop(0, 7, lambda p: copy(zrows.at[mine], zrows.at[mine], zr_s.at[0], zr_r.at[0], (r, z_peer(p))).start())
        loop(0, 8, lambda p: copy(zrows.at[mine], zrows.at[mine], zr_s.at[0], zr_r.at[2], (r, far_peer(p))).start())
        def to_cols(p):
            dev = 2 * lax.rem(y + spiral(p, 8), 8)
            when(dev != r, lambda: copy(zrows.at[mine], zcols.at[my_g], zc_s, zc_r, (dev, there)).start())

        loop(0, 8, to_cols)
        when(c != 0, lambda: arrived(some(2), ag_r.at[0]))
        pass_across()
        inverse()
        arrived(hrecv.at[pl.ds(0, 15)], h_r)
        hall[mine] = tree_sum([hrecv[i] for i in range(16)])
        loop(0, 31, lambda p: copy(hall.at[mine], hall.at[mine], ha_s, ha_r, (r, early_peer(p))).start())
        arrived(some(3), zr_r.at[0])
        z_across()
        @pl.when(c != 0)
        def _():
            arrived(some(6), ag_r.at[3])


    @pl.when(plain)
    def _():
        arrived(some(4), ag_r.at[0])
        pass_across()
        cholesky()
        inverse()
        arrived(some(4), zr_r.at[0])
        z_across()
        arrived(some(12), ag_r.at[3])

    def forward_cols():
        copy(zcols, zcols, fwd_s.at[1], zc_r, (r + 1, c)).start()

    home_next = lax.rem(c, 16) == r + 1

    @pl.when(jnp.logical_not(home) & (core == 0))
    def _():
        arrived(zcols, zc_r)
        when(jnp.logical_not(home_next), forward_cols)

    inverse_t = om[:, 0:NB]
    pad = jnp.zeros((NB, 128), F32)
    sub = lax.broadcasted_iota(jnp.int32, (NB, 128), 0)
    unit = jnp.where(sub == lane, 1.0, 0.0)
    s_mat = dot_nn(inverse_t, unit + c0[...])
    turned = jnp.transpose(jnp.concatenate([s_mat, pad], axis=0))
    c_cols = jnp.where(c == 0, c0[...], 0.0)
    c_rows = jnp.where(r == 0, c0[...], 0.0)
    n_cols = [panel_cols(colpb, s) for s in range(3)]
    n_cols = jnp.concatenate([n_cols[0] + c_cols] + n_cols[1:], axis=1)
    right_o[0:NB, :] = n_cols
    sn_high, sn_low = split(dot3(turned[:, 0:NB], n_cols, (1, 0)))
    sn_cols = jnp.concatenate([sn_high, sn_low, sn_high], axis=0)
    s_high, s_low = split(s_mat)
    s_left = jnp.concatenate([s_high, s_high, s_low], axis=1)

    arrived(some(4), zr_r.at[2])
    arrived(some(8), zr_r.at[1])

    y_rows, n_rows = [], []
    for t in range(6):
        h, i = t % 2, t // 2
        y_rows.append(zrows[8 * h : 8 * h + 8, i].reshape(NB, 128))
        n_t = rowpb[h, i, 0:NB, :]
        if t == 0:
            n_t = n_t + c_rows
        n_rows.append(n_t)
    w_rows = dot3(inverse_t, jnp.concatenate(y_rows, axis=1), (1, 0))
    for t in range(6):
        rows = jnp.concatenate([w_rows[:, 128 * t : 128 * t + 128], n_rows[t]], axis=0)
        high, low = split(jnp.transpose(rows))
        left_o[t] = jnp.concatenate([high, high, low], axis=1)

    @pl.when(home)
    def _():
        zcols[...] = zrows[pl.ds(8 * lax.div(c, 16), 8)]

    when(home & (core == 0), forward_cols)
    when(jnp.logical_not(home) & (core == 1), lambda: arrived(zcols, zc_r))

    y_cols = jnp.concatenate([zcols[:, s].reshape(NB, 128) for s in range(3)], axis=1)
    w_cols = dot3(inverse_t, y_cols, (1, 0))

    when(owner, lambda: arrived(hall.at[pl.ds(0, 15)], ha_r))
    when(plain, lambda: arrived(hall, ha_r))

    top = (hall[0:8] + hall[8:16]).reshape(NB, 128)
    turned = jnp.transpose(jnp.concatenate([top, pad], axis=0))
    bottom = jnp.where(lane < NB, turned[NB:, :], p1[...])
    m_high, m_low = split(jnp.concatenate([top, bottom], axis=0))
    m_left = jnp.concatenate([m_high, m_high, m_low], axis=1)
    high, low = split(jnp.dot(m_left, sn_cols, preferred_element_type=F32))
    inner = jnp.concatenate([high, low, high], axis=0)
    right_o[NB:, :] = w_cols - jnp.dot(s_left, inner, preferred_element_type=F32)

    @pl.when(r == 0)
    def _():
        sent(a_v.at[pl.ds(0, 8 * 192)], colp_s)
        sent(gx.at[pl.ds(0, 3)], g_s.at[0])
        sent(gz.at[pl.ds(0, 7)], g_s.at[1])
        sent(a_v.at[pl.ds(0, 15 * 32)], g_s.at[2])
        when(c == 0, lambda: sent(a_v.at[pl.ds(0, 3 * NB)], p1_s.at[0]))
        when(z == 0, lambda: sent(a_v.at[pl.ds(0, 7 * NB)], p1_s.at[1]))
        sent(a_v.at[pl.ds(0, 15 * NB)], p1_s.at[2])

    @pl.when((r != 0) & (core == 0))
    def _():
        sent(colpb, fwd_s.at[0])

    @pl.when(c == 0)
    def _():
        sent(some(31), sc_s)

    when(owner, lambda: sent_some(n_first, ag_s.at[0], 10, 14))
    sent_some(n_across, ag_s.at[1], 4, 12)
    sent(some(8), zr_s.at[1])
    when(plain, lambda: sent_some(n_b, ag_s.at[2], 7, 8))

    @pl.when(owner)
    def _():
        sent(some(15), rs_s)
        when(core == 0, lambda: sent(some(7), zc_s))
        when(core == 1, lambda: sent(some(8), zc_s))
        sent(some(15), zr_s.at[0])
        sent(a_v.at[pl.ds(0, 15 * 8)], h_s)
        sent(a_v.at[pl.ds(0, 31 * 8)], ha_s)

    when((core == 0) & jnp.logical_not(home_next), lambda: sent(zcols, fwd_s.at[1]))

    @pl.when(plain)
    def _():
        sent(some(16), rs_s)


def update(a, left, right, out, tiles, sems):
    high, low = split(right[...])
    columns = jnp.concatenate([high, low, high], axis=0)
    for t in range(6):
        change = jnp.dot(left[t], columns, preferred_element_type=F32)
        for s in range(3):
            rows = pl.ds(t * 384 + s, 128, stride=3)
            tiles[rows, :] = a[rows, :] - change[:, 128 * s : 128 * s + 128]
        rows = pl.ds(t * 384, 384)
        pltpu.make_async_copy(tiles.at[rows], out.at[rows], sems.at[t]).start()
    for t in range(6):
        rows = pl.ds(t * 384, 384)
        pltpu.make_async_copy(tiles.at[rows], out.at[rows], sems.at[t]).wait()


def vmem(*shape):
    return pltpu.VMEM(shape, F32)


def dma(*shape):
    return pltpu.SemaphoreType.DMA(shape)


def body(hessian):
    flat = hessian.reshape(2304, 128)
    whole = pl.BlockSpec(memory_space=pltpu.VMEM)
    left, right = pl.pallas_call(
        kernel,
        out_shape=[jax.ShapeDtypeStruct((6, 128, 384), jnp.bfloat16), jax.ShapeDtypeStruct((128, 384), F32)],
        in_specs=[pl.BlockSpec(memory_space=pltpu.HBM)],
        out_specs=[whole, whole],
        scratch_shapes=[
            vmem(2304, 128), vmem(192, 128), vmem(2, 3, 128, 128), vmem(16, 3, 8, 128), vmem(32, 3, 8, 128),
            vmem(16, 3, 8, 128), vmem(8, 3, 8, 128), vmem(4, 32, 128), vmem(8, 32, 128), vmem(32, 128),
            vmem(64, 128), vmem(1, 8, 128), vmem(16, 8, 128), vmem(16, 8, 128), vmem(128, 128), vmem(64, 128), vmem(64, 128),
            dma(), dma(), dma(), dma(2), dma(), dma(), dma(3), dma(4), dma(), dma(), dma(2), dma(3), dma(), dma(),
            dma(3), dma(3), dma(3), dma(), dma(), dma(), dma(), dma(),
        ],
        compiler_params=pltpu.CompilerParams(collective_id=0, has_side_effects=True, vmem_limit_bytes=54208 << 10),
        name="panel",
    )(flat)
    out = pl.pallas_call(
        update,
        out_shape=jax.ShapeDtypeStruct((2304, 128), F32),
        in_specs=[whole, whole, whole],
        out_specs=pl.BlockSpec(memory_space=pltpu.HBM),
        scratch_shapes=[vmem(2304, 128), dma(6)],
        compiler_params=pltpu.CompilerParams(vmem_limit_bytes=16 << 20),
        name="update",
    )(flat, left, right)
    return out.reshape(hessian.shape)


def solution(mesh):
    return jax.shard_map(
        body,
        mesh=mesh,
        in_specs=(P(None, "row", None, None, "col", None),),
        out_specs=P(None, "row", None, None, "col", None),
        check_vma=False,
    )
```
